32 devices in a mesh: groups: 2 (over y), seq: 4 (over z), tp: 2 (over x), rep: 2 (over core).
Axes of the slice: x: 2, y: 2, z: 4, core: 2. Of those that a mesh axis runs over, the one named last changes fastest.
Arguments:
- queries: bfloat16 [2, 128, 8192], P('rep', ('groups', 'seq', 'tp')), parts along dimension 1, may hold values from -8 to 8
- fresh_key_rows: bfloat16 [2, 128, 1024], P('rep', ('groups', 'seq', 'tp')), parts along dimension 1, may hold values from -8 to 8
- fresh_value_rows: bfloat16 [2, 128, 1024], P('rep', ('groups', 'seq', 'tp')), parts along dimension 1, may hold values from -8 to 8
- visible: int32 [2, 128], P('rep', 'groups'), parts along dimension 1, may hold values from 128 to 2048, as said below
- prefix_keys: bfloat16 [4096, 1024], P(('groups', 'seq'), 'tp'), parts along dimension 0, may hold values from -6 to 6
- cached_value_rows: bfloat16 [4096, 1024], P(('groups', 'seq'), 'tp'), parts along dimension 0, may hold values from -8 to 8
- out_weight: bfloat16 [8192, 8192], P('tp', 'seq'), may hold values from -0.0625 to 0.0625
Outputs:
- mixed: bfloat16 [2, 128, 8192], P('rep', ('groups', 'tp'), 'seq'), parts along dimension 1
The draws below stay inside these ranges and needn't reach their ends.
There are 2 independent parts, one for each index of `groups`. The reference program is written for one: setup_inputs(seed, part) draws one part's arguments, and reference() takes and returns one part's arrays. A program takes and returns all parts, laid end to end along the dimension named above; an argument that names none is the same for every part. Nothing has to cross between parts.
Inputs may be any that keep to these rules, and one draw needn't show every extreme that they name: Token i of half r sees prefix positions 0 to visible[r, i] - 1; in each half some token sees the whole prefix.
All inputs are finite; a program needn't handle non-finite values.
Results may differ from the reference program's by a relative error of at most 0.0051.
Values may be sent and summed in bfloat16 or wider, within the bound.
No kernel may reach another device: no remote copies, remote signals or barrier semaphores. Data moves between devices by JAX's collectives and lax.ppermute only.
A program may use at most 64 MiB of HBM per device.

```python
import math
import jax
import jax.numpy as jnp
from jax import lax

D = 8192
QUERY_HEAD_COUNT = 64
KEY_VALUE_HEADS = 8
HEAD_WIDTH = 128
PB = 512
PREFIX_LENGTH = 2048
HALF_TOKENS = 64
N_REP = 2


def draw_queries(key, part):
    sampled_items = 2.5 * jax.random.normal(jax.random.fold_in(key, 11), (N_REP, HALF_TOKENS, QUERY_HEAD_COUNT * HEAD_WIDTH), jnp.float32)
    sampled_items = jnp.clip(sampled_items, -7.5, 7.5)
    return sampled_items.astype(jnp.bfloat16)


def draw_prefix_keys(key, part):
    sampled_items = jax.random.normal(jax.random.fold_in(key, 12), (PREFIX_LENGTH, KEY_VALUE_HEADS * HEAD_WIDTH), jnp.float32)
    sampled_items = jnp.clip(sampled_items, -6.0, 6.0)
    return sampled_items.astype(jnp.bfloat16)


def draw_visible(key, part):
    cutoffs = jax.random.randint(jax.random.fold_in(key, 21), (N_REP, HALF_TOKENS), PREFIX_LENGTH // 16, PREFIX_LENGTH + 1)
    full_rows = jax.random.randint(jax.random.fold_in(key, 22), (N_REP, HALF_TOKENS), 0, 16) == 0
    cutoffs = jnp.where(full_rows, PREFIX_LENGTH, cutoffs)
    return cutoffs.at[:, 0].set(PREFIX_LENGTH).astype(jnp.int32)


def steps_of(own_key, extent, cuts, smallest, largest):
    level = 1.0
    for axis_at, blocks in cuts:
        heights = jax.random.uniform(jax.random.fold_in(jax.random.fold_in(own_key, 6), axis_at), (blocks,), jnp.float32, smallest / len(cuts), largest / len(cuts))
        level = level * jnp.repeat(jnp.exp(heights), extent[axis_at] // blocks).reshape((-1,) + (1,) * (len(extent) - 1 - axis_at))
    return level


def centred(rng, shape, scale, limit, cuts=(), held_as=jnp.bfloat16):
    gain = steps_of(rng, shape, cuts, -0.22, 0.18) if cuts else 1.0
    array = jax.random.normal(rng, shape, jnp.float32) * scale * gain
    return jnp.minimum(jnp.maximum(array, -limit), limit).astype(held_as)


def setup_inputs(seed: int = 0, part: int = 0) -> dict:
    arg_keys = jax.random.split(jax.random.key(seed), 8)
    part_keys = jax.random.split(jax.random.fold_in(arg_keys[7], part), 8)
    return {
        "queries": draw_queries(jax.random.fold_in(jax.random.fold_in(arg_keys[7], part), 71), part),
        "fresh_key_rows": centred(part_keys[1], (N_REP, HALF_TOKENS, KEY_VALUE_HEADS * HEAD_WIDTH), 2.0, 8.0, ((0, 2), (1, 8))),
        "fresh_value_rows": centred(part_keys[2], (N_REP, HALF_TOKENS, KEY_VALUE_HEADS * HEAD_WIDTH), 2.0, 8.0, ((0, 2), (1, 8))),
        "visible": draw_visible(jax.random.fold_in(jax.random.fold_in(arg_keys[7], part), 71), part),
        "prefix_keys": draw_prefix_keys(jax.random.fold_in(jax.random.fold_in(arg_keys[7], part), 71), part),
        "cached_value_rows": centred(part_keys[5], (PREFIX_LENGTH, KEY_VALUE_HEADS * HEAD_WIDTH), 2.0, 8.0, ((0, 4), (1, 2))),
        "out_weight": centred(arg_keys[6], (QUERY_HEAD_COUNT * HEAD_WIDTH, D), (QUERY_HEAD_COUNT * HEAD_WIDTH) ** -0.5, 0.0625, ((0, 2), (1, 4))),
    }


def attend(query_tile_rows, self_key_rows, own_values, lengths, key_table, value_table):
    logit_scale = 1.0 / math.sqrt(query_tile_rows.shape[-1])
    block_count = key_table.shape[0] // PB
    scores = jnp.einsum('bkgd,pkd->bkgp', query_tile_rows, key_table) * logit_scale
    self_score_row = jnp.einsum('tprl,tpl->tpr', query_tile_rows, self_key_rows) * logit_scale
    position = jnp.arange(key_table.shape[0])
    visible_mask = (position[None, :] < lengths[:, None])[:, None, None, :]
    shape_now = scores.shape[:3] + (block_count, PB)
    scores = scores.reshape(shape_now)
    visible_mask = jnp.broadcast_to(visible_mask, scores.shape[:3] + (key_table.shape[0],)).reshape(shape_now)
    block_peak = lax.optimization_barrier(jnp.max(jnp.where(visible_mask, scores, -jnp.inf), axis=-1))
    anchor = jnp.where(jnp.isinf(block_peak), 0.0, block_peak)
    raw_weights = jnp.where(visible_mask, jnp.exp(scores - anchor[..., None]), 0.0)
    block_sum = lax.optimization_barrier(jnp.sum(raw_weights, axis=-1))
    weights = lax.optimization_barrier(raw_weights.astype(jnp.bfloat16)).astype(jnp.float32)
    values_blocked = value_table.reshape(block_count, PB, value_table.shape[1], value_table.shape[2])
    block_context = jnp.einsum('bkgnp,npkd->bkgnd', weights, values_blocked)
    row_peak = jnp.maximum(lax.optimization_barrier(jnp.max(block_peak, axis=-1)), self_score_row)
    fade = jnp.exp(block_peak - row_peak[..., None])
    raw_own = jnp.exp(self_score_row - row_peak)
    weight_own = lax.optimization_barrier(raw_own.astype(jnp.bfloat16)).astype(jnp.float32)
    denominator = lax.optimization_barrier(jnp.sum(block_sum * fade, axis=-1)) + raw_own
    summed = lax.optimization_barrier(jnp.sum(block_context * fade[..., None], axis=3))
    summed = summed + weight_own[..., None] * own_values[:, :, None, :]
    return (summed / denominator[..., None]).astype(jnp.bfloat16)

def reference(queries, fresh_key_rows, fresh_value_rows, visible, prefix_keys, cached_value_rows, out_weight):
    halves, tokens, feature_width = queries.shape
    kv_heads = prefix_keys.shape[1] // HEAD_WIDTH
    per_group = feature_width // (kv_heads * HEAD_WIDTH)
    key_table = prefix_keys.astype(jnp.float32).reshape(-1, kv_heads, HEAD_WIDTH)
    value_table = cached_value_rows.astype(jnp.float32).reshape(-1, kv_heads, HEAD_WIDTH)
    token_block = math.gcd(tokens, 32)
    blocks_count = tokens // token_block
    outputs = []
    for half_index in range(halves):
        query_all = queries[half_index].astype(jnp.float32).reshape(blocks_count, token_block, kv_heads, per_group, HEAD_WIDTH)
        keys_own = fresh_key_rows[half_index].astype(jnp.float32).reshape(blocks_count, token_block, kv_heads, HEAD_WIDTH)
        values_own = fresh_value_rows[half_index].astype(jnp.float32).reshape(blocks_count, token_block, kv_heads, HEAD_WIDTH)
        lengths = visible[half_index].reshape(blocks_count, token_block)

        def attend_block(pieces):
            return attend(pieces[0], pieces[1], pieces[2], pieces[3], key_table, value_table)
        context = lax.map(attend_block, (query_all, keys_own, values_own, lengths)).reshape(tokens, feature_width)
        outputs.append(jnp.dot(context, out_weight, preferred_element_type=jnp.float32).astype(jnp.bfloat16))
    return jnp.stack(outputs)
```

```python
import functools
import math

import jax
import jax.numpy as jnp
from jax import lax
from jax.experimental import pallas as pl
from jax.experimental.pallas import tpu as pltpu
from jax.sharding import PartitionSpec as P

HEAD_WIDTH = 128
HIDDEN = -1e30
SCALE = 1.0 / math.sqrt(HEAD_WIDTH)


def block_partial(query_heads, lengths, key_rows, value_rows, offset):
    kv_heads = query_heads.shape[1]
    row_count = key_rows.shape[0]
    step_rows = math.gcd(row_count, 512)
    stat_shape = query_heads.shape[:3]

    def masked_scores(turn_index):
        first_row = turn_index * step_rows
        key_block = lax.dynamic_slice_in_dim(key_rows, first_row, step_rows, 0)
        key_block = key_block.reshape(step_rows, kv_heads, HEAD_WIDTH)
        scores = (
            jnp.einsum("tkgd,pkd->tkgp", query_heads, key_block, preferred_element_type=jnp.float32)
            * SCALE
        )
        position = offset + first_row + jnp.arange(step_rows, dtype=jnp.int32)
        visible_mask = (position[None, :] < lengths[:, None])[:, None, None, :]
        return (scores, visible_mask, first_row)

    def peak_step(turn_index, peak_now):
        scores, visible_mask, _ = masked_scores(turn_index)
        return jnp.maximum(peak_now, jnp.max(jnp.where(visible_mask, scores, -jnp.inf), axis=-1))

    block_peak = lax.fori_loop(
        0, row_count // step_rows, peak_step, jnp.full(stat_shape, -jnp.inf, jnp.float32)
    )
    anchor = jnp.where(jnp.isinf(block_peak), 0.0, block_peak)

    def weight_step(turn_index, state_now):
        sum_now, acc_now = state_now
        scores, visible_mask, first_row = masked_scores(turn_index)
        value_block = lax.dynamic_slice_in_dim(value_rows, first_row, step_rows, 0)
        value_block = value_block.reshape(step_rows, kv_heads, HEAD_WIDTH)
        weights = jnp.where(visible_mask, jnp.exp(scores - anchor[..., None]), 0.0)
        sum_now = sum_now + jnp.sum(weights, axis=-1)
        acc_now = acc_now + jnp.einsum(
            "tkgp,pkd->tkgd",
            weights.astype(jnp.bfloat16),
            value_block,
            preferred_element_type=jnp.float32,
        )
        return (sum_now, acc_now)

    block_sum, block_acc = lax.fori_loop(
        0,
        row_count // step_rows,
        weight_step,
        (jnp.zeros(stat_shape, jnp.float32), jnp.zeros(query_heads.shape, jnp.float32)),
    )
    return (block_peak, block_sum, block_acc)


def shards_any(
    queries, fresh_key_rows, fresh_value_rows, visible, prefix_keys, cached_value_rows, out_weight
):
    query_rows, self_key_rows, own_values = (
        lax.all_to_all(queries[0], "tp", split_axis=1, concat_axis=0, tiled=True),
        lax.all_to_all(fresh_key_rows[0], "tp", split_axis=1, concat_axis=0, tiled=True),
        lax.all_to_all(fresh_value_rows[0], "tp", split_axis=1, concat_axis=0, tiled=True),
    )
    kv_heads = prefix_keys.shape[1] // HEAD_WIDTH
    tok_rows = query_rows.shape[0]
    block_rows = prefix_keys.shape[0]
    per_group = query_rows.shape[1] // (kv_heads * HEAD_WIDTH)
    seq_index = lax.axis_index("seq")
    query_heads = query_rows.reshape(tok_rows, kv_heads, per_group, HEAD_WIDTH)
    self_key_rows = self_key_rows.reshape(tok_rows, kv_heads, HEAD_WIDTH)
    own_vectors = own_values.reshape(tok_rows, kv_heads, 1, HEAD_WIDTH).astype(jnp.float32)
    self_score_row = (
        jnp.einsum(
            "tkgd,tkd->tkg", query_heads, self_key_rows, preferred_element_type=jnp.float32
        )
        * SCALE
    )
    seq_count = lax.axis_size("seq")
    everyone = lax.all_gather(query_rows, "seq", axis=0, tiled=True)
    blocks = everyone.reshape(seq_count, tok_rows, kv_heads, per_group, HEAD_WIDTH)
    all_lengths = visible[0].reshape(seq_count, tok_rows)
    prefix_start = seq_index * block_rows

    def partial_block(item_pair):
        return block_partial(
            item_pair[0], item_pair[1], prefix_keys, cached_value_rows, prefix_start
        )

    part_max, part_sum, part_acc = lax.map(partial_block, (blocks, all_lengths))
    part_max, part_sum, part_acc = (
        lax.all_to_all(part_max, "seq", split_axis=0, concat_axis=0, tiled=True),
        lax.all_to_all(part_sum, "seq", split_axis=0, concat_axis=0, tiled=True),
        lax.all_to_all(part_acc, "seq", split_axis=0, concat_axis=0, tiled=True),
    )
    run_max = jnp.max(part_max, axis=0)
    anchor = jnp.where(jnp.isinf(run_max), 0.0, run_max)
    part_factor = jnp.exp(part_max - anchor[None])
    run_sum = jnp.sum(part_sum * part_factor, axis=0)
    run_acc = jnp.sum(part_acc * part_factor[..., None], axis=0)
    row_peak = jnp.maximum(run_max, self_score_row)
    fade = jnp.exp(run_max - row_peak)
    own_weight = jnp.exp(self_score_row - row_peak)
    own_rounded = lax.optimization_barrier(own_weight.astype(jnp.bfloat16)).astype(jnp.float32)
    total_sum = run_sum * fade + own_weight
    total_acc = run_acc * fade[..., None] + own_rounded[..., None] * own_vectors
    context = (
        (total_acc / total_sum[..., None])
        .astype(jnp.bfloat16)
        .reshape(tok_rows, kv_heads * per_group * HEAD_WIDTH)
    )
    partial_out = jnp.dot(
        lax.all_gather(context, "seq", axis=0, tiled=True),
        out_weight,
        preferred_element_type=jnp.float32,
    )
    summed = lax.psum_scatter(partial_out, "tp", scatter_dimension=0, tiled=True)
    return summed.astype(jnp.bfloat16)[None]


def swap(array, axis, mask):
    return lax.ppermute(array, axis, [(i, i ^ mask) for i in range(lax.axis_size(axis))])


def lanes(array, index, width):
    return lax.dynamic_slice_in_dim(array, index * width, width, 1)


def stack_heads(rows, heads):
    return jnp.concatenate(
        [rows[:, h * HEAD_WIDTH : (h + 1) * HEAD_WIDTH] for h in range(heads)], axis=0
    )


def attend_step(query, lengths, offset, keys, values, peak, total, acc):
    scores = (
        lax.dot_general(query, keys, (((1,), (1,)), ((), ())), preferred_element_type=jnp.float32)
        * SCALE
    )
    position = offset + lax.broadcasted_iota(jnp.int32, scores.shape, 1)
    scores = jnp.where(position < lengths, scores, HIDDEN)
    new_peak = jnp.maximum(peak, jnp.max(scores, axis=-1, keepdims=True))
    weights = jnp.exp(scores - new_peak)
    fade = jnp.exp(peak - new_peak)
    total = total * fade + jnp.sum(weights, axis=-1, keepdims=True)
    acc = acc * fade + jnp.dot(
        weights.astype(jnp.bfloat16), values, preferred_element_type=jnp.float32
    )
    return new_peak, total, acc


def attend_first(heads, where_ref, q_ref, len_ref, k_ref, v_ref, peak_ref, total_ref, acc_ref):
    tokens = q_ref.shape[0]
    q_width = heads * HEAD_WIDTH
    offset = where_ref[0]
    fresh_key = q_ref[:, q_width : q_width + HEAD_WIDTH].astype(jnp.float32)
    fresh_value = q_ref[:, q_width + HEAD_WIDTH :].astype(jnp.float32)
    lengths = len_ref[...]
    for h in range(heads):
        query = q_ref[:, h * HEAD_WIDTH : (h + 1) * HEAD_WIDTH]
        own = jnp.sum(query.astype(jnp.float32) * fresh_key, axis=-1, keepdims=True) * SCALE
        peak, total, acc = attend_step(
            query,
            lengths,
            offset,
            k_ref[...],
            v_ref[...],
            own,
            jnp.ones_like(own),
            fresh_value,
        )
        rows = slice(h * tokens, (h + 1) * tokens)
        peak_ref[rows, :] = peak
        total_ref[rows, :] = total
        acc_ref[rows, :] = acc


def attend_more(
    heads, blocks, last, where_ref, q_ref, len_ref, peak_in, total_in, acc_in, *refs
):
    pieces, outs = refs[:blocks], refs[blocks:]
    tokens = q_ref.shape[0]
    lengths = len_ref[...]
    for h in range(heads):
        query = q_ref[:, h * HEAD_WIDTH : (h + 1) * HEAD_WIDTH]
        rows = slice(h * tokens, (h + 1) * tokens)
        state = (peak_in[rows, :], total_in[rows, :], acc_in[rows, :])
        for b in range(blocks):
            half = pieces[b].shape[0] // 2
            state = attend_step(
                query,
                lengths,
                where_ref[b],
                pieces[b][:half, :],
                pieces[b][half:, :],
                *state,
            )
        peak, total, acc = state
        if last:
            outs[0][:, h * HEAD_WIDTH : (h + 1) * HEAD_WIDTH] = (acc / total).astype(jnp.bfloat16)
        else:
            for ref, value in zip(outs, state):
                ref[rows, :] = value


def in_vmem():
    return pl.BlockSpec(memory_space=pltpu.VMEM)


def in_smem():
    return pl.BlockSpec(memory_space=pltpu.SMEM)


def cost(flops, bytes_accessed, transcendentals=0):
    return pl.CostEstimate(
        flops=flops, bytes_accessed=bytes_accessed, transcendentals=transcendentals
    )


def state_shapes(rows):
    return (
        jax.ShapeDtypeStruct((rows, 1), jnp.float32),
        jax.ShapeDtypeStruct((rows, 1), jnp.float32),
        jax.ShapeDtypeStruct((rows, HEAD_WIDTH), jnp.float32),
    )


def first_call(heads, where, query, lengths, keys, values):
    rows = query.shape[0] * heads
    return pl.pallas_call(
        functools.partial(attend_first, heads),
        out_shape=state_shapes(rows),
        in_specs=[in_smem()] + [in_vmem()] * 4,
        out_specs=(in_vmem(),) * 3,
        compiler_params=pltpu.CompilerParams(vmem_limit_bytes=24 * 2**20),
        cost_estimate=cost(
            4 * rows * keys.shape[0] * HEAD_WIDTH, 2**20, rows * keys.shape[0]
        ),
        name="attend_first",
    )(where, query, lengths, keys, values)


def more_call(heads, last, where, query, lengths, state, pieces):
    tokens = query.shape[0]
    rows = tokens * heads
    positions = sum(p.shape[0] // 2 for p in pieces)
    shapes = (
        jax.ShapeDtypeStruct((tokens, heads * HEAD_WIDTH), jnp.bfloat16)
        if last
        else state_shapes(rows)
    )
    return pl.pallas_call(
        functools.partial(attend_more, heads, len(pieces), last),
        out_shape=shapes,
        in_specs=[in_smem()] + [in_vmem()] * (5 + len(pieces)),
        out_specs=in_vmem() if last else (in_vmem(),) * 3,
        compiler_params=pltpu.CompilerParams(vmem_limit_bytes=24 * 2**20),
        cost_estimate=cost(4 * rows * positions * HEAD_WIDTH, 2**20, rows * positions),
        name="attend_last" if last else "attend_more",
    )(where, query, lengths, *state, *pieces)


def project_kernel(row_ref, x_ref, w_ref, *refs):
    part = jnp.dot(x_ref[...], w_ref[...], preferred_element_type=jnp.float32)
    if len(refs) == 2:
        part = part + refs[0][...]
    refs[-1][...] = part


def project(row_block, context, weight, acc):
    tokens, depth = context.shape
    columns = weight.shape[1]
    step = math.gcd(columns, 512)
    specs = [
        pl.BlockSpec((tokens, depth), lambda n, row: (0, 0)),
        pl.BlockSpec((depth, step), lambda n, row: (row[0], n)),
    ]
    operands = [context, weight]
    if acc is not None:
        specs.append(pl.BlockSpec((tokens, step), lambda n, row: (0, n)))
        operands.append(acc)
    return pl.pallas_call(
        project_kernel,
        out_shape=jax.ShapeDtypeStruct((tokens, columns), jnp.float32),
        grid_spec=pltpu.PrefetchScalarGridSpec(
            num_scalar_prefetch=1,
            grid=(columns // step,),
            in_specs=specs,
            out_specs=pl.BlockSpec((tokens, step), lambda n, row: (0, n)),
        ),
        compiler_params=pltpu.CompilerParams(vmem_limit_bytes=24 * 2**20),
        cost_estimate=cost(2 * tokens * depth * columns, 2 * depth * columns),
        name="project",
    )(row_block, *operands)


def shards_by_head(
    queries, fresh_key_rows, fresh_value_rows, visible, prefix_keys, cached_value_rows, out_weight
):
    seq_count = lax.axis_size("seq")
    seq, tp, rep = lax.axis_index("seq"), lax.axis_index("tp"), lax.axis_index("rep")
    block_rows = prefix_keys.shape[0]
    half_rows = block_rows // 2
    heads = queries.shape[2] // (fresh_key_rows.shape[2])
    masks = list(range(1, seq_count))

    key_half = lax.dynamic_slice_in_dim(prefix_keys, rep * half_rows, half_rows, 0)
    value_half = lax.dynamic_slice_in_dim(cached_value_rows, rep * half_rows, half_rows, 0)
    halves = []
    for mask in masks:
        piece = jnp.concatenate(
            [lanes(key_half, seq ^ mask, HEAD_WIDTH), lanes(value_half, seq ^ mask, HEAD_WIDTH)]
        )
        halves.append(swap(piece, "seq", mask))

    rows = [queries[0], fresh_key_rows[0], fresh_value_rows[0]]
    away = jnp.concatenate([lanes(a, 1 - tp, a.shape[1] // 2) for a in rows], axis=1)
    home = jnp.concatenate([lanes(a, tp, a.shape[1] // 2) for a in rows], axis=1)
    arrived = swap(away, "tp", 1)
    both = jnp.concatenate([jnp.where(tp == 0, home, arrived), jnp.where(tp == 0, arrived, home)])
    widths = [a.shape[1] // 2 for a in rows]
    starts = [0, widths[0], widths[0] + widths[1]]

    def for_head(index):
        parts = [both[:, s : s + w] for s, w in zip(starts, widths)]
        return jnp.concatenate([lanes(p, index, p.shape[1] // seq_count) for p in parts], axis=1)

    blocks = [for_head(seq)] + [swap(for_head(seq ^ m), "seq", m) for m in masks]
    stacked = jnp.stack(blocks)
    query = jnp.concatenate([lax.dynamic_index_in_dim(stacked, seq ^ b, 0, False) for b in range(seq_count)])
    lengths = visible[0][:, None]

    other = [swap(h, "rep", 1) for h in halves]

    def place(mask, core):
        return (seq ^ mask) * block_rows + core * half_rows

    state = first_call(
        heads,
        (seq * block_rows)[None],
        query,
        lengths,
        lanes(prefix_keys, seq, HEAD_WIDTH),
        lanes(cached_value_rows, seq, HEAD_WIDTH),
    )
    for i, mask in enumerate(masks):
        state = more_call(
            heads,
            i == len(masks) - 1,
            jnp.stack([place(mask, rep), place(mask, 1 - rep)]),
            query,
            lengths,
            state,
            [halves[i], other[i]],
        )
    context = state
    gathered = [context] + [swap(context, "seq", m) for m in masks]
    acc = None
    for mask, chunk in zip([0] + masks, gathered):
        acc = project((seq ^ mask)[None], chunk, out_weight, acc)
    keep_rows = acc.shape[0] // 2
    keep = lax.dynamic_slice_in_dim(acc, tp * keep_rows, keep_rows, 0)
    send = lax.dynamic_slice_in_dim(acc, (1 - tp) * keep_rows, keep_rows, 0)
    got = swap(send.astype(jnp.bfloat16), "tp", 1)
    return (keep + got.astype(jnp.float32)).astype(jnp.bfloat16)[None]


def solution(mesh):
    in_specs = (
        P("rep", ("groups", "seq", "tp"), None),
        P("rep", ("groups", "seq", "tp"), None),
        P("rep", ("groups", "seq", "tp"), None),
        P("rep", "groups"),
        P(("groups", "seq"), "tp"),
        P(("groups", "seq"), "tp"),
        P("tp", "seq"),
    )
    out_specs = P("rep", ("groups", "tp"), "seq")
    sizes = mesh.shape
    seq_count = sizes["seq"]

    def shards(*args):
        local_heads = args[4].shape[1] // HEAD_WIDTH
        by_head = (
            local_heads == seq_count
            and seq_count & (seq_count - 1) == 0
            and sizes["tp"] == 2
            and sizes["rep"] == 2
        )
        return (shards_by_head if by_head else shards_any)(*args)

    return jax.shard_map(shards, mesh=mesh, in_specs=in_specs, out_specs=out_specs, check_vma=False)
```

```python
import functools
import math

import jax
import jax.numpy as jnp
from jax import lax
from jax.experimental import pallas as pl
from jax.experimental.pallas import tpu as pltpu
from jax.sharding import PartitionSpec as P

HEAD_WIDTH = 128
HIDDEN = -1e30
SCALE = 1.0 / math.sqrt(HEAD_WIDTH)


def block_partial(query_heads, lengths, key_rows, value_rows, offset):
    kv_heads = query_heads.shape[1]
    row_count = key_rows.shape[0]
    step_rows = math.gcd(row_count, 512)
    stat_shape = query_heads.shape[:3]

    def masked_scores(turn_index):
        first_row = turn_index * step_rows
        key_block = lax.dynamic_slice_in_dim(key_rows, first_row, step_rows, 0)
        key_block = key_block.reshape(step_rows, kv_heads, HEAD_WIDTH)
        scores = (
            jnp.einsum("tkgd,pkd->tkgp", query_heads, key_block, preferred_element_type=jnp.float32)
            * SCALE
        )
        position = offset + first_row + jnp.arange(step_rows, dtype=jnp.int32)
        visible_mask = (position[None, :] < lengths[:, None])[:, None, None, :]
        return (scores, visible_mask, first_row)

    def peak_step(turn_index, peak_now):
        scores, visible_mask, _ = masked_scores(turn_index)
        return jnp.maximum(peak_now, jnp.max(jnp.where(visible_mask, scores, -jnp.inf), axis=-1))

    block_peak = lax.fori_loop(
        0, row_count // step_rows, peak_step, jnp.full(stat_shape, -jnp.inf, jnp.float32)
    )
    anchor = jnp.where(jnp.isinf(block_peak), 0.0, block_peak)

    def weight_step(turn_index, state_now):
        sum_now, acc_now = state_now
        scores, visible_mask, first_row = masked_scores(turn_index)
        value_block = lax.dynamic_slice_in_dim(value_rows, first_row, step_rows, 0)
        value_block = value_block.reshape(step_rows, kv_heads, HEAD_WIDTH)
        weights = jnp.where(visible_mask, jnp.exp(scores - anchor[..., None]), 0.0)
        sum_now = sum_now + jnp.sum(weights, axis=-1)
        acc_now = acc_now + jnp.einsum(
            "tkgp,pkd->tkgd",
            weights.astype(jnp.bfloat16),
            value_block,
            preferred_element_type=jnp.float32,
        )
        return (sum_now, acc_now)

    block_sum, block_acc = lax.fori_loop(
        0,
        row_count // step_rows,
        weight_step,
        (jnp.zeros(stat_shape, jnp.float32), jnp.zeros(query_heads.shape, jnp.float32)),
    )
    return (block_peak, block_sum, block_acc)


def shards_any(
    queries, fresh_key_rows, fresh_value_rows, visible, prefix_keys, cached_value_rows, out_weight
):
    query_rows, self_key_rows, own_values = (
        lax.all_to_all(queries[0], "tp", split_axis=1, concat_axis=0, tiled=True),
        lax.all_to_all(fresh_key_rows[0], "tp", split_axis=1, concat_axis=0, tiled=True),
        lax.all_to_all(fresh_value_rows[0], "tp", split_axis=1, concat_axis=0, tiled=True),
    )
    kv_heads = prefix_keys.shape[1] // HEAD_WIDTH
    tok_rows = query_rows.shape[0]
    block_rows = prefix_keys.shape[0]
    per_group = query_rows.shape[1] // (kv_heads * HEAD_WIDTH)
    seq_index = lax.axis_index("seq")
    query_heads = query_rows.reshape(tok_rows, kv_heads, per_group, HEAD_WIDTH)
    self_key_rows = self_key_rows.reshape(tok_rows, kv_heads, HEAD_WIDTH)
    own_vectors = own_values.reshape(tok_rows, kv_heads, 1, HEAD_WIDTH).astype(jnp.float32)
    self_score_row = (
        jnp.einsum(
            "tkgd,tkd->tkg", query_heads, self_key_rows, preferred_element_type=jnp.float32
        )
        * SCALE
    )
    seq_count = lax.axis_size("seq")
    everyone = lax.all_gather(query_rows, "seq", axis=0, tiled=True)
    blocks = everyone.reshape(seq_count, tok_rows, kv_heads, per_group, HEAD_WIDTH)
    all_lengths = visible[0].reshape(seq_count, tok_rows)
    prefix_start = seq_index * block_rows

    def partial_block(item_pair):
        return block_partial(
            item_pair[0], item_pair[1], prefix_keys, cached_value_rows, prefix_start
        )

    part_max, part_sum, part_acc = lax.map(partial_block, (blocks, all_lengths))
    part_max, part_sum, part_acc = (
        lax.all_to_all(part_max, "seq", split_axis=0, concat_axis=0, tiled=True),
        lax.all_to_all(part_sum, "seq", split_axis=0, concat_axis=0, tiled=True),
        lax.all_to_all(part_acc, "seq", split_axis=0, concat_axis=0, tiled=True),
    )
    run_max = jnp.max(part_max, axis=0)
    anchor = jnp.where(jnp.isinf(run_max), 0.0, run_max)
    part_factor = jnp.exp(part_max - anchor[None])
    run_sum = jnp.sum(part_sum * part_factor, axis=0)
    run_acc = jnp.sum(part_acc * part_factor[..., None], axis=0)
    row_peak = jnp.maximum(run_max, self_score_row)
    fade = jnp.exp(run_max - row_peak)
    own_weight = jnp.exp(self_score_row - row_peak)
    own_rounded = lax.optimization_barrier(own_weight.astype(jnp.bfloat16)).astype(jnp.float32)
    total_sum = run_sum * fade + own_weight
    total_acc = run_acc * fade[..., None] + own_rounded[..., None] * own_vectors
    context = (
        (total_acc / total_sum[..., None])
        .astype(jnp.bfloat16)
        .reshape(tok_rows, kv_heads * per_group * HEAD_WIDTH)
    )
    partial_out = jnp.dot(
        lax.all_gather(context, "seq", axis=0, tiled=True),
        out_weight,
        preferred_element_type=jnp.float32,
    )
    summed = lax.psum_scatter(partial_out, "tp", scatter_dimension=0, tiled=True)
    return summed.astype(jnp.bfloat16)[None]


EXPONENT = SCALE * math.log2(math.e)
VMEM_BYTES = 20 * 2**20
SETTLE = 10**11
ORDER = -1
PACK_BYTES = int(63.5 * 2**20)
PROJECT_BYTES = 16 * 2**20
LOAD_BYTES = 30 * 2**20


def swap(array, axis, mask):
    return lax.ppermute(array, axis, [(i, i ^ mask) for i in range(lax.axis_size(axis))])


def tile_at(index, width):
    return pl.ds(pl.multiple_of(index * width, width), width)


def side_by_side(array, times):
    return jnp.concatenate([array] * times, axis=1)


def vmem():
    return pl.BlockSpec(memory_space=pltpu.VMEM)


def hbm():
    return pl.BlockSpec(memory_space=pltpu.HBM)


def params(limit=VMEM_BYTES):
    return pltpu.CompilerParams(vmem_limit_bytes=limit)


def cost(flops, bytes_accessed, transcendentals=0):
    return pl.CostEstimate(
        flops=flops, bytes_accessed=bytes_accessed, transcendentals=transcendentals
    )


def pack_prefix_kernel(masks, k_ref, v_ref, own_ref, *piece_refs):
    seq, rep = lax.axis_index("seq"), lax.axis_index("rep")
    rows = k_ref.shape[0]
    half = rows // 2
    for j, table in enumerate((k_ref, v_ref)):
        for mask, piece in zip(masks, piece_refs):
            piece[j * half : (j + 1) * half, :] = table[
                tile_at(rep, half), tile_at(seq ^ mask, HEAD_WIDTH)
            ]
    for j, table in enumerate((k_ref, v_ref)):
        own_ref[j * rows : (j + 1) * rows, :] = table[:, tile_at(seq, HEAD_WIDTH)]


def pack_prefix(prefix_keys, cached_value_rows, masks):
    rows = prefix_keys.shape[0]
    heights = [2 * rows] + [rows] * len(masks)
    return pl.pallas_call(
        functools.partial(pack_prefix_kernel, masks),
        out_shape=[jax.ShapeDtypeStruct((n, HEAD_WIDTH), jnp.bfloat16) for n in heights],
        in_specs=[vmem()] * 2,
        out_specs=[vmem()] * len(heights),
        compiler_params=params(),
        cost_estimate=cost(0, 2 * 2**20),
        name="pack_prefix",
    )(prefix_keys, cached_value_rows)


def pack_queries_kernel(seq_count, q_ref, fk_ref, fv_ref, out_ref):
    tokens = q_ref.shape[0]
    count = out_ref.shape[0] // tokens
    for owner in range(count):
        head = owner % 2 * seq_count + owner // 2
        to = 0
        for ref in (q_ref, fk_ref, fv_ref):
            part = ref.shape[1] // count
            out_ref[owner * tokens : (owner + 1) * tokens, to : to + part] = ref[
                :, head * part : (head + 1) * part
            ]
            to += part


def pack_queries(rows, seq_count):
    count = 2 * seq_count
    shape = (rows[0].shape[0] * count, sum(a.shape[1] for a in rows) // count)
    return pl.pallas_call(
        functools.partial(pack_queries_kernel, seq_count),
        out_shape=jax.ShapeDtypeStruct(shape, jnp.bfloat16),
        in_specs=[vmem()] * 3,
        out_specs=vmem(),
        compiler_params=params(),
        cost_estimate=cost(0, 2**19),
        name="pack_queries",
    )(*rows)


def settle_kernel(*refs):
    del refs


def settle(arrays):
    count = len(arrays)
    return pl.pallas_call(
        settle_kernel,
        out_shape=[jax.ShapeDtypeStruct(a.shape, a.dtype) for a in arrays],
        in_specs=[vmem()] * count,
        out_specs=[vmem()] * count,
        input_output_aliases={i: i for i in range(count)},
        compiler_params=params(2**20),
        cost_estimate=cost(SETTLE, 2**20),
        name="settle",
    )(*arrays)


def lengths_kernel(visible_ref, out_ref):
    tokens = out_ref.shape[0]
    diagonal = lax.broadcasted_iota(jnp.int32, (tokens, tokens), 0) == lax.broadcasted_iota(
        jnp.int32, (tokens, tokens), 1
    )
    lengths = jnp.sum(jnp.where(diagonal, visible_ref[...], 0), axis=-1, keepdims=True)
    out_ref[...] = jnp.broadcast_to(lengths, out_ref.shape)


def spread_lengths(visible):
    return pl.pallas_call(
        lengths_kernel,
        out_shape=jax.ShapeDtypeStruct((visible.shape[1], HEAD_WIDTH), jnp.int32),
        in_specs=[vmem()],
        out_specs=vmem(),
        compiler_params=params(),
        cost_estimate=cost(0, 2**15),
        name="spread_lengths",
    )(visible)


def attend_step(query, lengths, position, keys, values, peak, acc):
    count = keys.shape[0]
    scores = lax.dot_general(
        query, keys, (((1,), (1,)), ((), ())), preferred_element_type=jnp.float32
    )
    scores = jnp.where(position < side_by_side(lengths, count // HEAD_WIDTH), scores, HIDDEN)
    new_peak = jnp.maximum(peak, jnp.max(scores, axis=-1, keepdims=True))
    weights = jnp.exp2((scores - side_by_side(new_peak, count // HEAD_WIDTH)) * EXPONENT)
    fade = jnp.exp2((peak - new_peak) * EXPONENT)
    with_ones = jnp.concatenate([values, jnp.ones_like(values)], axis=1)
    acc = acc * side_by_side(fade, 2) + jnp.dot(
        weights.astype(jnp.bfloat16), with_ones, preferred_element_type=jnp.float32
    )
    return new_peak, acc


def join(refs, first, count):
    return jnp.concatenate([ref[first : first + count, :] for ref in refs], axis=0)


def attend_first_kernel(
    heads, block_rows, rows_ref, lengths_ref, own_ref, stacked_ref, peak_ref, acc_ref
):
    seq = lax.axis_index("seq")
    tokens = rows_ref.shape[0]
    lengths = lengths_ref[...]
    width = heads * HEAD_WIDTH
    fresh_key = rows_ref[:, width : width + HEAD_WIDTH].astype(jnp.float32)
    fresh_value = rows_ref[:, width + HEAD_WIDTH :].astype(jnp.float32)
    start = jnp.concatenate([fresh_value, jnp.ones_like(fresh_value)], axis=1)
    keys, values = own_ref[:block_rows, :], own_ref[block_rows:, :]
    position = seq * block_rows + lax.broadcasted_iota(jnp.int32, (1, block_rows), 1)
    for h in range(0, heads, 2):
        rows = slice(h * tokens, (h + 2) * tokens)
        query = jnp.concatenate(
            [rows_ref[:, i * HEAD_WIDTH : (i + 1) * HEAD_WIDTH] for i in (h, h + 1)], axis=0
        )
        own = jnp.sum(
            query.astype(jnp.float32) * jnp.concatenate([fresh_key] * 2, axis=0),
            axis=-1,
            keepdims=True,
        )
        stacked_ref[rows, :] = query
        peak, acc = attend_step(
            query,
            jnp.concatenate([lengths] * 2, axis=0),
            position,
            keys,
            values,
            jnp.broadcast_to(own, (2 * tokens, HEAD_WIDTH)),
            jnp.concatenate([start] * 2, axis=0),
        )
        peak_ref[rows, :] = peak
        acc_ref[rows, :] = acc


def attend_first(heads, query_rows, lengths, own):
    rows = heads * query_rows.shape[0]
    block_rows = own.shape[0] // 2
    return pl.pallas_call(
        functools.partial(attend_first_kernel, heads, block_rows),
        out_shape=(
            jax.ShapeDtypeStruct((rows, HEAD_WIDTH), jnp.bfloat16),
            jax.ShapeDtypeStruct((rows, HEAD_WIDTH), jnp.float32),
            jax.ShapeDtypeStruct((rows, 2 * HEAD_WIDTH), jnp.float32),
        ),
        in_specs=[vmem()] * 3,
        out_specs=(vmem(),) * 3,
        compiler_params=params(),
        cost_estimate=cost(6 * rows * block_rows * HEAD_WIDTH, 2**20, rows * block_rows),
        name="attend_first",
    )(query_rows, lengths, own)


def attend_more_kernel(
    block_rows, mask, last, query_ref, lengths_ref, peak_in, acc_in, mine_ref, other_ref, *outs
):
    seq, rep = lax.axis_index("seq"), lax.axis_index("rep")
    half = block_rows // 2
    tokens = lengths_ref.shape[0]
    lengths = jnp.concatenate([lengths_ref[...]] * 2, axis=0)
    base = (seq ^ mask) * 2 * half
    keys = join((mine_ref, other_ref), 0, half)
    values = join((mine_ref, other_ref), half, half)
    lane = lax.broadcasted_iota(jnp.int32, (1, 2 * half), 1)
    position = base + jnp.where(rep == 0, lane, jnp.where(lane < half, lane + half, lane - half))
    for first in range(0, query_ref.shape[0], 2 * tokens):
        rows = slice(first, first + 2 * tokens)
        state = peak_in[rows, :], acc_in[rows, :]
        state = attend_step(
            query_ref[rows, :], lengths, position, keys, values, *state
        )
        if last:
            context = state[1][:, :HEAD_WIDTH] / state[1][:, HEAD_WIDTH:]
            for i in range(2):
                column = (first // tokens + i) * HEAD_WIDTH
                outs[0][:, column : column + HEAD_WIDTH] = context[
                    i * tokens : (i + 1) * tokens, :
                ].astype(jnp.bfloat16)
        else:
            outs[0][rows, :], outs[1][rows, :] = state


def attend_more(positions, mask, last, stacked, lengths, state, mine, other):
    rows, tokens = stacked.shape[0], lengths.shape[0]
    shapes = (
        (jax.ShapeDtypeStruct((tokens, rows // tokens * HEAD_WIDTH), jnp.bfloat16),)
        if last
        else tuple(jax.ShapeDtypeStruct(a.shape, a.dtype) for a in state)
    )
    return pl.pallas_call(
        functools.partial(attend_more_kernel, positions, mask, last),
        out_shape=shapes,
        in_specs=[vmem()] * 6,
        out_specs=(vmem(),) * len(shapes),
        compiler_params=params(),
        cost_estimate=cost(6 * rows * positions * HEAD_WIDTH, 2**20, rows * positions),
        name="attend_last" if last else "attend_more",
    )(stacked, lengths, *state, mine, other)


def load_kernel(masks, weight_ref, *refs):
    tile_refs, sems = refs[:-1], refs[-1]
    seq = lax.axis_index("seq")
    depth = tile_refs[0].shape[0]
    steps = sems.shape[0] // len(tile_refs)
    rows = depth // steps
    copies = [
        pltpu.make_async_copy(
            weight_ref.at[pl.ds(pl.multiple_of((seq ^ mask) * depth + n * rows, rows), rows), :],
            tile_ref.at[pl.ds(n * rows, rows), :],
            sems.at[i * steps + n],
        )
        for i, (mask, tile_ref) in enumerate(zip([0] + masks, tile_refs))
        for n in range(steps)
    ]
    for copy in copies:
        copy.start()
    for copy in copies:
        copy.wait()


def load(weight, masks):
    count = 1 + len(masks)
    shape = jax.ShapeDtypeStruct((weight.shape[0] // count, weight.shape[1]), weight.dtype)
    return pl.pallas_call(
        functools.partial(load_kernel, masks),
        out_shape=[shape] * count,
        in_specs=[hbm()],
        out_specs=[vmem()] * count,
        scratch_shapes=[pltpu.SemaphoreType.DMA((4 * count,))],
        compiler_params=params(LOAD_BYTES),
        cost_estimate=cost(0, weight.size * 2),
        name="load",
    )(weight)


def project_kernel(first, last, *refs):
    x_ref, w_ref = refs[:2]
    acc_ref = None if first else refs[2]
    outs = refs[2 if first else 3 :]
    tp = lax.axis_index("tp")
    columns = w_ref.shape[1]
    width = math.gcd(columns, 512)
    keep_rows = x_ref.shape[0] // 2
    for start in range(0, columns, width):
        at = slice(start, start + width)
        part = jnp.dot(x_ref[...], w_ref[:, at], preferred_element_type=jnp.float32)
        if not first:
            part = part + acc_ref[:, at]
        if last:
            low, high = part[:keep_rows, :], part[keep_rows:, :]
            outs[0][:, at] = jnp.where(tp == 0, low, high)
            outs[1][:, at] = jnp.where(tp == 0, high, low).astype(jnp.bfloat16)
        else:
            outs[0][:, at] = part


def project(context, tile, acc, last):
    tokens, depth = context.shape
    columns = tile.shape[1]
    if last:
        shapes = [
            jax.ShapeDtypeStruct((tokens // 2, columns), jnp.float32),
            jax.ShapeDtypeStruct((tokens // 2, columns), jnp.bfloat16),
        ]
    else:
        shapes = [jax.ShapeDtypeStruct((tokens, columns), jnp.float32)]
    operands = [context, tile] + ([] if acc is None else [acc])
    return pl.pallas_call(
        functools.partial(project_kernel, acc is None, last),
        out_shape=shapes,
        in_specs=[vmem()] * len(operands),
        out_specs=[vmem()] * len(shapes),
        compiler_params=params(PROJECT_BYTES),
        cost_estimate=cost(2 * tokens * depth * columns, 2 * depth * columns),
        name="project",
    )(*operands)


def shards_by_head(
    queries, fresh_key_rows, fresh_value_rows, visible, prefix_keys, cached_value_rows, out_weight
):
    heads = queries.shape[2] // fresh_key_rows.shape[2]
    masks = list(range(1, lax.axis_size("seq")))[::ORDER]
    rows = [queries[0], fresh_key_rows[0], fresh_value_rows[0]]
    own, *pieces = pack_prefix(prefix_keys, cached_value_rows, masks)
    mine = [swap(piece, "seq", mask) for piece, mask in zip(pieces, masks)]
    query_rows = lax.all_to_all(
        pack_queries(rows, 1 + len(masks)), ("seq", "tp"), split_axis=0, concat_axis=0, tiled=True
    )
    lengths = spread_lengths(visible)
    mine = settle(mine)
    other = [swap(piece, "rep", 1) for piece in mine]

    stacked, *state = attend_first(heads, query_rows, lengths, own)
    for i, mask in enumerate(masks):
        state = attend_more(
            prefix_keys.shape[0], mask, mask == masks[-1], stacked, lengths, state, mine[i], other[i]
        )
    context = state[0]
    tiles = load(out_weight, masks)
    acc, send = None, None
    for mask, tile in zip([0] + masks, tiles):
        chunk = swap(context, "seq", mask) if mask else context
        acc, *send = project(chunk, tile, acc, mask == masks[-1])
    got = swap(send[0], "tp", 1)
    return (acc + got.astype(jnp.float32)).astype(jnp.bfloat16)[None]


def solution(mesh):
    in_specs = (
        P("rep", ("groups", "seq", "tp"), None),
        P("rep", ("groups", "seq", "tp"), None),
        P("rep", ("groups", "seq", "tp"), None),
        P("rep", "groups"),
        P(("groups", "seq"), "tp"),
        P(("groups", "seq"), "tp"),
        P("tp", "seq"),
    )
    out_specs = P("rep", ("groups", "tp"), "seq")
    sizes = mesh.shape
    seq_count = sizes["seq"]

    def shards(*args):
        local_heads = args[4].shape[1] // HEAD_WIDTH
        by_head = (
            local_heads == seq_count
            and seq_count & (seq_count - 1) == 0
            and sizes["tp"] == 2
            and sizes["rep"] == 2
            and args[0].shape[2] // args[1].shape[2] % 2 == 0
        )
        return (shards_by_head if by_head else shards_any)(*args)

    return jax.shard_map(shards, mesh=mesh, in_specs=in_specs, out_specs=out_specs, check_vma=False)
```

```python
import functools
import math

import jax
import jax.numpy as jnp
from jax import lax
from jax.experimental import pallas as pl
from jax.experimental.pallas import tpu as pltpu
from jax.sharding import PartitionSpec as P

HEAD_WIDTH = 128
HIDDEN = -1e30
SCALE = 1.0 / math.sqrt(HEAD_WIDTH)


def block_partial(query_heads, lengths, key_rows, value_rows, offset):
    kv_heads = query_heads.shape[1]
    row_count = key_rows.shape[0]
    step_rows = math.gcd(row_count, 512)
    stat_shape = query_heads.shape[:3]

    def masked_scores(turn_index):
        first_row = turn_index * step_rows
        key_block = lax.dynamic_slice_in_dim(key_rows, first_row, step_rows, 0)
        key_block = key_block.reshape(step_rows, kv_heads, HEAD_WIDTH)
        scores = (
            jnp.einsum("tkgd,pkd->tkgp", query_heads, key_block, preferred_element_type=jnp.float32)
            * SCALE
        )
        position = offset + first_row + jnp.arange(step_rows, dtype=jnp.int32)
        visible_mask = (position[None, :] < lengths[:, None])[:, None, None, :]
        return (scores, visible_mask, first_row)

    def peak_step(turn_index, peak_now):
        scores, visible_mask, _ = masked_scores(turn_index)
        return jnp.maximum(peak_now, jnp.max(jnp.where(visible_mask, scores, -jnp.inf), axis=-1))

    block_peak = lax.fori_loop(
        0, row_count // step_rows, peak_step, jnp.full(stat_shape, -jnp.inf, jnp.float32)
    )
    anchor = jnp.where(jnp.isinf(block_peak), 0.0, block_peak)

    def weight_step(turn_index, state_now):
        sum_now, acc_now = state_now
        scores, visible_mask, first_row = masked_scores(turn_index)
        value_block = lax.dynamic_slice_in_dim(value_rows, first_row, step_rows, 0)
        value_block = value_block.reshape(step_rows, kv_heads, HEAD_WIDTH)
        weights = jnp.where(visible_mask, jnp.exp(scores - anchor[..., None]), 0.0)
        sum_now = sum_now + jnp.sum(weights, axis=-1)
        acc_now = acc_now + jnp.einsum(
            "tkgp,pkd->tkgd",
            weights.astype(jnp.bfloat16),
            value_block,
            preferred_element_type=jnp.float32,
        )
        return (sum_now, acc_now)

    block_sum, block_acc = lax.fori_loop(
        0,
        row_count // step_rows,
        weight_step,
        (jnp.zeros(stat_shape, jnp.float32), jnp.zeros(query_heads.shape, jnp.float32)),
    )
    return (block_peak, block_sum, block_acc)


def shards_any(
    queries, fresh_key_rows, fresh_value_rows, visible, prefix_keys, cached_value_rows, out_weight
):
    query_rows, self_key_rows, own_values = (
        lax.all_to_all(queries[0], "tp", split_axis=1, concat_axis=0, tiled=True),
        lax.all_to_all(fresh_key_rows[0], "tp", split_axis=1, concat_axis=0, tiled=True),
        lax.all_to_all(fresh_value_rows[0], "tp", split_axis=1, concat_axis=0, tiled=True),
    )
    kv_heads = prefix_keys.shape[1] // HEAD_WIDTH
    tok_rows = query_rows.shape[0]
    block_rows = prefix_keys.shape[0]
    per_group = query_rows.shape[1] // (kv_heads * HEAD_WIDTH)
    seq_index = lax.axis_index("seq")
    query_heads = query_rows.reshape(tok_rows, kv_heads, per_group, HEAD_WIDTH)
    self_key_rows = self_key_rows.reshape(tok_rows, kv_heads, HEAD_WIDTH)
    own_vectors = own_values.reshape(tok_rows, kv_heads, 1, HEAD_WIDTH).astype(jnp.float32)
    self_score_row = (
        jnp.einsum(
            "tkgd,tkd->tkg", query_heads, self_key_rows, preferred_element_type=jnp.float32
        )
        * SCALE
    )
    seq_count = lax.axis_size("seq")
    everyone = lax.all_gather(query_rows, "seq", axis=0, tiled=True)
    blocks = everyone.reshape(seq_count, tok_rows, kv_heads, per_group, HEAD_WIDTH)
    all_lengths = visible[0].reshape(seq_count, tok_rows)
    prefix_start = seq_index * block_rows

    def partial_block(item_pair):
        return block_partial(
            item_pair[0], item_pair[1], prefix_keys, cached_value_rows, prefix_start
        )

    part_max, part_sum, part_acc = lax.map(partial_block, (blocks, all_lengths))
    part_max, part_sum, part_acc = (
        lax.all_to_all(part_max, "seq", split_axis=0, concat_axis=0, tiled=True),
        lax.all_to_all(part_sum, "seq", split_axis=0, concat_axis=0, tiled=True),
        lax.all_to_all(part_acc, "seq", split_axis=0, concat_axis=0, tiled=True),
    )
    run_max = jnp.max(part_max, axis=0)
    anchor = jnp.where(jnp.isinf(run_max), 0.0, run_max)
    part_factor = jnp.exp(part_max - anchor[None])
    run_sum = jnp.sum(part_sum * part_factor, axis=0)
    run_acc = jnp.sum(part_acc * part_factor[..., None], axis=0)
    row_peak = jnp.maximum(run_max, self_score_row)
    fade = jnp.exp(run_max - row_peak)
    own_weight = jnp.exp(self_score_row - row_peak)
    own_rounded = lax.optimization_barrier(own_weight.astype(jnp.bfloat16)).astype(jnp.float32)
    total_sum = run_sum * fade + own_weight
    total_acc = run_acc * fade[..., None] + own_rounded[..., None] * own_vectors
    context = (
        (total_acc / total_sum[..., None])
        .astype(jnp.bfloat16)
        .reshape(tok_rows, kv_heads * per_group * HEAD_WIDTH)
    )
    partial_out = jnp.dot(
        lax.all_gather(context, "seq", axis=0, tiled=True),
        out_weight,
        preferred_element_type=jnp.float32,
    )
    summed = lax.psum_scatter(partial_out, "tp", scatter_dimension=0, tiled=True)
    return summed.astype(jnp.bfloat16)[None]


EXPONENT = SCALE * math.log2(math.e)
VMEM_BYTES = 20 * 2**20
SETTLE = 10**11
UNIT_ROWS = 128
PACK_BYTES = 56 * 2**20
LATE_NEAR = False
PARTS = 1
ORDER = 1
LOAD_BYTES = 30 * 2**20
PROJECT_BYTES = 16 * 2**20


def swap(array, axis, mask):
    return lax.ppermute(array, axis, [(i, i ^ mask) for i in range(lax.axis_size(axis))])


def tile_at(index, width):
    return pl.ds(pl.multiple_of(index * width, width), width)


def side_by_side(array, times):
    return jnp.concatenate([array] * times, axis=1)


def vmem():
    return pl.BlockSpec(memory_space=pltpu.VMEM)


def hbm():
    return pl.BlockSpec(memory_space=pltpu.HBM)


def params(limit=VMEM_BYTES):
    return pltpu.CompilerParams(vmem_limit_bytes=limit)


def cost(flops, bytes_accessed, transcendentals=0):
    return pl.CostEstimate(
        flops=flops, bytes_accessed=bytes_accessed, transcendentals=transcendentals
    )


def pack_prefix_kernel(masks, k_ref, v_ref, own_ref, *piece_refs):
    seq, rep = lax.axis_index("seq"), lax.axis_index("rep")
    rows = k_ref.shape[0]
    half = rows // 2
    for j, table in enumerate((k_ref, v_ref)):
        for mask, piece in zip(masks, piece_refs):
            piece[j * half : (j + 1) * half, :] = table[
                tile_at(rep, half), tile_at(seq ^ mask, HEAD_WIDTH)
            ]
    for j, table in enumerate((k_ref, v_ref)):
        own_ref[j * rows : (j + 1) * rows, :] = table[:, tile_at(seq, HEAD_WIDTH)]


def pack_prefix(prefix_keys, cached_value_rows, masks):
    rows = prefix_keys.shape[0]
    heights = [2 * rows] + [rows] * len(masks)
    return pl.pallas_call(
        functools.partial(pack_prefix_kernel, masks),
        out_shape=[jax.ShapeDtypeStruct((n, HEAD_WIDTH), jnp.bfloat16) for n in heights],
        in_specs=[vmem()] * 2,
        out_specs=[vmem()] * len(heights),
        compiler_params=params(),
        cost_estimate=cost(0, 2 * 2**20),
        name="pack_prefix",
    )(prefix_keys, cached_value_rows)


def pack_queries_kernel(seq_count, *refs):
    row_refs, out_ref, held_refs, sems = refs[:3], refs[3], refs[4:7], refs[7]
    copies = [
        pltpu.make_async_copy(ref, held, sems.at[i])
        for i, (ref, held) in enumerate(zip(row_refs, held_refs))
    ]
    for copy in copies:
        copy.start()
    for copy in copies:
        copy.wait()
    tokens = row_refs[0].shape[0]
    count = out_ref.shape[0] // tokens
    for owner in range(count):
        head = owner % 2 * seq_count + owner // 2
        to = 0
        for ref in held_refs:
            part = ref.shape[1] // count
            out_ref[owner * tokens : (owner + 1) * tokens, to : to + part] = ref[
                :, head * part : (head + 1) * part
            ]
            to += part


def pack_queries(rows, seq_count):
    count = 2 * seq_count
    shape = (rows[0].shape[0] * count, sum(a.shape[1] for a in rows) // count)
    return pl.pallas_call(
        functools.partial(pack_queries_kernel, seq_count),
        out_shape=jax.ShapeDtypeStruct(shape, jnp.bfloat16),
        in_specs=[hbm()] * 3,
        out_specs=vmem(),
        scratch_shapes=[pltpu.VMEM(a.shape, a.dtype) for a in rows]
        + [pltpu.SemaphoreType.DMA((3,))],
        compiler_params=params(PACK_BYTES),
        cost_estimate=cost(0, 2**19),
        name="pack_queries",
    )(*rows)


def settle_kernel(*refs):
    del refs


def settle(arrays):
    count = len(arrays)
    return pl.pallas_call(
        settle_kernel,
        out_shape=[jax.ShapeDtypeStruct(a.shape, a.dtype) for a in arrays],
        in_specs=[vmem()] * count,
        out_specs=[vmem()] * count,
        input_output_aliases={i: i for i in range(count)},
        compiler_params=params(2**20),
        cost_estimate=cost(SETTLE, 2**20),
        name="settle",
    )(*arrays)


def lengths_kernel(visible_ref, out_ref):
    tokens = out_ref.shape[0]
    diagonal = lax.broadcasted_iota(jnp.int32, (tokens, tokens), 0) == lax.broadcasted_iota(
        jnp.int32, (tokens, tokens), 1
    )
    lengths = jnp.sum(jnp.where(diagonal, visible_ref[...], 0), axis=-1, keepdims=True)
    out_ref[...] = jnp.broadcast_to(lengths, out_ref.shape)


def spread_lengths(visible):
    return pl.pallas_call(
        lengths_kernel,
        out_shape=jax.ShapeDtypeStruct((visible.shape[1], HEAD_WIDTH), jnp.int32),
        in_specs=[vmem()],
        out_specs=vmem(),
        compiler_params=params(),
        cost_estimate=cost(0, 2**15),
        name="spread_lengths",
    )(visible)


def attend_kernel(
    heads, masks, block_rows, rows_ref, lengths_ref, own_ref, *refs
):
    piece_refs, out_ref = refs[:-1], refs[-1]
    seq, rep = lax.axis_index("seq"), lax.axis_index("rep")
    tokens = out_ref.shape[0]
    half = block_rows // 2
    lane = lax.broadcasted_iota(jnp.int32, (1, half), 1)
    blocks = []
    for core in range(2):
        rows = slice(core * half, (core + 1) * half)
        values = slice(block_rows + core * half, block_rows + (core + 1) * half)
        blocks.append((own_ref, rows, values, seq * block_rows + core * half + lane))
    for i, ref in enumerate(piece_refs):
        mask, core = masks[i // 2], (rep if i % 2 == 0 else 1 - rep)
        first = (seq ^ mask) * block_rows + core * half
        blocks.append((ref, slice(0, half), slice(half, 2 * half), first + lane))
    width = heads * HEAD_WIDTH
    fresh_key = rows_ref[:, width : width + HEAD_WIDTH].astype(jnp.float32)
    fresh_value = rows_ref[:, width + HEAD_WIDTH :].astype(jnp.float32)
    group = max(1, UNIT_ROWS // tokens)
    lengths = jnp.concatenate([lengths_ref[...]] * group, axis=0)
    fresh_key = jnp.concatenate([fresh_key] * group, axis=0)
    start = jnp.concatenate([fresh_value, jnp.ones_like(fresh_value)], axis=1)
    start = jnp.concatenate([start] * group, axis=0)
    for first in range(0, heads, group):
        query = jnp.concatenate(
            [
                rows_ref[:, h * HEAD_WIDTH : (h + 1) * HEAD_WIDTH]
                for h in range(first, first + group)
            ],
            axis=0,
        )
        own = jnp.sum(query.astype(jnp.float32) * fresh_key, axis=-1, keepdims=True)
        own = jnp.broadcast_to(own, (group * tokens, HEAD_WIDTH))
        top, scores = own, []
        for ref, rows, _, position in blocks:
            score = lax.dot_general(
                query, ref[rows, :], (((1,), (1,)), ((), ())), preferred_element_type=jnp.float32
            )
            hidden = position >= side_by_side(lengths, half // HEAD_WIDTH)
            score = jnp.where(hidden, HIDDEN, score)
            for i in range(0, half, HEAD_WIDTH):
                top = jnp.maximum(top, score[:, i : i + HEAD_WIDTH])
            scores.append(score)
        peak = jnp.broadcast_to(jnp.max(top, axis=-1, keepdims=True), own.shape)
        acc = start * side_by_side(jnp.exp2((own - peak) * EXPONENT), 2)
        for score, (ref, _, rows, _) in zip(scores, blocks):
            weights = jnp.exp2((score - side_by_side(peak, half // HEAD_WIDTH)) * EXPONENT)
            values = ref[rows, :]
            acc = acc + jnp.dot(
                weights.astype(jnp.bfloat16),
                jnp.concatenate([values, jnp.ones_like(values)], axis=1),
                preferred_element_type=jnp.float32,
            )
        context = (acc[:, :HEAD_WIDTH] / acc[:, HEAD_WIDTH:]).astype(jnp.bfloat16)
        for i in range(group):
            column = (first + i) * HEAD_WIDTH
            out_ref[:, column : column + HEAD_WIDTH] = context[i * tokens : (i + 1) * tokens, :]


def attend(heads, masks, query_rows, lengths, own, pieces):
    tokens = query_rows.shape[0]
    block_rows = own.shape[0] // 2
    work = tokens * heads * block_rows * (1 + len(masks))
    return pl.pallas_call(
        functools.partial(attend_kernel, heads, masks, block_rows),
        out_shape=jax.ShapeDtypeStruct((tokens, heads * HEAD_WIDTH), jnp.bfloat16),
        in_specs=[vmem()] * (3 + len(pieces)),
        out_specs=vmem(),
        compiler_params=params(),
        cost_estimate=cost(6 * work * HEAD_WIDTH, 2**20, work),
        name="attend",
    )(query_rows, lengths, own, *pieces)


def load_kernel(masks, weight_ref, *refs):
    tile_refs, sems = refs[:-1], refs[-1]
    seq = lax.axis_index("seq")
    depth = tile_refs[0].shape[0]
    steps = sems.shape[0] // len(tile_refs)
    rows = depth // steps
    copies = [
        pltpu.make_async_copy(
            weight_ref.at[pl.ds(pl.multiple_of((seq ^ mask) * depth + n * rows, rows), rows), :],
            tile_ref.at[pl.ds(n * rows, rows), :],
            sems.at[i * steps + n],
        )
        for i, (mask, tile_ref) in enumerate(zip(masks, tile_refs))
        for n in range(steps)
    ]
    for copy in copies:
        copy.start()
    for copy in copies:
        copy.wait()


def load(weight, masks, count):
    depth, columns = weight.shape[0] // count, weight.shape[1]
    return pl.pallas_call(
        functools.partial(load_kernel, masks),
        out_shape=[jax.ShapeDtypeStruct((depth, columns), weight.dtype)] * len(masks),
        in_specs=[hbm()],
        out_specs=[vmem()] * len(masks),
        scratch_shapes=[pltpu.SemaphoreType.DMA((4 * len(masks),))],
        compiler_params=params(LOAD_BYTES),
        cost_estimate=cost(0, len(masks) * depth * columns * 2),
        name="load",
    )(weight)


def project_kernel(x_ref, w_ref, *refs):
    acc_refs, out_ref = refs[:-1], refs[-1]
    columns = w_ref.shape[1]
    width = math.gcd(columns, 512)
    for start in range(0, columns, width):
        at = slice(start, start + width)
        part = jnp.dot(x_ref[...], w_ref[:, at], preferred_element_type=jnp.float32)
        for acc_ref in acc_refs:
            part = part + acc_ref[:, at]
        out_ref[:, at] = part


def project(context, tile, acc):
    tokens, columns = context.shape[0], tile.shape[1]
    return pl.pallas_call(
        project_kernel,
        out_shape=jax.ShapeDtypeStruct((tokens, columns), jnp.float32),
        in_specs=[vmem()] * (2 + len(acc)),
        out_specs=vmem(),
        compiler_params=params(PROJECT_BYTES),
        cost_estimate=cost(2 * context.size * columns, 2 * tile.size),
        name="project",
    )(context, tile, *acc)


def last_kernel(first, x_ref, w_ref, acc_ref, keep_ref, send_ref):
    tp = lax.axis_index("tp")
    half = x_ref.shape[0] // 2
    columns = send_ref.shape[1]
    width = math.gcd(columns, 512)
    for start in range(0, columns, width):
        at, to = slice(first + start, first + start + width), slice(start, start + width)
        part = jnp.dot(x_ref[...], w_ref[:, at], preferred_element_type=jnp.float32)
        part = part + acc_ref[:, at]
        low, high = part[:half, :], part[half:, :]
        keep_ref[:, to] = jnp.where(tp == 0, low, high)
        send_ref[:, to] = jnp.where(tp == 0, high, low).astype(jnp.bfloat16)


def project_last(context, tile, acc, first, columns):
    tokens = context.shape[0] // 2
    return pl.pallas_call(
        functools.partial(last_kernel, first),
        out_shape=[
            jax.ShapeDtypeStruct((tokens, columns), jnp.float32),
            jax.ShapeDtypeStruct((tokens, columns), jnp.bfloat16),
        ],
        in_specs=[vmem()] * 3,
        out_specs=[vmem()] * 2,
        compiler_params=params(PROJECT_BYTES),
        cost_estimate=cost(2 * context.size * columns, 2 * tile.shape[0] * columns),
        name="project_last",
    )(context, tile, acc)


def add_kernel(*refs):
    out_ref = refs[-1]
    count = (len(refs) - 1) // 2
    start = 0
    for keep_ref, got_ref in zip(refs[:count], refs[count:-1]):
        width = keep_ref.shape[1]
        total = keep_ref[...] + got_ref[...].astype(jnp.float32)
        out_ref[0, :, start : start + width] = total.astype(out_ref.dtype)
        start += width


def add(keeps, gots):
    shape = (1, keeps[0].shape[0], sum(a.shape[1] for a in keeps))
    return pl.pallas_call(
        add_kernel,
        out_shape=jax.ShapeDtypeStruct(shape, jnp.bfloat16),
        in_specs=[vmem()] * (2 * len(keeps)),
        out_specs=vmem(),
        compiler_params=params(PROJECT_BYTES),
        cost_estimate=cost(0, 2**19),
        name="add",
    )(*keeps, *gots)


def shards_by_head(
    queries, fresh_key_rows, fresh_value_rows, visible, prefix_keys, cached_value_rows, out_weight
):
    heads = queries.shape[2] // fresh_key_rows.shape[2]
    masks = list(range(1, lax.axis_size("seq")))[::ORDER]
    rows = [queries[0], fresh_key_rows[0], fresh_value_rows[0]]
    own, *pieces = pack_prefix(prefix_keys, cached_value_rows, masks)
    near = masks.index(1)
    mine = [swap(p, "seq", m) if m != 1 else p for p, m in zip(pieces, masks)]
    if LATE_NEAR:
        mine = list(lax.optimization_barrier(mine))
    mine[near] = swap(mine[near], "seq", 1)
    query_rows = lax.all_to_all(
        pack_queries(rows, 1 + len(masks)), ("seq", "tp"), split_axis=0, concat_axis=0, tiled=True
    )
    lengths = spread_lengths(visible)
    far = settle([piece for piece, mask in zip(mine, masks) if mask != 1])
    mine = [*far[:near], mine[near], *far[near:]]
    other = [swap(piece, "rep", 1) for piece in mine]

    pieces = [piece for pair in zip(mine, other) for piece in pair]
    context = attend(heads, masks, query_rows, lengths, own, pieces)

    chunks = [swap(context, "seq", mask) for mask in masks]
    tiles = load(out_weight, [0] + masks, 1 + len(masks))
    acc = []
    for chunk, tile in zip([context] + chunks[:-1], tiles):
        acc = [project(chunk, tile, acc)]
    acc = acc[0]
    columns = acc.shape[1] // PARTS
    parts = [
        project_last(chunks[-1], tiles[-1], acc, i * columns, columns) for i in range(PARTS)
    ]
    return add([keep for keep, _ in parts], [swap(send, "tp", 1) for _, send in parts])


def solution(mesh):
    in_specs = (
        P("rep", ("groups", "seq", "tp"), None),
        P("rep", ("groups", "seq", "tp"), None),
        P("rep", ("groups", "seq", "tp"), None),
        P("rep", "groups"),
        P(("groups", "seq"), "tp"),
        P(("groups", "seq"), "tp"),
        P("tp", "seq"),
    )
    out_specs = P("rep", ("groups", "tp"), "seq")
    sizes = mesh.shape
    seq_count = sizes["seq"]

    def shards(*args):
        local_heads = args[4].shape[1] // HEAD_WIDTH
        by_head = (
            local_heads == seq_count
            and seq_count & (seq_count - 1) == 0
            and sizes["tp"] == 2
            and sizes["rep"] == 2
            and args[0].shape[2] // args[1].shape[2] % 2 == 0
        )
        return (shards_by_head if by_head else shards_any)(*args)

    return jax.shard_map(shards, mesh=mesh, in_specs=in_specs, out_specs=out_specs, check_vma=False)
```

```python
import functools
import math

import jax
import jax.numpy as jnp
from jax import lax
from jax.experimental import pallas as pl
from jax.experimental.pallas import tpu as pltpu
from jax.sharding import PartitionSpec as P

HEAD_WIDTH = 128
HIDDEN = -1e30
SCALE = 1.0 / math.sqrt(HEAD_WIDTH)


def block_partial(query_heads, lengths, key_rows, value_rows, offset):
    kv_heads = query_heads.shape[1]
    row_count = key_rows.shape[0]
    step_rows = math.gcd(row_count, 512)
    stat_shape = query_heads.shape[:3]

    def masked_scores(turn_index):
        first_row = turn_index * step_rows
        key_block = lax.dynamic_slice_in_dim(key_rows, first_row, step_rows, 0)
        key_block = key_block.reshape(step_rows, kv_heads, HEAD_WIDTH)
        scores = (
            jnp.einsum("tkgd,pkd->tkgp", query_heads, key_block, preferred_element_type=jnp.float32)
            * SCALE
        )
        position = offset + first_row + jnp.arange(step_rows, dtype=jnp.int32)
        visible_mask = (position[None, :] < lengths[:, None])[:, None, None, :]
        return (scores, visible_mask, first_row)

    def peak_step(turn_index, peak_now):
        scores, visible_mask, _ = masked_scores(turn_index)
        return jnp.maximum(peak_now, jnp.max(jnp.where(visible_mask, scores, -jnp.inf), axis=-1))

    block_peak = lax.fori_loop(
        0, row_count // step_rows, peak_step, jnp.full(stat_shape, -jnp.inf, jnp.float32)
    )
    anchor = jnp.where(jnp.isinf(block_peak), 0.0, block_peak)

    def weight_step(turn_index, state_now):
        sum_now, acc_now = state_now
        scores, visible_mask, first_row = masked_scores(turn_index)
        value_block = lax.dynamic_slice_in_dim(value_rows, first_row, step_rows, 0)
        value_block = value_block.reshape(step_rows, kv_heads, HEAD_WIDTH)
        weights = jnp.where(visible_mask, jnp.exp(scores - anchor[..., None]), 0.0)
        sum_now = sum_now + jnp.sum(weights, axis=-1)
        acc_now = acc_now + jnp.einsum(
            "tkgp,pkd->tkgd",
            weights.astype(jnp.bfloat16),
            value_block,
            preferred_element_type=jnp.float32,
        )
        return (sum_now, acc_now)

    block_sum, block_acc = lax.fori_loop(
        0,
        row_count // step_rows,
        weight_step,
        (jnp.zeros(stat_shape, jnp.float32), jnp.zeros(query_heads.shape, jnp.float32)),
    )
    return (block_peak, block_sum, block_acc)


def shards_any(
    queries, fresh_key_rows, fresh_value_rows, visible, prefix_keys, cached_value_rows, out_weight
):
    query_rows, self_key_rows, own_values = (
        lax.all_to_all(queries[0], "tp", split_axis=1, concat_axis=0, tiled=True),
        lax.all_to_all(fresh_key_rows[0], "tp", split_axis=1, concat_axis=0, tiled=True),
        lax.all_to_all(fresh_value_rows[0], "tp", split_axis=1, concat_axis=0, tiled=True),
    )
    kv_heads = prefix_keys.shape[1] // HEAD_WIDTH
    tok_rows = query_rows.shape[0]
    block_rows = prefix_keys.shape[0]
    per_group = query_rows.shape[1] // (kv_heads * HEAD_WIDTH)
    seq_index = lax.axis_index("seq")
    query_heads = query_rows.reshape(tok_rows, kv_heads, per_group, HEAD_WIDTH)
    self_key_rows = self_key_rows.reshape(tok_rows, kv_heads, HEAD_WIDTH)
    own_vectors = own_values.reshape(tok_rows, kv_heads, 1, HEAD_WIDTH).astype(jnp.float32)
    self_score_row = (
        jnp.einsum(
            "tkgd,tkd->tkg", query_heads, self_key_rows, preferred_element_type=jnp.float32
        )
        * SCALE
    )
    seq_count = lax.axis_size("seq")
    everyone = lax.all_gather(query_rows, "seq", axis=0, tiled=True)
    blocks = everyone.reshape(seq_count, tok_rows, kv_heads, per_group, HEAD_WIDTH)
    all_lengths = visible[0].reshape(seq_count, tok_rows)
    prefix_start = seq_index * block_rows

    def partial_block(item_pair):
        return block_partial(
            item_pair[0], item_pair[1], prefix_keys, cached_value_rows, prefix_start
        )

    part_max, part_sum, part_acc = lax.map(partial_block, (blocks, all_lengths))
    part_max, part_sum, part_acc = (
        lax.all_to_all(part_max, "seq", split_axis=0, concat_axis=0, tiled=True),
        lax.all_to_all(part_sum, "seq", split_axis=0, concat_axis=0, tiled=True),
        lax.all_to_all(part_acc, "seq", split_axis=0, concat_axis=0, tiled=True),
    )
    run_max = jnp.max(part_max, axis=0)
    anchor = jnp.where(jnp.isinf(run_max), 0.0, run_max)
    part_factor = jnp.exp(part_max - anchor[None])
    run_sum = jnp.sum(part_sum * part_factor, axis=0)
    run_acc = jnp.sum(part_acc * part_factor[..., None], axis=0)
    row_peak = jnp.maximum(run_max, self_score_row)
    fade = jnp.exp(run_max - row_peak)
    own_weight = jnp.exp(self_score_row - row_peak)
    own_rounded = lax.optimization_barrier(own_weight.astype(jnp.bfloat16)).astype(jnp.float32)
    total_sum = run_sum * fade + own_weight
    total_acc = run_acc * fade[..., None] + own_rounded[..., None] * own_vectors
    context = (
        (total_acc / total_sum[..., None])
        .astype(jnp.bfloat16)
        .reshape(tok_rows, kv_heads * per_group * HEAD_WIDTH)
    )
    partial_out = jnp.dot(
        lax.all_gather(context, "seq", axis=0, tiled=True),
        out_weight,
        preferred_element_type=jnp.float32,
    )
    summed = lax.psum_scatter(partial_out, "tp", scatter_dimension=0, tiled=True)
    return summed.astype(jnp.bfloat16)[None]


EXPONENT = SCALE * math.log2(math.e)
VMEM_BYTES = 20 * 2**20
UNIT_ROWS = 128
FETCHES = 4
SETTLE_FIRST = 10**11
SETTLE_LAST = 10**10
PACK_BYTES = 56 * 2**20
ATTEND_BYTES = 40 * 2**20
LOAD_BYTES = 30 * 2**20
PROJECT_BYTES = 16 * 2**20


def swap(array, axis, mask):
    return lax.ppermute(array, axis, [(i, i ^ mask) for i in range(lax.axis_size(axis))])


def tile_at(index, width):
    return pl.ds(pl.multiple_of(index * width, width), width)


def side_by_side(array, times):
    return jnp.concatenate([array] * times, axis=1)


def vmem():
    return pl.BlockSpec(memory_space=pltpu.VMEM)


def hbm():
    return pl.BlockSpec(memory_space=pltpu.HBM)


def params(limit=VMEM_BYTES):
    return pltpu.CompilerParams(vmem_limit_bytes=limit)


def cost(flops, bytes_accessed, transcendentals=0):
    return pl.CostEstimate(
        flops=flops, bytes_accessed=bytes_accessed, transcendentals=transcendentals
    )


def pack_queries_kernel(seq_count, *refs):
    row_refs, out_ref, held_refs, sems = refs[:3], refs[3], refs[4:7], refs[7]
    copies = [
        pltpu.make_async_copy(ref, held, sems.at[i])
        for i, (ref, held) in enumerate(zip(row_refs, held_refs))
    ]
    for copy in copies:
        copy.start()
    for copy in copies:
        copy.wait()
    tokens = row_refs[0].shape[0]
    count = out_ref.shape[0] // tokens
    for owner in range(count):
        head = owner % 2 * seq_count + owner // 2
        to = 0
        for ref in held_refs:
            part = ref.shape[1] // count
            out_ref[owner * tokens : (owner + 1) * tokens, to : to + part] = ref[
                :, head * part : (head + 1) * part
            ]
            to += part


def pack_queries(rows, seq_count):
    count = 2 * seq_count
    shape = (rows[0].shape[0] * count, sum(a.shape[1] for a in rows) // count)
    return pl.pallas_call(
        functools.partial(pack_queries_kernel, seq_count),
        out_shape=jax.ShapeDtypeStruct(shape, jnp.bfloat16),
        in_specs=[hbm()] * 3,
        out_specs=vmem(),
        scratch_shapes=[pltpu.VMEM(a.shape, a.dtype) for a in rows]
        + [pltpu.SemaphoreType.DMA((3,))],
        compiler_params=params(PACK_BYTES),
        cost_estimate=cost(0, 2**19),
        name="pack_queries",
    )(*rows)


def settle_kernel(*refs):
    del refs


def settle(arrays, declared):
    count = len(arrays)
    return pl.pallas_call(
        settle_kernel,
        out_shape=[jax.ShapeDtypeStruct(a.shape, a.dtype) for a in arrays],
        in_specs=[vmem()] * count,
        out_specs=[vmem()] * count,
        input_output_aliases={i: i for i in range(count)},
        compiler_params=params(2**20),
        cost_estimate=cost(declared, 2**20),
        name="settle",
    )(*arrays)


def lengths_kernel(visible_ref, out_ref):
    tokens = out_ref.shape[0]
    diagonal = lax.broadcasted_iota(jnp.int32, (tokens, tokens), 0) == lax.broadcasted_iota(
        jnp.int32, (tokens, tokens), 1
    )
    lengths = jnp.sum(jnp.where(diagonal, visible_ref[...], 0), axis=-1, keepdims=True)
    out_ref[...] = jnp.broadcast_to(lengths, out_ref.shape)


def spread_lengths(visible):
    return pl.pallas_call(
        lengths_kernel,
        out_shape=jax.ShapeDtypeStruct((visible.shape[1], HEAD_WIDTH), jnp.int32),
        in_specs=[vmem()],
        out_specs=vmem(),
        compiler_params=params(),
        cost_estimate=cost(0, 2**15),
        name="spread_lengths",
    )(visible)


def half_of(rows, side):
    half = rows.shape[0] // 2
    return jnp.where(side == 0, rows[:half, :], rows[half:, :])


def tile_copies(masks, weight_ref, tile_refs, sems):
    depth = tile_refs[0].shape[0]
    rows = depth // FETCHES
    seq = lax.axis_index("seq")
    return [
        pltpu.make_async_copy(
            weight_ref.at[pl.ds(pl.multiple_of((seq ^ mask) * depth + n * rows, rows), rows), :],
            tile_ref.at[pl.ds(n * rows, rows), :],
            sems.at[i * FETCHES + n],
        )
        for i, (mask, tile_ref) in enumerate(zip(masks, tile_refs))
        for n in range(FETCHES)
    ]


def multiply(x_ref, w_ref, finish):
    columns = w_ref.shape[1]
    width = math.gcd(columns, 512)
    for start in range(0, columns, width):
        at = slice(start, start + width)
        finish(at, jnp.dot(x_ref[...], w_ref[:, at], preferred_element_type=jnp.float32))


def attend_kernel(heads, masks, block_rows, rows_ref, lengths_ref, own_ref, *refs):
    pieces = 2 * len(masks)
    piece_refs, weight_ref = refs[:pieces], refs[pieces]
    out_ref, theirs_ref, tile_ref, sems = refs[pieces + 1 :]
    seq, tp, rep = lax.axis_index("seq"), lax.axis_index("tp"), lax.axis_index("rep")
    copies = tile_copies([0], weight_ref, [tile_ref], sems)
    for copy in copies:
        copy.start()
    @pl.when(tp >= 0)
    def compute():
        tokens = out_ref.shape[0]
        half = block_rows // 2
        lane = lax.broadcasted_iota(jnp.int32, (1, half), 1)
        blocks = []
        for core in range(2):
            rows = slice(core * half, (core + 1) * half)
            values = slice(block_rows + core * half, block_rows + (core + 1) * half)
            blocks.append((own_ref, rows, values, seq * block_rows + core * half + lane))
        for i, ref in enumerate(piece_refs):
            mask, core = masks[i // 2], (rep if i % 2 == 0 else 1 - rep)
            first = (seq ^ mask) * block_rows + core * half
            blocks.append((ref, slice(0, half), slice(half, 2 * half), first + lane))
        width = heads * HEAD_WIDTH
        fresh_key = rows_ref[:, width : width + HEAD_WIDTH].astype(jnp.float32)
        fresh_value = rows_ref[:, width + HEAD_WIDTH :].astype(jnp.float32)
        group = max(1, UNIT_ROWS // tokens)
        lengths = jnp.concatenate([lengths_ref[...]] * group, axis=0)
        fresh_key = jnp.concatenate([fresh_key] * group, axis=0)
        start = jnp.concatenate([fresh_value, jnp.ones_like(fresh_value)], axis=1)
        start = jnp.concatenate([start] * group, axis=0)
        for first in range(0, heads, group):
            query = jnp.concatenate(
                [
                    rows_ref[:, h * HEAD_WIDTH : (h + 1) * HEAD_WIDTH]
                    for h in range(first, first + group)
                ],
                axis=0,
            )
            own = jnp.sum(query.astype(jnp.float32) * fresh_key, axis=-1, keepdims=True)
            own = jnp.broadcast_to(own, (group * tokens, HEAD_WIDTH))
            top, scores = own, []
            for ref, rows, _, position in blocks:
                score = lax.dot_general(
                    query, ref[rows, :], (((1,), (1,)), ((), ())), preferred_element_type=jnp.float32
                )
                hidden = position >= side_by_side(lengths, half // HEAD_WIDTH)
                score = jnp.where(hidden, HIDDEN, score)
                for i in range(0, half, HEAD_WIDTH):
                    top = jnp.maximum(top, score[:, i : i + HEAD_WIDTH])
                scores.append(score)
            peak = jnp.broadcast_to(jnp.max(top, axis=-1, keepdims=True), own.shape)
            acc = start * side_by_side(jnp.exp2((own - peak) * EXPONENT), 2)
            for score, (ref, _, rows, _) in zip(scores, blocks):
                weights = jnp.exp2((score - side_by_side(peak, half // HEAD_WIDTH)) * EXPONENT)
                values = ref[rows, :]
                acc = acc + jnp.dot(
                    weights.astype(jnp.bfloat16),
                    jnp.concatenate([values, jnp.ones_like(values)], axis=1),
                    preferred_element_type=jnp.float32,
                )
            context = (acc[:, :HEAD_WIDTH] / acc[:, HEAD_WIDTH:]).astype(jnp.bfloat16)
            for i in range(group):
                column = (first + i) * HEAD_WIDTH
                head = context[i * tokens : (i + 1) * tokens, :]
                out_ref[:, column : column + HEAD_WIDTH] = head
                theirs_ref[:, column : column + HEAD_WIDTH] = half_of(head, 1 - tp)

    for copy in copies:
        copy.wait()


def attend(heads, masks, query_rows, lengths, own, pieces, weight):
    tokens = query_rows.shape[0]
    block_rows = own.shape[0] // 2
    work = tokens * heads * block_rows * (1 + len(masks))
    depth = heads * HEAD_WIDTH
    return pl.pallas_call(
        functools.partial(attend_kernel, heads, masks, block_rows),
        out_shape=[
            jax.ShapeDtypeStruct((tokens, depth), jnp.bfloat16),
            jax.ShapeDtypeStruct((tokens // 2, depth), jnp.bfloat16),
            jax.ShapeDtypeStruct((depth, weight.shape[1]), weight.dtype),
        ],
        in_specs=[vmem()] * (3 + len(pieces)) + [hbm()],
        out_specs=[vmem()] * 3,
        scratch_shapes=[pltpu.SemaphoreType.DMA((FETCHES,))],
        compiler_params=params(ATTEND_BYTES),
        cost_estimate=cost(6 * work * HEAD_WIDTH, 2**20, work),
        name="attend",
    )(query_rows, lengths, own, *pieces, weight)


def load_kernel(masks, weight_ref, x_ref, first_ref, acc_ref, ours_ref, *refs):
    tile_refs, sems = refs[:-1], refs[-1]
    tp = lax.axis_index("tp")
    copies = tile_copies(masks, weight_ref, tile_refs, sems)
    for copy in copies:
        copy.start()
    ours_ref[...] = half_of(x_ref[...], tp)

    def finish(at, part):
        acc_ref[:, at] = part

    @pl.when(tp >= 0)
    def compute():
        multiply(x_ref, first_ref, finish)

    for copy in copies:
        copy.wait()


def load(weight, context, tile, masks):
    tokens, (depth, columns) = context.shape[0], tile.shape
    return pl.pallas_call(
        functools.partial(load_kernel, masks),
        out_shape=[
            jax.ShapeDtypeStruct((tokens, columns), jnp.float32),
            jax.ShapeDtypeStruct((tokens // 2, depth), jnp.bfloat16),
        ]
        + [jax.ShapeDtypeStruct(tile.shape, tile.dtype)] * len(masks),
        in_specs=[hbm(), vmem(), vmem()],
        out_specs=[vmem()] * (2 + len(masks)),
        scratch_shapes=[pltpu.SemaphoreType.DMA((FETCHES * len(masks),))],
        compiler_params=params(LOAD_BYTES),
        cost_estimate=cost(2 * tokens * depth * columns, len(masks) * depth * columns * 2),
        name="load",
    )(weight, context, tile)


def project_kernel(side, x_ref, w_ref, acc_ref, out_ref):
    tp = lax.axis_index("tp")

    def finish(at, part):
        acc = acc_ref[:, at]
        if side is not None:
            acc = half_of(acc, tp if side == 0 else 1 - tp)
        out_ref[:, at] = (part + acc).astype(out_ref.dtype)

    multiply(x_ref, w_ref, finish)


def project(context, tile, acc, side=None, dtype=jnp.float32):
    tokens, columns = context.shape[0], tile.shape[1]
    return pl.pallas_call(
        functools.partial(project_kernel, side),
        out_shape=jax.ShapeDtypeStruct((tokens, columns), dtype),
        in_specs=[vmem()] * 3,
        out_specs=vmem(),
        compiler_params=params(PROJECT_BYTES),
        cost_estimate=cost(2 * context.size * columns, 2 * tile.size),
        name="project",
    )(context, tile, acc)


def add_kernel(*refs):
    out_ref = refs[-1]
    count = (len(refs) - 1) // 2
    start = 0
    for keep_ref, got_ref in zip(refs[:count], refs[count:-1]):
        width = keep_ref.shape[1]
        total = keep_ref[...] + got_ref[...].astype(jnp.float32)
        out_ref[0, :, start : start + width] = total.astype(out_ref.dtype)
        start += width


def add(keeps, gots):
    shape = (1, keeps[0].shape[0], sum(a.shape[1] for a in keeps))
    return pl.pallas_call(
        add_kernel,
        out_shape=jax.ShapeDtypeStruct(shape, jnp.bfloat16),
        in_specs=[vmem()] * (2 * len(keeps)),
        out_specs=vmem(),
        compiler_params=params(PROJECT_BYTES),
        cost_estimate=cost(0, 2**19),
        name="add",
    )(*keeps, *gots)


def shards_by_head(
    queries, fresh_key_rows, fresh_value_rows, visible, prefix_keys, cached_value_rows, out_weight
):
    heads = queries.shape[2] // fresh_key_rows.shape[2]
    masks = list(range(1, lax.axis_size("seq")))
    rows = [queries[0], fresh_key_rows[0], fresh_value_rows[0]]
    seq, rep = lax.axis_index("seq"), lax.axis_index("rep")
    half_rows = prefix_keys.shape[0] // 2

    def cut(first, count, head):
        return jnp.concatenate(
            [
                lax.dynamic_slice(table, (first, head * HEAD_WIDTH), (count, HEAD_WIDTH))
                for table in (prefix_keys, cached_value_rows)
            ]
        )

    pieces = [cut(rep * half_rows, half_rows, seq ^ mask) for mask in masks]
    own = cut(0, 2 * half_rows, seq)
    near = masks.index(1)
    mine = [swap(piece, "seq", mask) for piece, mask in zip(pieces, masks)]
    query_rows = lax.all_to_all(
        pack_queries(rows, 1 + len(masks)), ("seq", "tp"), split_axis=0, concat_axis=0, tiled=True
    )
    lengths = spread_lengths(visible)
    far = settle([piece for piece, mask in zip(mine, masks) if mask != 1], SETTLE_FIRST)
    mine = [*far[:near], mine[near], *far[near:]]
    other = [swap(piece, "rep", 1) for piece in mine]

    pieces = [piece for pair in zip(mine, other) for piece in pair]
    context, theirs, tile = attend(heads, masks, query_rows, lengths, own, pieces, out_weight)

    order = masks[-1:] + masks[:-1]
    far = order[-1]
    chunks = [swap(context, "seq", mask) for mask in order[:-1]]
    first = swap(theirs, "seq", far)
    acc, ours, *tiles = load(out_weight, context, tile, order)
    (second,) = settle([swap(ours, "seq", far)], SETTLE_LAST)
    for chunk, tile in zip(chunks, tiles):
        acc = project(chunk, tile, acc)
    got = swap(project(first, tiles[-1], acc, 1, jnp.bfloat16), "tp", 1)
    return add([project(second, tiles[-1], acc, 0)], [got])


def solution(mesh):
    in_specs = (
        P("rep", ("groups", "seq", "tp"), None),
        P("rep", ("groups", "seq", "tp"), None),
        P("rep", ("groups", "seq", "tp"), None),
        P("rep", "groups"),
        P(("groups", "seq"), "tp"),
        P(("groups", "seq"), "tp"),
        P("tp", "seq"),
    )
    out_specs = P("rep", ("groups", "tp"), "seq")
    sizes = mesh.shape
    seq_count = sizes["seq"]

    def shards(*args):
        local_heads = args[4].shape[1] // HEAD_WIDTH
        by_head = (
            local_heads == seq_count
            and seq_count in (4, 8)
            and sizes["tp"] == 2
            and sizes["rep"] == 2
            and args[0].shape[2] // args[1].shape[2] % 2 == 0
        )
        return (shards_by_head if by_head else shards_any)(*args)

    return jax.shard_map(shards, mesh=mesh, in_specs=in_specs, out_specs=out_specs, check_vma=False)
```

```python
import functools
import math

import jax
import jax.numpy as jnp
from jax import lax
from jax.experimental import pallas as pl
from jax.experimental.pallas import tpu as pltpu
from jax.sharding import PartitionSpec as P

HEAD_WIDTH = 128
HIDDEN = -1e30
SCALE = 1.0 / math.sqrt(HEAD_WIDTH)


def block_partial(query_heads, lengths, key_rows, value_rows, offset):
    kv_heads = query_heads.shape[1]
    row_count = key_rows.shape[0]
    step_rows = math.gcd(row_count, 512)
    stat_shape = query_heads.shape[:3]

    def masked_scores(turn_index):
        first_row = turn_index * step_rows
        key_block = lax.dynamic_slice_in_dim(key_rows, first_row, step_rows, 0)
        key_block = key_block.reshape(step_rows, kv_heads, HEAD_WIDTH)
        scores = (
            jnp.einsum("tkgd,pkd->tkgp", query_heads, key_block, preferred_element_type=jnp.float32)
            * SCALE
        )
        position = offset + first_row + jnp.arange(step_rows, dtype=jnp.int32)
        visible_mask = (position[None, :] < lengths[:, None])[:, None, None, :]
        return (scores, visible_mask, first_row)

    def peak_step(turn_index, peak_now):
        scores, visible_mask, _ = masked_scores(turn_index)
        return jnp.maximum(peak_now, jnp.max(jnp.where(visible_mask, scores, -jnp.inf), axis=-1))

    block_peak = lax.fori_loop(
        0, row_count // step_rows, peak_step, jnp.full(stat_shape, -jnp.inf, jnp.float32)
    )
    anchor = jnp.where(jnp.isinf(block_peak), 0.0, block_peak)

    def weight_step(turn_index, state_now):
        sum_now, acc_now = state_now
        scores, visible_mask, first_row = masked_scores(turn_index)
        value_block = lax.dynamic_slice_in_dim(value_rows, first_row, step_rows, 0)
        value_block = value_block.reshape(step_rows, kv_heads, HEAD_WIDTH)
        weights = jnp.where(visible_mask, jnp.exp(scores - anchor[..., None]), 0.0)
        sum_now = sum_now + jnp.sum(weights, axis=-1)
        acc_now = acc_now + jnp.einsum(
            "tkgp,pkd->tkgd",
            weights.astype(jnp.bfloat16),
            value_block,
            preferred_element_type=jnp.float32,
        )
        return (sum_now, acc_now)

    block_sum, block_acc = lax.fori_loop(
        0,
        row_count // step_rows,
        weight_step,
        (jnp.zeros(stat_shape, jnp.float32), jnp.zeros(query_heads.shape, jnp.float32)),
    )
    return (block_peak, block_sum, block_acc)


def shards_any(
    queries, fresh_key_rows, fresh_value_rows, visible, prefix_keys, cached_value_rows, out_weight
):
    query_rows, self_key_rows, own_values = (
        lax.all_to_all(queries[0], "tp", split_axis=1, concat_axis=0, tiled=True),
        lax.all_to_all(fresh_key_rows[0], "tp", split_axis=1, concat_axis=0, tiled=True),
        lax.all_to_all(fresh_value_rows[0], "tp", split_axis=1, concat_axis=0, tiled=True),
    )
    kv_heads = prefix_keys.shape[1] // HEAD_WIDTH
    tok_rows = query_rows.shape[0]
    block_rows = prefix_keys.shape[0]
    per_group = query_rows.shape[1] // (kv_heads * HEAD_WIDTH)
    seq_index = lax.axis_index("seq")
    query_heads = query_rows.reshape(tok_rows, kv_heads, per_group, HEAD_WIDTH)
    self_key_rows = self_key_rows.reshape(tok_rows, kv_heads, HEAD_WIDTH)
    own_vectors = own_values.reshape(tok_rows, kv_heads, 1, HEAD_WIDTH).astype(jnp.float32)
    self_score_row = (
        jnp.einsum(
            "tkgd,tkd->tkg", query_heads, self_key_rows, preferred_element_type=jnp.float32
        )
        * SCALE
    )
    seq_count = lax.axis_size("seq")
    everyone = lax.all_gather(query_rows, "seq", axis=0, tiled=True)
    blocks = everyone.reshape(seq_count, tok_rows, kv_heads, per_group, HEAD_WIDTH)
    all_lengths = visible[0].reshape(seq_count, tok_rows)
    prefix_start = seq_index * block_rows

    def partial_block(item_pair):
        return block_partial(
            item_pair[0], item_pair[1], prefix_keys, cached_value_rows, prefix_start
        )

    part_max, part_sum, part_acc = lax.map(partial_block, (blocks, all_lengths))
    part_max, part_sum, part_acc = (
        lax.all_to_all(part_max, "seq", split_axis=0, concat_axis=0, tiled=True),
        lax.all_to_all(part_sum, "seq", split_axis=0, concat_axis=0, tiled=True),
        lax.all_to_all(part_acc, "seq", split_axis=0, concat_axis=0, tiled=True),
    )
    run_max = jnp.max(part_max, axis=0)
    anchor = jnp.where(jnp.isinf(run_max), 0.0, run_max)
    part_factor = jnp.exp(part_max - anchor[None])
    run_sum = jnp.sum(part_sum * part_factor, axis=0)
    run_acc = jnp.sum(part_acc * part_factor[..., None], axis=0)
    row_peak = jnp.maximum(run_max, self_score_row)
    fade = jnp.exp(run_max - row_peak)
    own_weight = jnp.exp(self_score_row - row_peak)
    own_rounded = lax.optimization_barrier(own_weight.astype(jnp.bfloat16)).astype(jnp.float32)
    total_sum = run_sum * fade + own_weight
    total_acc = run_acc * fade[..., None] + own_rounded[..., None] * own_vectors
    context = (
        (total_acc / total_sum[..., None])
        .astype(jnp.bfloat16)
        .reshape(tok_rows, kv_heads * per_group * HEAD_WIDTH)
    )
    partial_out = jnp.dot(
        lax.all_gather(context, "seq", axis=0, tiled=True),
        out_weight,
        preferred_element_type=jnp.float32,
    )
    summed = lax.psum_scatter(partial_out, "tp", scatter_dimension=0, tiled=True)
    return summed.astype(jnp.bfloat16)[None]


EXPONENT = SCALE * math.log2(math.e)
VMEM_BYTES = 20 * 2**20
UNIT_ROWS = 128
FETCHES = 4
SETTLE_FIRST = 10**11
SETTLE_LAST = 10**10
PACK_BYTES = 56 * 2**20
ATTEND_BYTES = 40 * 2**20
LOAD_BYTES = 30 * 2**20
PROJECT_BYTES = 16 * 2**20


def swap(array, axis, mask):
    return lax.ppermute(array, axis, [(i, i ^ mask) for i in range(lax.axis_size(axis))])


def swap_by_core(array, mask):
    count = 2 * lax.axis_size("seq")
    pairs = [(i, i ^ (2 * (mask + i % 2))) for i in range(count)]
    return lax.ppermute(array, ("seq", "rep"), pairs)


def tile_at(index, width):
    return pl.ds(pl.multiple_of(index * width, width), width)


def side_by_side(array, times):
    return jnp.concatenate([array] * times, axis=1)


def vmem():
    return pl.BlockSpec(memory_space=pltpu.VMEM)


def hbm():
    return pl.BlockSpec(memory_space=pltpu.HBM)


def params(limit=VMEM_BYTES):
    return pltpu.CompilerParams(vmem_limit_bytes=limit)


def cost(flops, bytes_accessed, transcendentals=0):
    return pl.CostEstimate(
        flops=flops, bytes_accessed=bytes_accessed, transcendentals=transcendentals
    )


def pack_queries_kernel(seq_count, *refs):
    row_refs, out_ref, held_refs, sems = refs[:3], refs[3], refs[4:7], refs[7]
    copies = [
        pltpu.make_async_copy(ref, held, sems.at[i])
        for i, (ref, held) in enumerate(zip(row_refs, held_refs))
    ]
    for copy in copies:
        copy.start()
    for copy in copies:
        copy.wait()
    tokens = row_refs[0].shape[0]
    count = out_ref.shape[0] // tokens
    for owner in range(count):
        head = owner % 2 * seq_count + owner // 2
        to = 0
        for ref in held_refs:
            part = ref.shape[1] // count
            out_ref[owner * tokens : (owner + 1) * tokens, to : to + part] = ref[
                :, head * part : (head + 1) * part
            ]
            to += part


def pack_queries(rows, seq_count):
    count = 2 * seq_count
    shape = (rows[0].shape[0] * count, sum(a.shape[1] for a in rows) // count)
    return pl.pallas_call(
        functools.partial(pack_queries_kernel, seq_count),
        out_shape=jax.ShapeDtypeStruct(shape, jnp.bfloat16),
        in_specs=[hbm()] * 3,
        out_specs=vmem(),
        scratch_shapes=[pltpu.VMEM(a.shape, a.dtype) for a in rows]
        + [pltpu.SemaphoreType.DMA((3,))],
        compiler_params=params(PACK_BYTES),
        cost_estimate=cost(0, 2**19),
        name="pack_queries",
    )(*rows)


def settle_kernel(*refs):
    del refs


def settle(arrays, declared):
    count = len(arrays)
    return pl.pallas_call(
        settle_kernel,
        out_shape=[jax.ShapeDtypeStruct(a.shape, a.dtype) for a in arrays],
        in_specs=[vmem()] * count,
        out_specs=[vmem()] * count,
        input_output_aliases={i: i for i in range(count)},
        compiler_params=params(2**20),
        cost_estimate=cost(declared, 2**20),
        name="settle",
    )(*arrays)


def lengths_kernel(visible_ref, out_ref):
    tokens = out_ref.shape[0]
    diagonal = lax.broadcasted_iota(jnp.int32, (tokens, tokens), 0) == lax.broadcasted_iota(
        jnp.int32, (tokens, tokens), 1
    )
    lengths = jnp.sum(jnp.where(diagonal, visible_ref[...], 0), axis=-1, keepdims=True)
    out_ref[...] = jnp.broadcast_to(lengths, out_ref.shape)


def spread_lengths(visible):
    return pl.pallas_call(
        lengths_kernel,
        out_shape=jax.ShapeDtypeStruct((visible.shape[1], HEAD_WIDTH), jnp.int32),
        in_specs=[vmem()],
        out_specs=vmem(),
        compiler_params=params(),
        cost_estimate=cost(0, 2**15),
        name="spread_lengths",
    )(visible)


def half_of(rows, side):
    half = rows.shape[0] // 2
    return jnp.where(side == 0, rows[:half, :], rows[half:, :])


def tile_copies(masks, weight_ref, tile_refs, sems):
    depth = tile_refs[0].shape[0]
    rows = depth // FETCHES
    seq = lax.axis_index("seq")
    return [
        pltpu.make_async_copy(
            weight_ref.at[pl.ds(pl.multiple_of((seq ^ mask) * depth + n * rows, rows), rows), :],
            tile_ref.at[pl.ds(n * rows, rows), :],
            sems.at[i * FETCHES + n],
        )
        for i, (mask, tile_ref) in enumerate(zip(masks, tile_refs))
        for n in range(FETCHES)
    ]


def multiply(x_ref, w_ref, finish):
    columns = w_ref.shape[1]
    width = math.gcd(columns, 512)
    for start in range(0, columns, width):
        at = slice(start, start + width)
        finish(at, jnp.dot(x_ref[...], w_ref[:, at], preferred_element_type=jnp.float32))


def attend_kernel(heads, far_masks, block_rows, rows_ref, lengths_ref, own_ref, *refs):
    pieces = 2 * len(far_masks) + 2
    piece_refs, weight_ref = refs[:pieces], refs[pieces]
    out_ref, theirs_ref, tile_ref, sems = refs[pieces + 1 :]
    seq, tp, rep = lax.axis_index("seq"), lax.axis_index("tp"), lax.axis_index("rep")
    copies = tile_copies([0], weight_ref, [tile_ref], sems)
    for copy in copies:
        copy.start()
    @pl.when(tp >= 0)
    def compute():
        tokens = out_ref.shape[0]
        half = block_rows // 2
        lane = lax.broadcasted_iota(jnp.int32, (1, half), 1)
        blocks = []

        def whole(ref, mask):
            for first in (0, half):
                rows, values = slice(first, first + half), slice(block_rows + first, block_rows + first + half)
                blocks.append((ref, rows, values, (seq ^ mask) * block_rows + first + lane))

        whole(own_ref, 0)
        for i, ref in enumerate(piece_refs[:-2]):
            core = rep if i % 2 == 0 else 1 - rep
            whole(ref, far_masks[i // 2] + core)
        for ref, core in zip(piece_refs[-2:], (rep, 1 - rep)):
            first = (seq ^ 1) * block_rows + core * half
            blocks.append((ref, slice(0, half), slice(half, 2 * half), first + lane))
        width = heads * HEAD_WIDTH
        fresh_key = rows_ref[:, width : width + HEAD_WIDTH].astype(jnp.float32)
        fresh_value = rows_ref[:, width + HEAD_WIDTH :].astype(jnp.float32)
        group = max(1, UNIT_ROWS // tokens)
        lengths = jnp.concatenate([lengths_ref[...]] * group, axis=0)
        fresh_key = jnp.concatenate([fresh_key] * group, axis=0)
        start = jnp.concatenate([fresh_value, jnp.ones_like(fresh_value)], axis=1)
        start = jnp.concatenate([start] * group, axis=0)
        for first in range(0, heads, group):
            query = jnp.concatenate(
                [
                    rows_ref[:, h * HEAD_WIDTH : (h + 1) * HEAD_WIDTH]
                    for h in range(first, first + group)
                ],
                axis=0,
            )
            own = jnp.sum(query.astype(jnp.float32) * fresh_key, axis=-1, keepdims=True)
            own = jnp.broadcast_to(own, (group * tokens, HEAD_WIDTH))
            top, scores = own, []
            for ref, rows, _, position in blocks:
                score = lax.dot_general(
                    query, ref[rows, :], (((1,), (1,)), ((), ())), preferred_element_type=jnp.float32
                )
                hidden = position >= side_by_side(lengths, half // HEAD_WIDTH)
                score = jnp.where(hidden, HIDDEN, score)
                for i in range(0, half, HEAD_WIDTH):
                    top = jnp.maximum(top, score[:, i : i + HEAD_WIDTH])
                scores.append(score)
            peak = jnp.broadcast_to(jnp.max(top, axis=-1, keepdims=True), own.shape)
            acc = start * side_by_side(jnp.exp2((own - peak) * EXPONENT), 2)
            for score, (ref, _, rows, _) in zip(scores, blocks):
                weights = jnp.exp2((score - side_by_side(peak, half // HEAD_WIDTH)) * EXPONENT)
                values = ref[rows, :]
                acc = acc + jnp.dot(
                    weights.astype(jnp.bfloat16),
                    jnp.concatenate([values, jnp.ones_like(values)], axis=1),
                    preferred_element_type=jnp.float32,
                )
            context = (acc[:, :HEAD_WIDTH] / acc[:, HEAD_WIDTH:]).astype(jnp.bfloat16)
            for i in range(group):
                column = (first + i) * HEAD_WIDTH
                head = context[i * tokens : (i + 1) * tokens, :]
                out_ref[:, column : column + HEAD_WIDTH] = head
                theirs_ref[:, column : column + HEAD_WIDTH] = half_of(head, 1 - tp)

    for copy in copies:
        copy.wait()


def attend(heads, far_masks, query_rows, lengths, own, pieces, weight):
    tokens = query_rows.shape[0]
    block_rows = own.shape[0] // 2
    work = tokens * heads * block_rows * 2 * (1 + len(far_masks))
    depth = heads * HEAD_WIDTH
    return pl.pallas_call(
        functools.partial(attend_kernel, heads, far_masks, block_rows),
        out_shape=[
            jax.ShapeDtypeStruct((tokens, depth), jnp.bfloat16),
            jax.ShapeDtypeStruct((tokens // 2, depth), jnp.bfloat16),
            jax.ShapeDtypeStruct((depth, weight.shape[1]), weight.dtype),
        ],
        in_specs=[vmem()] * (3 + len(pieces)) + [hbm()],
        out_specs=[vmem()] * 3,
        scratch_shapes=[pltpu.SemaphoreType.DMA((FETCHES,))],
        compiler_params=params(ATTEND_BYTES),
        cost_estimate=cost(6 * work * HEAD_WIDTH, 2**20, work),
        name="attend",
    )(query_rows, lengths, own, *pieces, weight)


def load_kernel(masks, weight_ref, x_ref, first_ref, acc_ref, ours_ref, *refs):
    tile_refs, sems = refs[:-1], refs[-1]
    tp = lax.axis_index("tp")
    copies = tile_copies(masks, weight_ref, tile_refs, sems)
    for copy in copies:
        copy.start()
    ours_ref[...] = half_of(x_ref[...], tp)

    def finish(at, part):
        acc_ref[:, at] = part

    @pl.when(tp >= 0)
    def compute():
        multiply(x_ref, first_ref, finish)

    for copy in copies:
        copy.wait()


def load(weight, context, tile, masks):
    tokens, (depth, columns) = context.shape[0], tile.shape
    return pl.pallas_call(
        functools.partial(load_kernel, masks),
        out_shape=[
            jax.ShapeDtypeStruct((tokens, columns), jnp.float32),
            jax.ShapeDtypeStruct((tokens // 2, depth), jnp.bfloat16),
        ]
        + [jax.ShapeDtypeStruct(tile.shape, tile.dtype)] * len(masks),
        in_specs=[hbm(), vmem(), vmem()],
        out_specs=[vmem()] * (2 + len(masks)),
        scratch_shapes=[pltpu.SemaphoreType.DMA((FETCHES * len(masks),))],
        compiler_params=params(LOAD_BYTES),
        cost_estimate=cost(2 * tokens * depth * columns, len(masks) * depth * columns * 2),
        name="load",
    )(weight, context, tile)


def project_kernel(side, x_ref, w_ref, acc_ref, out_ref):
    tp = lax.axis_index("tp")

    def finish(at, part):
        acc = acc_ref[:, at]
        if side is not None:
            acc = half_of(acc, tp if side == 0 else 1 - tp)
        out_ref[:, at] = (part + acc).astype(out_ref.dtype)

    multiply(x_ref, w_ref, finish)


def project(context, tile, acc, side=None, dtype=jnp.float32):
    tokens, columns = context.shape[0], tile.shape[1]
    return pl.pallas_call(
        functools.partial(project_kernel, side),
        out_shape=jax.ShapeDtypeStruct((tokens, columns), dtype),
        in_specs=[vmem()] * 3,
        out_specs=vmem(),
        compiler_params=params(PROJECT_BYTES),
        cost_estimate=cost(2 * context.size * columns, 2 * tile.size),
        name="project",
    )(context, tile, acc)


def add_kernel(*refs):
    out_ref = refs[-1]
    count = (len(refs) - 1) // 2
    start = 0
    for keep_ref, got_ref in zip(refs[:count], refs[count:-1]):
        width = keep_ref.shape[1]
        total = keep_ref[...] + got_ref[...].astype(jnp.float32)
        out_ref[0, :, start : start + width] = total.astype(out_ref.dtype)
        start += width


def add(keeps, gots):
    shape = (1, keeps[0].shape[0], sum(a.shape[1] for a in keeps))
    return pl.pallas_call(
        add_kernel,
        out_shape=jax.ShapeDtypeStruct(shape, jnp.bfloat16),
        in_specs=[vmem()] * (2 * len(keeps)),
        out_specs=vmem(),
        compiler_params=params(PROJECT_BYTES),
        cost_estimate=cost(0, 2**19),
        name="add",
    )(*keeps, *gots)


def shards_by_head(
    queries, fresh_key_rows, fresh_value_rows, visible, prefix_keys, cached_value_rows, out_weight
):
    heads = queries.shape[2] // fresh_key_rows.shape[2]
    masks = list(range(1, lax.axis_size("seq")))
    rows = [queries[0], fresh_key_rows[0], fresh_value_rows[0]]
    seq, rep = lax.axis_index("seq"), lax.axis_index("rep")
    half_rows = prefix_keys.shape[0] // 2

    def cut(first, count, head):
        return jnp.concatenate(
            [
                lax.dynamic_slice(table, (first, head * HEAD_WIDTH), (count, HEAD_WIDTH))
                for table in (prefix_keys, cached_value_rows)
            ]
        )

    far_masks = masks[1::2]
    far = [swap_by_core(cut(0, 2 * half_rows, seq ^ (m + rep)), m) for m in far_masks]
    near = swap(cut(rep * half_rows, half_rows, seq ^ 1), "seq", 1)
    own = cut(0, 2 * half_rows, seq)
    query_rows = lax.all_to_all(
        pack_queries(rows, 1 + len(masks)), ("seq", "tp"), split_axis=0, concat_axis=0, tiled=True
    )
    lengths = spread_lengths(visible)
    far = settle(far, SETTLE_FIRST)
    pieces = [piece for mine in (*far, near) for piece in (mine, swap(mine, "rep", 1))]
    context, theirs, tile = attend(heads, far_masks, query_rows, lengths, own, pieces, out_weight)

    order = masks[-1:] + masks[:-1]
    chunks = [swap(context, "seq", mask) for mask in order[:-1]]
    first = swap(theirs, "seq", order[-1])
    acc, ours, *tiles = load(out_weight, context, tile, order)
    (second,) = settle([swap(ours, "seq", order[-1])], SETTLE_LAST)
    for chunk, tile in zip(chunks, tiles):
        acc = project(chunk, tile, acc)
    got = swap(project(first, tiles[-1], acc, 1, jnp.bfloat16), "tp", 1)
    return add([project(second, tiles[-1], acc, 0)], [got])


def solution(mesh):
    in_specs = (
        P("rep", ("groups", "seq", "tp"), None),
        P("rep", ("groups", "seq", "tp"), None),
        P("rep", ("groups", "seq", "tp"), None),
        P("rep", "groups"),
        P(("groups", "seq"), "tp"),
        P(("groups", "seq"), "tp"),
        P("tp", "seq"),
    )
    out_specs = P("rep", ("groups", "tp"), "seq")
    sizes = mesh.shape
    seq_count = sizes["seq"]

    def shards(*args):
        local_heads = args[4].shape[1] // HEAD_WIDTH
        by_head = (
            local_heads == seq_count
            and seq_count in (4, 8)
            and sizes["tp"] == 2
            and sizes["rep"] == 2
            and args[0].shape[2] // args[1].shape[2] % 2 == 0
        )
        return (shards_by_head if by_head else shards_any)(*args)

    return jax.shard_map(shards, mesh=mesh, in_specs=in_specs, out_specs=out_specs, check_vma=False)
```

```python
import functools
import math

import jax
import jax.numpy as jnp
from jax import lax
from jax.experimental import pallas as pl
from jax.experimental.pallas import tpu as pltpu
from jax.sharding import PartitionSpec as P

HEAD_WIDTH = 128
HIDDEN = -1e30
SCALE = 1.0 / math.sqrt(HEAD_WIDTH)


def block_partial(query_heads, lengths, key_rows, value_rows, offset):
    kv_heads = query_heads.shape[1]
    row_count = key_rows.shape[0]
    step_rows = math.gcd(row_count, 512)
    stat_shape = query_heads.shape[:3]

    def masked_scores(turn_index):
        first_row = turn_index * step_rows
        key_block = lax.dynamic_slice_in_dim(key_rows, first_row, step_rows, 0)
        key_block = key_block.reshape(step_rows, kv_heads, HEAD_WIDTH)
        scores = (
            jnp.einsum("tkgd,pkd->tkgp", query_heads, key_block, preferred_element_type=jnp.float32)
            * SCALE
        )
        position = offset + first_row + jnp.arange(step_rows, dtype=jnp.int32)
        visible_mask = (position[None, :] < lengths[:, None])[:, None, None, :]
        return (scores, visible_mask, first_row)

    def peak_step(turn_index, peak_now):
        scores, visible_mask, _ = masked_scores(turn_index)
        return jnp.maximum(peak_now, jnp.max(jnp.where(visible_mask, scores, -jnp.inf), axis=-1))

    block_peak = lax.fori_loop(
        0, row_count // step_rows, peak_step, jnp.full(stat_shape, -jnp.inf, jnp.float32)
    )
    anchor = jnp.where(jnp.isinf(block_peak), 0.0, block_peak)

    def weight_step(turn_index, state_now):
        sum_now, acc_now = state_now
        scores, visible_mask, first_row = masked_scores(turn_index)
        value_block = lax.dynamic_slice_in_dim(value_rows, first_row, step_rows, 0)
        value_block = value_block.reshape(step_rows, kv_heads, HEAD_WIDTH)
        weights = jnp.where(visible_mask, jnp.exp(scores - anchor[..., None]), 0.0)
        sum_now = sum_now + jnp.sum(weights, axis=-1)
        acc_now = acc_now + jnp.einsum(
            "tkgp,pkd->tkgd",
            weights.astype(jnp.bfloat16),
            value_block,
            preferred_element_type=jnp.float32,
        )
        return (sum_now, acc_now)

    block_sum, block_acc = lax.fori_loop(
        0,
        row_count // step_rows,
        weight_step,
        (jnp.zeros(stat_shape, jnp.float32), jnp.zeros(query_heads.shape, jnp.float32)),
    )
    return (block_peak, block_sum, block_acc)


def shards_any(
    queries, fresh_key_rows, fresh_value_rows, visible, prefix_keys, cached_value_rows, out_weight
):
    query_rows, self_key_rows, own_values = (
        lax.all_to_all(queries[0], "tp", split_axis=1, concat_axis=0, tiled=True),
        lax.all_to_all(fresh_key_rows[0], "tp", split_axis=1, concat_axis=0, tiled=True),
        lax.all_to_all(fresh_value_rows[0], "tp", split_axis=1, concat_axis=0, tiled=True),
    )
    kv_heads = prefix_keys.shape[1] // HEAD_WIDTH
    tok_rows = query_rows.shape[0]
    block_rows = prefix_keys.shape[0]
    per_group = query_rows.shape[1] // (kv_heads * HEAD_WIDTH)
    seq_index = lax.axis_index("seq")
    query_heads = query_rows.reshape(tok_rows, kv_heads, per_group, HEAD_WIDTH)
    self_key_rows = self_key_rows.reshape(tok_rows, kv_heads, HEAD_WIDTH)
    own_vectors = own_values.reshape(tok_rows, kv_heads, 1, HEAD_WIDTH).astype(jnp.float32)
    self_score_row = (
        jnp.einsum(
            "tkgd,tkd->tkg", query_heads, self_key_rows, preferred_element_type=jnp.float32
        )
        * SCALE
    )
    seq_count = lax.axis_size("seq")
    everyone = lax.all_gather(query_rows, "seq", axis=0, tiled=True)
    blocks = everyone.reshape(seq_count, tok_rows, kv_heads, per_group, HEAD_WIDTH)
    all_lengths = visible[0].reshape(seq_count, tok_rows)
    prefix_start = seq_index * block_rows

    def partial_block(item_pair):
        return block_partial(
            item_pair[0], item_pair[1], prefix_keys, cached_value_rows, prefix_start
        )

    part_max, part_sum, part_acc = lax.map(partial_block, (blocks, all_lengths))
    part_max, part_sum, part_acc = (
        lax.all_to_all(part_max, "seq", split_axis=0, concat_axis=0, tiled=True),
        lax.all_to_all(part_sum, "seq", split_axis=0, concat_axis=0, tiled=True),
        lax.all_to_all(part_acc, "seq", split_axis=0, concat_axis=0, tiled=True),
    )
    run_max = jnp.max(part_max, axis=0)
    anchor = jnp.where(jnp.isinf(run_max), 0.0, run_max)
    part_factor = jnp.exp(part_max - anchor[None])
    run_sum = jnp.sum(part_sum * part_factor, axis=0)
    run_acc = jnp.sum(part_acc * part_factor[..., None], axis=0)
    row_peak = jnp.maximum(run_max, self_score_row)
    fade = jnp.exp(run_max - row_peak)
    own_weight = jnp.exp(self_score_row - row_peak)
    own_rounded = lax.optimization_barrier(own_weight.astype(jnp.bfloat16)).astype(jnp.float32)
    total_sum = run_sum * fade + own_weight
    total_acc = run_acc * fade[..., None] + own_rounded[..., None] * own_vectors
    context = (
        (total_acc / total_sum[..., None])
        .astype(jnp.bfloat16)
        .reshape(tok_rows, kv_heads * per_group * HEAD_WIDTH)
    )
    partial_out = jnp.dot(
        lax.all_gather(context, "seq", axis=0, tiled=True),
        out_weight,
        preferred_element_type=jnp.float32,
    )
    summed = lax.psum_scatter(partial_out, "tp", scatter_dimension=0, tiled=True)
    return summed.astype(jnp.bfloat16)[None]


EXPONENT = SCALE * math.log2(math.e)
VMEM_BYTES = 20 * 2**20
UNIT_ROWS = 128
FETCHES = 4
SETTLE_FIRST = 10**11
SETTLE_LAST = 10**10
PACK_BYTES = 56 * 2**20
ATTEND_BYTES = 40 * 2**20
LOAD_BYTES = 30 * 2**20
PROJECT_BYTES = 16 * 2**20


def swap(array, axis, mask):
    return lax.ppermute(array, axis, [(i, i ^ mask) for i in range(lax.axis_size(axis))])


def swap_by_core(array, mask):
    count = 2 * lax.axis_size("seq")
    pairs = [(i, i ^ (2 * (mask + i % 2))) for i in range(count)]
    return lax.ppermute(array, ("seq", "rep"), pairs)


def tile_at(index, width):
    return pl.ds(pl.multiple_of(index * width, width), width)


def side_by_side(array, times):
    return jnp.concatenate([array] * times, axis=1)


def vmem():
    return pl.BlockSpec(memory_space=pltpu.VMEM)


def hbm():
    return pl.BlockSpec(memory_space=pltpu.HBM)


def params(limit=VMEM_BYTES):
    return pltpu.CompilerParams(vmem_limit_bytes=limit)


def cost(flops, bytes_accessed, transcendentals=0):
    return pl.CostEstimate(
        flops=flops, bytes_accessed=bytes_accessed, transcendentals=transcendentals
    )


def pack_queries_kernel(seq_count, *refs):
    row_refs, out_ref, held_refs, sems = refs[:3], refs[3], refs[4:7], refs[7]
    copies = [
        pltpu.make_async_copy(ref, held, sems.at[i])
        for i, (ref, held) in enumerate(zip(row_refs, held_refs))
    ]
    for copy in copies:
        copy.start()
    for copy in copies:
        copy.wait()
    tokens = row_refs[0].shape[0]
    count = out_ref.shape[0] // tokens
    for owner in range(count):
        head = owner % 2 * seq_count + owner // 2
        to = 0
        for ref in held_refs:
            part = ref.shape[1] // count
            out_ref[owner * tokens : (owner + 1) * tokens, to : to + part] = ref[
                :, head * part : (head + 1) * part
            ]
            to += part


def pack_queries(rows, seq_count):
    count = 2 * seq_count
    shape = (rows[0].shape[0] * count, sum(a.shape[1] for a in rows) // count)
    return pl.pallas_call(
        functools.partial(pack_queries_kernel, seq_count),
        out_shape=jax.ShapeDtypeStruct(shape, jnp.bfloat16),
        in_specs=[hbm()] * 3,
        out_specs=vmem(),
        scratch_shapes=[pltpu.VMEM(a.shape, a.dtype) for a in rows]
        + [pltpu.SemaphoreType.DMA((3,))],
        compiler_params=params(PACK_BYTES),
        cost_estimate=cost(0, 2**19),
        name="pack_queries",
    )(*rows)


def settle_kernel(*refs):
    del refs


def settle(arrays, declared):
    count = len(arrays)
    return pl.pallas_call(
        settle_kernel,
        out_shape=[jax.ShapeDtypeStruct(a.shape, a.dtype) for a in arrays],
        in_specs=[vmem()] * count,
        out_specs=[vmem()] * count,
        input_output_aliases={i: i for i in range(count)},
        compiler_params=params(2**20),
        cost_estimate=cost(declared, 2**20),
        name="settle",
    )(*arrays)


def lengths_kernel(visible_ref, out_ref):
    tokens = out_ref.shape[0]
    diagonal = lax.broadcasted_iota(jnp.int32, (tokens, tokens), 0) == lax.broadcasted_iota(
        jnp.int32, (tokens, tokens), 1
    )
    lengths = jnp.sum(jnp.where(diagonal, visible_ref[...], 0), axis=-1, keepdims=True)
    out_ref[...] = jnp.broadcast_to(lengths, out_ref.shape)


def spread_lengths(visible):
    return pl.pallas_call(
        lengths_kernel,
        out_shape=jax.ShapeDtypeStruct((visible.shape[1], HEAD_WIDTH), jnp.int32),
        in_specs=[vmem()],
        out_specs=vmem(),
        compiler_params=params(),
        cost_estimate=cost(0, 2**15),
        name="spread_lengths",
    )(visible)


def half_of(rows, side):
    half = rows.shape[0] // 2
    return jnp.where(side == 0, rows[:half, :], rows[half:, :])


def tile_copies(masks, weight_ref, tile_refs, sems):
    depth = tile_refs[0].shape[0]
    rows = depth // FETCHES
    seq = lax.axis_index("seq")
    return [
        pltpu.make_async_copy(
            weight_ref.at[pl.ds(pl.multiple_of((seq ^ mask) * depth + n * rows, rows), rows), :],
            tile_ref.at[pl.ds(n * rows, rows), :],
            sems.at[i * FETCHES + n],
        )
        for i, (mask, tile_ref) in enumerate(zip(masks, tile_refs))
        for n in range(FETCHES)
    ]


def multiply(x_ref, w_ref, finish):
    columns = w_ref.shape[1]
    width = math.gcd(columns, 512)
    for start in range(0, columns, width):
        at = slice(start, start + width)
        finish(at, jnp.dot(x_ref[...], w_ref[:, at], preferred_element_type=jnp.float32))


def attend_kernel(heads, far_masks, block_rows, rows_ref, lengths_ref, own_ref, *refs):
    pieces = 2 * len(far_masks) + 2
    piece_refs, weight_ref = refs[:pieces], refs[pieces]
    out_ref, theirs_ref, tile_ref, sems = refs[pieces + 1 :]
    seq, tp, rep = lax.axis_index("seq"), lax.axis_index("tp"), lax.axis_index("rep")
    copies = tile_copies([0], weight_ref, [tile_ref], sems)
    for copy in copies:
        copy.start()
    @pl.when(tp >= 0)
    def compute():
        tokens = out_ref.shape[0]
        half = block_rows // 2
        lane = lax.broadcasted_iota(jnp.int32, (1, half), 1)
        blocks = []

        def whole(ref, mask):
            for first in (0, half):
                rows, values = slice(first, first + half), slice(block_rows + first, block_rows + first + half)
                blocks.append((ref, rows, values, (seq ^ mask) * block_rows + first + lane))

        whole(own_ref, 0)
        for i, ref in enumerate(piece_refs[:-2]):
            core = rep if i % 2 == 0 else 1 - rep
            whole(ref, far_masks[i // 2] + core)
        for ref, core in zip(piece_refs[-2:], (rep, 1 - rep)):
            first = (seq ^ 1) * block_rows + core * half
            blocks.append((ref, slice(0, half), slice(half, 2 * half), first + lane))
        width = heads * HEAD_WIDTH
        fresh_key = rows_ref[:, width : width + HEAD_WIDTH].astype(jnp.float32)
        fresh_value = rows_ref[:, width + HEAD_WIDTH :].astype(jnp.float32)
        group = max(1, UNIT_ROWS // tokens)
        lengths = jnp.concatenate([lengths_ref[...]] * group, axis=0)
        fresh_key = jnp.concatenate([fresh_key] * group, axis=0)
        start = jnp.concatenate([fresh_value, jnp.ones_like(fresh_value)], axis=1)
        start = jnp.concatenate([start] * group, axis=0)
        for first in range(0, heads, group):
            query = jnp.concatenate(
                [
                    rows_ref[:, h * HEAD_WIDTH : (h + 1) * HEAD_WIDTH]
                    for h in range(first, first + group)
                ],
                axis=0,
            )
            own = jnp.sum(query.astype(jnp.float32) * fresh_key, axis=-1, keepdims=True)
            own = jnp.broadcast_to(own, (group * tokens, HEAD_WIDTH))
            top, scores = own, []
            for ref, rows, _, position in blocks:
                score = lax.dot_general(
                    query, ref[rows, :], (((1,), (1,)), ((), ())), preferred_element_type=jnp.float32
                )
                hidden = position >= side_by_side(lengths, half // HEAD_WIDTH)
                score = jnp.where(hidden, HIDDEN, score)
                for i in range(0, half, HEAD_WIDTH):
                    top = jnp.maximum(top, score[:, i : i + HEAD_WIDTH])
                scores.append(score)
            peak = jnp.broadcast_to(jnp.max(top, axis=-1, keepdims=True), own.shape)
            acc = start * side_by_side(jnp.exp2((own - peak) * EXPONENT), 2)
            for score, (ref, _, rows, _) in zip(scores, blocks):
                weights = jnp.exp2((score - side_by_side(peak, half // HEAD_WIDTH)) * EXPONENT)
                values = ref[rows, :]
                acc = acc + jnp.dot(
                    weights.astype(jnp.bfloat16),
                    jnp.concatenate([values, jnp.ones_like(values)], axis=1),
                    preferred_element_type=jnp.float32,
                )
            context = (acc[:, :HEAD_WIDTH] / acc[:, HEAD_WIDTH:]).astype(jnp.bfloat16)
            for i in range(group):
                column = (first + i) * HEAD_WIDTH
                head = context[i * tokens : (i + 1) * tokens, :]
                out_ref[:, column : column + HEAD_WIDTH] = head
                theirs_ref[:, column : column + HEAD_WIDTH] = half_of(head, 1 - tp)

    for copy in copies:
        copy.wait()


def attend(heads, far_masks, query_rows, lengths, own, pieces, weight):
    tokens = query_rows.shape[0]
    block_rows = own.shape[0] // 2
    work = tokens * heads * block_rows * 2 * (1 + len(far_masks))
    depth = heads * HEAD_WIDTH
    return pl.pallas_call(
        functools.partial(attend_kernel, heads, far_masks, block_rows),
        out_shape=[
            jax.ShapeDtypeStruct((tokens, depth), jnp.bfloat16),
            jax.ShapeDtypeStruct((tokens // 2, depth), jnp.bfloat16),
            jax.ShapeDtypeStruct((depth, weight.shape[1]), weight.dtype),
        ],
        in_specs=[vmem()] * (3 + len(pieces)) + [hbm()],
        out_specs=[vmem()] * 3,
        scratch_shapes=[pltpu.SemaphoreType.DMA((FETCHES,))],
        compiler_params=params(ATTEND_BYTES),
        cost_estimate=cost(6 * work * HEAD_WIDTH, 2**20, work),
        name="attend",
    )(query_rows, lengths, own, *pieces, weight)


def load_kernel(masks, weight_ref, x_ref, first_ref, acc_ref, *refs):
    tile_refs, sems = refs[:-1], refs[-1]
    tp = lax.axis_index("tp")
    copies = tile_copies(masks, weight_ref, tile_refs, sems)
    for copy in copies:
        copy.start()

    def finish(at, part):
        acc_ref[:, at] = part

    @pl.when(tp >= 0)
    def compute():
        multiply(x_ref, first_ref, finish)

    for copy in copies:
        copy.wait()


def load(weight, context, tile, masks):
    tokens, (depth, columns) = context.shape[0], tile.shape
    return pl.pallas_call(
        functools.partial(load_kernel, masks),
        out_shape=[
            jax.ShapeDtypeStruct((tokens, columns), jnp.float32),
        ]
        + [jax.ShapeDtypeStruct(tile.shape, tile.dtype)] * len(masks),
        in_specs=[hbm(), vmem(), vmem()],
        out_specs=[vmem()] * (1 + len(masks)),
        scratch_shapes=[pltpu.SemaphoreType.DMA((FETCHES * len(masks),))],
        compiler_params=params(LOAD_BYTES),
        cost_estimate=cost(2 * tokens * depth * columns, len(masks) * depth * columns * 2),
        name="load",
    )(weight, context, tile)


def project_kernel(side, pass_on, x_ref, w_ref, acc_ref, *refs):
    tp = lax.axis_index("tp")
    out_ref = refs[-1]
    if pass_on:
        out_ref = refs[1]
        refs[2][...] = half_of(refs[0][...], tp)

    def finish(at, part):
        acc = acc_ref[:, at]
        if side is not None:
            acc = half_of(acc, tp if side == 0 else 1 - tp)
        out_ref[:, at] = (part + acc).astype(out_ref.dtype)

    multiply(x_ref, w_ref, finish)


def project(context, tile, acc, side=None, dtype=jnp.float32, pass_on=None):
    tokens, columns = context.shape[0], tile.shape[1]
    shapes = [jax.ShapeDtypeStruct((tokens, columns), dtype)]
    operands = [context, tile, acc]
    if pass_on is not None:
        operands.append(pass_on)
        shapes.append(jax.ShapeDtypeStruct((tokens // 2, pass_on.shape[1]), pass_on.dtype))
    return pl.pallas_call(
        functools.partial(project_kernel, side, pass_on is not None),
        out_shape=shapes,
        in_specs=[vmem()] * len(operands),
        out_specs=[vmem()] * len(shapes),
        compiler_params=params(PROJECT_BYTES),
        cost_estimate=cost(2 * context.size * columns, 2 * tile.size),
        name="project",
    )(*operands)


def add_kernel(*refs):
    out_ref = refs[-1]
    count = (len(refs) - 1) // 2
    start = 0
    for keep_ref, got_ref in zip(refs[:count], refs[count:-1]):
        width = keep_ref.shape[1]
        total = keep_ref[...] + got_ref[...].astype(jnp.float32)
        out_ref[0, :, start : start + width] = total.astype(out_ref.dtype)
        start += width


def add(keeps, gots):
    shape = (1, keeps[0].shape[0], sum(a.shape[1] for a in keeps))
    return pl.pallas_call(
        add_kernel,
        out_shape=jax.ShapeDtypeStruct(shape, jnp.bfloat16),
        in_specs=[vmem()] * (2 * len(keeps)),
        out_specs=vmem(),
        compiler_params=params(PROJECT_BYTES),
        cost_estimate=cost(0, 2**19),
        name="add",
    )(*keeps, *gots)


def shards_by_head(
    queries, fresh_key_rows, fresh_value_rows, visible, prefix_keys, cached_value_rows, out_weight
):
    heads = queries.shape[2] // fresh_key_rows.shape[2]
    masks = list(range(1, lax.axis_size("seq")))
    rows = [queries[0], fresh_key_rows[0], fresh_value_rows[0]]
    seq, rep = lax.axis_index("seq"), lax.axis_index("rep")
    half_rows = prefix_keys.shape[0] // 2

    def cut(first, count, head):
        return jnp.concatenate(
            [
                lax.dynamic_slice(table, (first, head * HEAD_WIDTH), (count, HEAD_WIDTH))
                for table in (prefix_keys, cached_value_rows)
            ]
        )

    far_masks = masks[1::2]
    far = [swap_by_core(cut(0, 2 * half_rows, seq ^ (m + rep)), m) for m in far_masks]
    near = swap(cut(rep * half_rows, half_rows, seq ^ 1), "seq", 1)
    own = cut(0, 2 * half_rows, seq)
    query_rows = lax.all_to_all(
        pack_queries(rows, 1 + len(masks)), ("seq", "tp"), split_axis=0, concat_axis=0, tiled=True
    )
    lengths = spread_lengths(visible)
    far = settle(far, SETTLE_FIRST)
    pieces = [piece for mine in (*far, near) for piece in (mine, swap(mine, "rep", 1))]
    context, theirs, tile = attend(heads, far_masks, query_rows, lengths, own, pieces, out_weight)

    order = masks[-1:] + masks[:-1]
    chunks = [swap(context, "seq", mask) for mask in order[:-1]]
    first = swap(theirs, "seq", order[-1])
    acc, *tiles = load(out_weight, context, tile, order)
    for i, (chunk, tile) in enumerate(zip(chunks, tiles)):
        acc, *ours = project(chunk, tile, acc, pass_on=context if i == 0 else None)
        if i == 0:
            (second,) = settle([swap(ours[0], "seq", order[-1])], SETTLE_LAST)
    (sums,) = project(first, tiles[-1], acc, 1, jnp.bfloat16)
    got = swap(sums, "tp", 1)
    (kept,) = project(second, tiles[-1], acc, 0)
    return add([kept], [got])


def solution(mesh):
    in_specs = (
        P("rep", ("groups", "seq", "tp"), None),
        P("rep", ("groups", "seq", "tp"), None),
        P("rep", ("groups", "seq", "tp"), None),
        P("rep", "groups"),
        P(("groups", "seq"), "tp"),
        P(("groups", "seq"), "tp"),
        P("tp", "seq"),
    )
    out_specs = P("rep", ("groups", "tp"), "seq")
    sizes = mesh.shape
    seq_count = sizes["seq"]

    def shards(*args):
        local_heads = args[4].shape[1] // HEAD_WIDTH
        by_head = (
            local_heads == seq_count
            and seq_count in (4, 8)
            and sizes["tp"] == 2
            and sizes["rep"] == 2
            and args[0].shape[2] // args[1].shape[2] % 2 == 0
        )
        return (shards_by_head if by_head else shards_any)(*args)

    return jax.shard_map(shards, mesh=mesh, in_specs=in_specs, out_specs=out_specs, check_vma=False)
```

```python
import functools
import math

import jax
import jax.numpy as jnp
from jax import lax
from jax.experimental import pallas as pl
from jax.experimental.pallas import tpu as pltpu
from jax.sharding import PartitionSpec as P

HEAD_WIDTH = 128
HIDDEN = -1e30
SCALE = 1.0 / math.sqrt(HEAD_WIDTH)


def block_partial(query_heads, lengths, key_rows, value_rows, offset):
    kv_heads = query_heads.shape[1]
    row_count = key_rows.shape[0]
    step_rows = math.gcd(row_count, 512)
    stat_shape = query_heads.shape[:3]

    def masked_scores(turn_index):
        first_row = turn_index * step_rows
        key_block = lax.dynamic_slice_in_dim(key_rows, first_row, step_rows, 0)
        key_block = key_block.reshape(step_rows, kv_heads, HEAD_WIDTH)
        scores = (
            jnp.einsum("tkgd,pkd->tkgp", query_heads, key_block, preferred_element_type=jnp.float32)
            * SCALE
        )
        position = offset + first_row + jnp.arange(step_rows, dtype=jnp.int32)
        visible_mask = (position[None, :] < lengths[:, None])[:, None, None, :]
        return (scores, visible_mask, first_row)

    def peak_step(turn_index, peak_now):
        scores, visible_mask, _ = masked_scores(turn_index)
        return jnp.maximum(peak_now, jnp.max(jnp.where(visible_mask, scores, -jnp.inf), axis=-1))

    block_peak = lax.fori_loop(
        0, row_count // step_rows, peak_step, jnp.full(stat_shape, -jnp.inf, jnp.float32)
    )
    anchor = jnp.where(jnp.isinf(block_peak), 0.0, block_peak)

    def weight_step(turn_index, state_now):
        sum_now, acc_now = state_now
        scores, visible_mask, first_row = masked_scores(turn_index)
        value_block = lax.dynamic_slice_in_dim(value_rows, first_row, step_rows, 0)
        value_block = value_block.reshape(step_rows, kv_heads, HEAD_WIDTH)
        weights = jnp.where(visible_mask, jnp.exp(scores - anchor[..., None]), 0.0)
        sum_now = sum_now + jnp.sum(weights, axis=-1)
        acc_now = acc_now + jnp.einsum(
            "tkgp,pkd->tkgd",
            weights.astype(jnp.bfloat16),
            value_block,
            preferred_element_type=jnp.float32,
        )
        return (sum_now, acc_now)

    block_sum, block_acc = lax.fori_loop(
        0,
        row_count // step_rows,
        weight_step,
        (jnp.zeros(stat_shape, jnp.float32), jnp.zeros(query_heads.shape, jnp.float32)),
    )
    return (block_peak, block_sum, block_acc)


def shards_any(
    queries, fresh_key_rows, fresh_value_rows, visible, prefix_keys, cached_value_rows, out_weight
):
    query_rows, self_key_rows, own_values = (
        lax.all_to_all(queries[0], "tp", split_axis=1, concat_axis=0, tiled=True),
        lax.all_to_all(fresh_key_rows[0], "tp", split_axis=1, concat_axis=0, tiled=True),
        lax.all_to_all(fresh_value_rows[0], "tp", split_axis=1, concat_axis=0, tiled=True),
    )
    kv_heads = prefix_keys.shape[1] // HEAD_WIDTH
    tok_rows = query_rows.shape[0]
    block_rows = prefix_keys.shape[0]
    per_group = query_rows.shape[1] // (kv_heads * HEAD_WIDTH)
    seq_index = lax.axis_index("seq")
    query_heads = query_rows.reshape(tok_rows, kv_heads, per_group, HEAD_WIDTH)
    self_key_rows = self_key_rows.reshape(tok_rows, kv_heads, HEAD_WIDTH)
    own_vectors = own_values.reshape(tok_rows, kv_heads, 1, HEAD_WIDTH).astype(jnp.float32)
    self_score_row = (
        jnp.einsum(
            "tkgd,tkd->tkg", query_heads, self_key_rows, preferred_element_type=jnp.float32
        )
        * SCALE
    )
    seq_count = lax.axis_size("seq")
    everyone = lax.all_gather(query_rows, "seq", axis=0, tiled=True)
    blocks = everyone.reshape(seq_count, tok_rows, kv_heads, per_group, HEAD_WIDTH)
    all_lengths = visible[0].reshape(seq_count, tok_rows)
    prefix_start = seq_index * block_rows

    def partial_block(item_pair):
        return block_partial(
            item_pair[0], item_pair[1], prefix_keys, cached_value_rows, prefix_start
        )

    part_max, part_sum, part_acc = lax.map(partial_block, (blocks, all_lengths))
    part_max, part_sum, part_acc = (
        lax.all_to_all(part_max, "seq", split_axis=0, concat_axis=0, tiled=True),
        lax.all_to_all(part_sum, "seq", split_axis=0, concat_axis=0, tiled=True),
        lax.all_to_all(part_acc, "seq", split_axis=0, concat_axis=0, tiled=True),
    )
    run_max = jnp.max(part_max, axis=0)
    anchor = jnp.where(jnp.isinf(run_max), 0.0, run_max)
    part_factor = jnp.exp(part_max - anchor[None])
    run_sum = jnp.sum(part_sum * part_factor, axis=0)
    run_acc = jnp.sum(part_acc * part_factor[..., None], axis=0)
    row_peak = jnp.maximum(run_max, self_score_row)
    fade = jnp.exp(run_max - row_peak)
    own_weight = jnp.exp(self_score_row - row_peak)
    own_rounded = lax.optimization_barrier(own_weight.astype(jnp.bfloat16)).astype(jnp.float32)
    total_sum = run_sum * fade + own_weight
    total_acc = run_acc * fade[..., None] + own_rounded[..., None] * own_vectors
    context = (
        (total_acc / total_sum[..., None])
        .astype(jnp.bfloat16)
        .reshape(tok_rows, kv_heads * per_group * HEAD_WIDTH)
    )
    partial_out = jnp.dot(
        lax.all_gather(context, "seq", axis=0, tiled=True),
        out_weight,
        preferred_element_type=jnp.float32,
    )
    summed = lax.psum_scatter(partial_out, "tp", scatter_dimension=0, tiled=True)
    return summed.astype(jnp.bfloat16)[None]


EXPONENT = SCALE * math.log2(math.e)
VMEM_BYTES = 20 * 2**20
UNIT_ROWS = 256
FETCHES = 1
SETTLE_FIRST = 10**11
SETTLE_LAST = 10**10
PACK_BYTES = 56 * 2**20
ATTEND_BYTES = 40 * 2**20
LOAD_BYTES = 30 * 2**20
PROJECT_BYTES = 16 * 2**20


def swap(array, axis, mask):
    return lax.ppermute(array, axis, [(i, i ^ mask) for i in range(lax.axis_size(axis))])


def swap_by_core(array, mask):
    count = 2 * lax.axis_size("seq")
    pairs = [(i, i ^ (2 * (mask + i % 2))) for i in range(count)]
    return lax.ppermute(array, ("seq", "rep"), pairs)


def tile_at(index, width):
    return pl.ds(pl.multiple_of(index * width, width), width)


def side_by_side(array, times):
    return jnp.concatenate([array] * times, axis=1)


def vmem():
    return pl.BlockSpec(memory_space=pltpu.VMEM)


def hbm():
    return pl.BlockSpec(memory_space=pltpu.HBM)


def params(limit=VMEM_BYTES):
    return pltpu.CompilerParams(vmem_limit_bytes=limit)


def cost(flops, bytes_accessed, transcendentals=0):
    return pl.CostEstimate(
        flops=flops, bytes_accessed=bytes_accessed, transcendentals=transcendentals
    )


def pack_queries_kernel(seq_count, *refs):
    row_refs, out_ref, held_refs, sems = refs[:3], refs[3], refs[4:7], refs[7]
    copies = [
        pltpu.make_async_copy(ref, held, sems.at[i])
        for i, (ref, held) in enumerate(zip(row_refs, held_refs))
    ]
    for copy in copies:
        copy.start()
    for copy in copies:
        copy.wait()
    tokens = row_refs[0].shape[0]
    count = out_ref.shape[0] // tokens
    for owner in range(count):
        head = owner % 2 * seq_count + owner // 2
        to = 0
        for ref in held_refs:
            part = ref.shape[1] // count
            out_ref[owner * tokens : (owner + 1) * tokens, to : to + part] = ref[
                :, head * part : (head + 1) * part
            ]
            to += part


def pack_queries(rows, seq_count):
    count = 2 * seq_count
    shape = (rows[0].shape[0] * count, sum(a.shape[1] for a in rows) // count)
    return pl.pallas_call(
        functools.partial(pack_queries_kernel, seq_count),
        out_shape=jax.ShapeDtypeStruct(shape, jnp.bfloat16),
        in_specs=[hbm()] * 3,
        out_specs=vmem(),
        scratch_shapes=[pltpu.VMEM(a.shape, a.dtype) for a in rows]
        + [pltpu.SemaphoreType.DMA((3,))],
        compiler_params=params(PACK_BYTES),
        cost_estimate=cost(0, 2**19),
        name="pack_queries",
    )(*rows)


def settle_kernel(*refs):
    del refs


def settle(arrays, declared):
    count = len(arrays)
    return pl.pallas_call(
        settle_kernel,
        out_shape=[jax.ShapeDtypeStruct(a.shape, a.dtype) for a in arrays],
        in_specs=[vmem()] * count,
        out_specs=[vmem()] * count,
        input_output_aliases={i: i for i in range(count)},
        compiler_params=params(2**20),
        cost_estimate=cost(declared, 2**20),
        name="settle",
    )(*arrays)


def lengths_kernel(visible_ref, out_ref):
    tokens = out_ref.shape[0]
    diagonal = lax.broadcasted_iota(jnp.int32, (tokens, tokens), 0) == lax.broadcasted_iota(
        jnp.int32, (tokens, tokens), 1
    )
    lengths = jnp.sum(jnp.where(diagonal, visible_ref[...], 0), axis=-1, keepdims=True)
    out_ref[...] = jnp.broadcast_to(lengths, out_ref.shape)


def spread_lengths(visible):
    return pl.pallas_call(
        lengths_kernel,
        out_shape=jax.ShapeDtypeStruct((visible.shape[1], HEAD_WIDTH), jnp.int32),
        in_specs=[vmem()],
        out_specs=vmem(),
        compiler_params=params(),
        cost_estimate=cost(0, 2**15),
        name="spread_lengths",
    )(visible)


def half_of(rows, side):
    half = rows.shape[0] // 2
    return jnp.where(side == 0, rows[:half, :], rows[half:, :])


def tile_copies(masks, weight_ref, tile_refs, sems):
    depth = tile_refs[0].shape[0]
    rows = depth // FETCHES
    seq = lax.axis_index("seq")
    return [
        pltpu.make_async_copy(
            weight_ref.at[pl.ds(pl.multiple_of((seq ^ mask) * depth + n * rows, rows), rows), :],
            tile_ref.at[pl.ds(n * rows, rows), :],
            sems.at[i * FETCHES + n],
        )
        for i, (mask, tile_ref) in enumerate(zip(masks, tile_refs))
        for n in range(FETCHES)
    ]


def multiply(x_ref, w_ref, finish):
    columns = w_ref.shape[1]
    width = math.gcd(columns, 512)
    for start in range(0, columns, width):
        at = slice(start, start + width)
        finish(at, jnp.dot(x_ref[...], w_ref[:, at], preferred_element_type=jnp.float32))


def attend_kernel(heads, far_masks, block_rows, rows_ref, lengths_ref, own_ref, *refs):
    pieces = 2 * len(far_masks) + 2
    piece_refs, weight_ref = refs[:pieces], refs[pieces]
    out_ref, theirs_ref, tile_ref, sems = refs[pieces + 1 :]
    seq, tp, rep = lax.axis_index("seq"), lax.axis_index("tp"), lax.axis_index("rep")
    copies = tile_copies([0], weight_ref, [tile_ref], sems)
    for copy in copies:
        copy.start()
    @pl.when(tp >= 0)
    def compute():
        tokens = out_ref.shape[0]
        half = block_rows // 2
        lane = lax.broadcasted_iota(jnp.int32, (1, half), 1)
        blocks = []

        def whole(ref, mask):
            for first in (0, half):
                rows, values = slice(first, first + half), slice(block_rows + first, block_rows + first + half)
                blocks.append((ref, rows, values, (seq ^ mask) * block_rows + first + lane))

        whole(own_ref, 0)
        for i, ref in enumerate(piece_refs[:-2]):
            core = rep if i % 2 == 0 else 1 - rep
            whole(ref, far_masks[i // 2] + core)
        for ref, core in zip(piece_refs[-2:], (rep, 1 - rep)):
            first = (seq ^ 1) * block_rows + core * half
            blocks.append((ref, slice(0, half), slice(half, 2 * half), first + lane))
        width = heads * HEAD_WIDTH
        fresh_key = rows_ref[:, width : width + HEAD_WIDTH].astype(jnp.float32)
        fresh_value = rows_ref[:, width + HEAD_WIDTH :].astype(jnp.float32)
        group = max(1, UNIT_ROWS // tokens)
        lengths = jnp.concatenate([lengths_ref[...]] * group, axis=0)
        fresh_key = jnp.concatenate([fresh_key] * group, axis=0)
        start = jnp.concatenate([fresh_value, jnp.ones_like(fresh_value)], axis=1)
        start = jnp.concatenate([start] * group, axis=0)
        for first in range(0, heads, group):
            query = jnp.concatenate(
                [
                    rows_ref[:, h * HEAD_WIDTH : (h + 1) * HEAD_WIDTH]
                    for h in range(first, first + group)
                ],
                axis=0,
            )
            own = jnp.sum(query.astype(jnp.float32) * fresh_key, axis=-1, keepdims=True)
            own = jnp.broadcast_to(own, (group * tokens, HEAD_WIDTH))
            top, scores = own, []
            for ref, rows, _, position in blocks:
                score = lax.dot_general(
                    query, ref[rows, :], (((1,), (1,)), ((), ())), preferred_element_type=jnp.float32
                )
                hidden = position >= side_by_side(lengths, half // HEAD_WIDTH)
                score = jnp.where(hidden, HIDDEN, score)
                for i in range(0, half, HEAD_WIDTH):
                    top = jnp.maximum(top, score[:, i : i + HEAD_WIDTH])
                scores.append(score)
            peak = jnp.broadcast_to(jnp.max(top, axis=-1, keepdims=True), own.shape)
            acc = start * side_by_side(jnp.exp2((own - peak) * EXPONENT), 2)
            for score, (ref, _, rows, _) in zip(scores, blocks):
                weights = jnp.exp2((score - side_by_side(peak, half // HEAD_WIDTH)) * EXPONENT)
                values = ref[rows, :]
                acc = acc + jnp.dot(
                    weights.astype(jnp.bfloat16),
                    jnp.concatenate([values, jnp.ones_like(values)], axis=1),
                    preferred_element_type=jnp.float32,
                )
            context = (acc[:, :HEAD_WIDTH] / acc[:, HEAD_WIDTH:]).astype(jnp.bfloat16)
            for i in range(group):
                column = (first + i) * HEAD_WIDTH
                head = context[i * tokens : (i + 1) * tokens, :]
                out_ref[:, column : column + HEAD_WIDTH] = head
                theirs_ref[:, column : column + HEAD_WIDTH] = half_of(head, 1 - tp)

    for copy in copies:
        copy.wait()


def attend(heads, far_masks, query_rows, lengths, own, pieces, weight):
    tokens = query_rows.shape[0]
    block_rows = own.shape[0] // 2
    work = tokens * heads * block_rows * 2 * (1 + len(far_masks))
    depth = heads * HEAD_WIDTH
    return pl.pallas_call(
        functools.partial(attend_kernel, heads, far_masks, block_rows),
        out_shape=[
            jax.ShapeDtypeStruct((tokens, depth), jnp.bfloat16),
            jax.ShapeDtypeStruct((tokens // 2, depth), jnp.bfloat16),
            jax.ShapeDtypeStruct((depth, weight.shape[1]), weight.dtype),
        ],
        in_specs=[vmem()] * (3 + len(pieces)) + [hbm()],
        out_specs=[vmem()] * 3,
        scratch_shapes=[pltpu.SemaphoreType.DMA((FETCHES,))],
        compiler_params=params(ATTEND_BYTES),
        cost_estimate=cost(6 * work * HEAD_WIDTH, 2**20, work),
        name="attend",
    )(query_rows, lengths, own, *pieces, weight)


def load_kernel(masks, weight_ref, x_ref, first_ref, acc_ref, *refs):
    tile_refs, sems = refs[:-1], refs[-1]
    tp = lax.axis_index("tp")
    copies = tile_copies(masks, weight_ref, tile_refs, sems)
    for copy in copies:
        copy.start()

    def finish(at, part):
        acc_ref[:, at] = part

    @pl.when(tp >= 0)
    def compute():
        multiply(x_ref, first_ref, finish)

    for copy in copies:
        copy.wait()


def load(weight, context, tile, masks):
    tokens, (depth, columns) = context.shape[0], tile.shape
    return pl.pallas_call(
        functools.partial(load_kernel, masks),
        out_shape=[
            jax.ShapeDtypeStruct((tokens, columns), jnp.float32),
        ]
        + [jax.ShapeDtypeStruct(tile.shape, tile.dtype)] * len(masks),
        in_specs=[hbm(), vmem(), vmem()],
        out_specs=[vmem()] * (1 + len(masks)),
        scratch_shapes=[pltpu.SemaphoreType.DMA((FETCHES * len(masks),))],
        compiler_params=params(LOAD_BYTES),
        cost_estimate=cost(2 * tokens * depth * columns, len(masks) * depth * columns * 2),
        name="load",
    )(weight, context, tile)


def project_kernel(side, pass_on, x_ref, w_ref, acc_ref, *refs):
    tp = lax.axis_index("tp")
    out_ref = refs[-1]
    if pass_on:
        out_ref = refs[1]
        refs[2][...] = half_of(refs[0][...], tp)

    def finish(at, part):
        acc = acc_ref[:, at]
        if side is not None:
            acc = half_of(acc, tp if side == 0 else 1 - tp)
        out_ref[:, at] = (part + acc).astype(out_ref.dtype)

    multiply(x_ref, w_ref, finish)


def project(context, tile, acc, side=None, dtype=jnp.float32, pass_on=None):
    tokens, columns = context.shape[0], tile.shape[1]
    shapes = [jax.ShapeDtypeStruct((tokens, columns), dtype)]
    operands = [context, tile, acc]
    if pass_on is not None:
        operands.append(pass_on)
        shapes.append(jax.ShapeDtypeStruct((tokens // 2, pass_on.shape[1]), pass_on.dtype))
    return pl.pallas_call(
        functools.partial(project_kernel, side, pass_on is not None),
        out_shape=shapes,
        in_specs=[vmem()] * len(operands),
        out_specs=[vmem()] * len(shapes),
        compiler_params=params(PROJECT_BYTES),
        cost_estimate=cost(2 * context.size * columns, 2 * tile.size),
        name="project",
    )(*operands)


def add_kernel(*refs):
    out_ref = refs[-1]
    count = (len(refs) - 1) // 2
    start = 0
    for keep_ref, got_ref in zip(refs[:count], refs[count:-1]):
        width = keep_ref.shape[1]
        total = keep_ref[...] + got_ref[...].astype(jnp.float32)
        out_ref[0, :, start : start + width] = total.astype(out_ref.dtype)
        start += width


def add(keeps, gots):
    shape = (1, keeps[0].shape[0], sum(a.shape[1] for a in keeps))
    return pl.pallas_call(
        add_kernel,
        out_shape=jax.ShapeDtypeStruct(shape, jnp.bfloat16),
        in_specs=[vmem()] * (2 * len(keeps)),
        out_specs=vmem(),
        compiler_params=params(PROJECT_BYTES),
        cost_estimate=cost(0, 2**19),
        name="add",
    )(*keeps, *gots)


def shards_by_head(
    queries, fresh_key_rows, fresh_value_rows, visible, prefix_keys, cached_value_rows, out_weight
):
    heads = queries.shape[2] // fresh_key_rows.shape[2]
    masks = list(range(1, lax.axis_size("seq")))
    rows = [queries[0], fresh_key_rows[0], fresh_value_rows[0]]
    seq, rep = lax.axis_index("seq"), lax.axis_index("rep")
    half_rows = prefix_keys.shape[0] // 2

    def cut(first, count, head):
        return jnp.concatenate(
            [
                lax.dynamic_slice(table, (first, head * HEAD_WIDTH), (count, HEAD_WIDTH))
                for table in (prefix_keys, cached_value_rows)
            ]
        )

    far_masks = masks[1::2]
    far = [swap_by_core(cut(0, 2 * half_rows, seq ^ (m + rep)), m) for m in far_masks]
    near = swap(cut(rep * half_rows, half_rows, seq ^ 1), "seq", 1)
    own = cut(0, 2 * half_rows, seq)
    query_rows = lax.all_to_all(
        pack_queries(rows, 1 + len(masks)), ("seq", "tp"), split_axis=0, concat_axis=0, tiled=True
    )
    lengths = spread_lengths(visible)
    far = settle(far, SETTLE_FIRST)
    pieces = [piece for mine in (*far, near) for piece in (mine, swap(mine, "rep", 1))]
    context, theirs, tile = attend(heads, far_masks, query_rows, lengths, own, pieces, out_weight)

    order = masks[-1:] + masks[:-1]
    chunks = [swap(context, "seq", mask) for mask in order[:-1]]
    first = swap(theirs, "seq", order[-1])
    acc, *tiles = load(out_weight, context, tile, order)
    for i, (chunk, tile) in enumerate(zip(chunks, tiles)):
        acc, *ours = project(chunk, tile, acc, pass_on=context if i == 0 else None)
        if i == 0:
            (second,) = settle([swap(ours[0], "seq", order[-1])], SETTLE_LAST)
    (sums,) = project(first, tiles[-1], acc, 1, jnp.bfloat16)
    got = swap(sums, "tp", 1)
    (kept,) = project(second, tiles[-1], acc, 0)
    return add([kept], [got])


def solution(mesh):
    in_specs = (
        P("rep", ("groups", "seq", "tp"), None),
        P("rep", ("groups", "seq", "tp"), None),
        P("rep", ("groups", "seq", "tp"), None),
        P("rep", "groups"),
        P(("groups", "seq"), "tp"),
        P(("groups", "seq"), "tp"),
        P("tp", "seq"),
    )
    out_specs = P("rep", ("groups", "tp"), "seq")
    sizes = mesh.shape
    seq_count = sizes["seq"]

    def shards(*args):
        local_heads = args[4].shape[1] // HEAD_WIDTH
        by_head = (
            local_heads == seq_count
            and seq_count in (4, 8)
            and sizes["tp"] == 2
            and sizes["rep"] == 2
            and args[0].shape[2] // args[1].shape[2] % 4 == 0
        )
        return (shards_by_head if by_head else shards_any)(*args)

    return jax.shard_map(shards, mesh=mesh, in_specs=in_specs, out_specs=out_specs, check_vma=False)
```

```python
import functools
import math

import jax
import jax.numpy as jnp
from jax import lax
from jax.experimental import pallas as pl
from jax.experimental.pallas import tpu as pltpu
from jax.sharding import PartitionSpec as P

HEAD_WIDTH = 128
HIDDEN = -1e30
SCALE = 1.0 / math.sqrt(HEAD_WIDTH)


def block_partial(query_heads, lengths, key_rows, value_rows, offset):
    kv_heads = query_heads.shape[1]
    row_count = key_rows.shape[0]
    step_rows = math.gcd(row_count, 512)
    stat_shape = query_heads.shape[:3]

    def masked_scores(turn_index):
        first_row = turn_index * step_rows
        key_block = lax.dynamic_slice_in_dim(key_rows, first_row, step_rows, 0)
        key_block = key_block.reshape(step_rows, kv_heads, HEAD_WIDTH)
        scores = (
            jnp.einsum("tkgd,pkd->tkgp", query_heads, key_block, preferred_element_type=jnp.float32)
            * SCALE
        )
        position = offset + first_row + jnp.arange(step_rows, dtype=jnp.int32)
        visible_mask = (position[None, :] < lengths[:, None])[:, None, None, :]
        return (scores, visible_mask, first_row)

    def peak_step(turn_index, peak_now):
        scores, visible_mask, _ = masked_scores(turn_index)
        return jnp.maximum(peak_now, jnp.max(jnp.where(visible_mask, scores, -jnp.inf), axis=-1))

    block_peak = lax.fori_loop(
        0, row_count // step_rows, peak_step, jnp.full(stat_shape, -jnp.inf, jnp.float32)
    )
    anchor = jnp.where(jnp.isinf(block_peak), 0.0, block_peak)

    def weight_step(turn_index, state_now):
        sum_now, acc_now = state_now
        scores, visible_mask, first_row = masked_scores(turn_index)
        value_block = lax.dynamic_slice_in_dim(value_rows, first_row, step_rows, 0)
        value_block = value_block.reshape(step_rows, kv_heads, HEAD_WIDTH)
        weights = jnp.where(visible_mask, jnp.exp(scores - anchor[..., None]), 0.0)
        sum_now = sum_now + jnp.sum(weights, axis=-1)
        acc_now = acc_now + jnp.einsum(
            "tkgp,pkd->tkgd",
            weights.astype(jnp.bfloat16),
            value_block,
            preferred_element_type=jnp.float32,
        )
        return (sum_now, acc_now)

    block_sum, block_acc = lax.fori_loop(
        0,
        row_count // step_rows,
        weight_step,
        (jnp.zeros(stat_shape, jnp.float32), jnp.zeros(query_heads.shape, jnp.float32)),
    )
    return (block_peak, block_sum, block_acc)


def shards_any(
    queries, fresh_key_rows, fresh_value_rows, visible, prefix_keys, cached_value_rows, out_weight
):
    query_rows, self_key_rows, own_values = (
        lax.all_to_all(queries[0], "tp", split_axis=1, concat_axis=0, tiled=True),
        lax.all_to_all(fresh_key_rows[0], "tp", split_axis=1, concat_axis=0, tiled=True),
        lax.all_to_all(fresh_value_rows[0], "tp", split_axis=1, concat_axis=0, tiled=True),
    )
    kv_heads = prefix_keys.shape[1] // HEAD_WIDTH
    tok_rows = query_rows.shape[0]
    block_rows = prefix_keys.shape[0]
    per_group = query_rows.shape[1] // (kv_heads * HEAD_WIDTH)
    seq_index = lax.axis_index("seq")
    query_heads = query_rows.reshape(tok_rows, kv_heads, per_group, HEAD_WIDTH)
    self_key_rows = self_key_rows.reshape(tok_rows, kv_heads, HEAD_WIDTH)
    own_vectors = own_values.reshape(tok_rows, kv_heads, 1, HEAD_WIDTH).astype(jnp.float32)
    self_score_row = (
        jnp.einsum(
            "tkgd,tkd->tkg", query_heads, self_key_rows, preferred_element_type=jnp.float32
        )
        * SCALE
    )
    seq_count = lax.axis_size("seq")
    everyone = lax.all_gather(query_rows, "seq", axis=0, tiled=True)
    blocks = everyone.reshape(seq_count, tok_rows, kv_heads, per_group, HEAD_WIDTH)
    all_lengths = visible[0].reshape(seq_count, tok_rows)
    prefix_start = seq_index * block_rows

    def partial_block(item_pair):
        return block_partial(
            item_pair[0], item_pair[1], prefix_keys, cached_value_rows, prefix_start
        )

    part_max, part_sum, part_acc = lax.map(partial_block, (blocks, all_lengths))
    part_max, part_sum, part_acc = (
        lax.all_to_all(part_max, "seq", split_axis=0, concat_axis=0, tiled=True),
        lax.all_to_all(part_sum, "seq", split_axis=0, concat_axis=0, tiled=True),
        lax.all_to_all(part_acc, "seq", split_axis=0, concat_axis=0, tiled=True),
    )
    run_max = jnp.max(part_max, axis=0)
    anchor = jnp.where(jnp.isinf(run_max), 0.0, run_max)
    part_factor = jnp.exp(part_max - anchor[None])
    run_sum = jnp.sum(part_sum * part_factor, axis=0)
    run_acc = jnp.sum(part_acc * part_factor[..., None], axis=0)
    row_peak = jnp.maximum(run_max, self_score_row)
    fade = jnp.exp(run_max - row_peak)
    own_weight = jnp.exp(self_score_row - row_peak)
    own_rounded = lax.optimization_barrier(own_weight.astype(jnp.bfloat16)).astype(jnp.float32)
    total_sum = run_sum * fade + own_weight
    total_acc = run_acc * fade[..., None] + own_rounded[..., None] * own_vectors
    context = (
        (total_acc / total_sum[..., None])
        .astype(jnp.bfloat16)
        .reshape(tok_rows, kv_heads * per_group * HEAD_WIDTH)
    )
    partial_out = jnp.dot(
        lax.all_gather(context, "seq", axis=0, tiled=True),
        out_weight,
        preferred_element_type=jnp.float32,
    )
    summed = lax.psum_scatter(partial_out, "tp", scatter_dimension=0, tiled=True)
    return summed.astype(jnp.bfloat16)[None]


EXPONENT = SCALE * math.log2(math.e)
VMEM_BYTES = 20 * 2**20
UNIT_ROWS = 256
FETCHES = 1
SETTLE_FIRST = 10**11
SETTLE_LAST = 10**10
PACK_BYTES = 56 * 2**20
ATTEND_BYTES = 40 * 2**20
LOAD_BYTES = 30 * 2**20
PROJECT_BYTES = 16 * 2**20


def swap(array, axis, mask):
    return lax.ppermute(array, axis, [(i, i ^ mask) for i in range(lax.axis_size(axis))])


def swap_by_core(array, mask):
    count = 2 * lax.axis_size("seq")
    pairs = [(i, i ^ (2 * (mask + i % 2))) for i in range(count)]
    return lax.ppermute(array, ("seq", "rep"), pairs)


def tile_at(index, width):
    return pl.ds(pl.multiple_of(index * width, width), width)


def side_by_side(array, times):
    return jnp.concatenate([array] * times, axis=1)


def vmem():
    return pl.BlockSpec(memory_space=pltpu.VMEM)


def hbm():
    return pl.BlockSpec(memory_space=pltpu.HBM)


def params(limit=VMEM_BYTES):
    return pltpu.CompilerParams(vmem_limit_bytes=limit)


def cost(flops, bytes_accessed, transcendentals=0):
    return pl.CostEstimate(
        flops=flops, bytes_accessed=bytes_accessed, transcendentals=transcendentals
    )


def pack_queries_kernel(seq_count, *refs):
    row_refs, out_ref, held_refs, sems = refs[:3], refs[3], refs[4:7], refs[7]
    copies = [
        pltpu.make_async_copy(ref, held, sems.at[i])
        for i, (ref, held) in enumerate(zip(row_refs, held_refs))
    ]
    for copy in copies:
        copy.start()
    for copy in copies:
        copy.wait()
    tokens = row_refs[0].shape[0]
    count = out_ref.shape[0] // tokens
    for owner in range(count):
        head = owner % 2 * seq_count + owner // 2
        to = 0
        for ref in held_refs:
            part = ref.shape[1] // count
            out_ref[owner * tokens : (owner + 1) * tokens, to : to + part] = ref[
                :, head * part : (head + 1) * part
            ]
            to += part


def pack_queries(rows, seq_count):
    count = 2 * seq_count
    shape = (rows[0].shape[0] * count, sum(a.shape[1] for a in rows) // count)
    return pl.pallas_call(
        functools.partial(pack_queries_kernel, seq_count),
        out_shape=jax.ShapeDtypeStruct(shape, jnp.bfloat16),
        in_specs=[hbm()] * 3,
        out_specs=vmem(),
        scratch_shapes=[pltpu.VMEM(a.shape, a.dtype) for a in rows]
        + [pltpu.SemaphoreType.DMA((3,))],
        compiler_params=params(PACK_BYTES),
        cost_estimate=cost(0, 2**19),
        name="pack_queries",
    )(*rows)


def settle_kernel(*refs):
    del refs


def settle(arrays, declared):
    count = len(arrays)
    return pl.pallas_call(
        settle_kernel,
        out_shape=[jax.ShapeDtypeStruct(a.shape, a.dtype) for a in arrays],
        in_specs=[vmem()] * count,
        out_specs=[vmem()] * count,
        input_output_aliases={i: i for i in range(count)},
        compiler_params=params(2**20),
        cost_estimate=cost(declared, 2**20),
        name="settle",
    )(*arrays)


def lengths_kernel(visible_ref, out_ref):
    tokens = out_ref.shape[0]
    diagonal = lax.broadcasted_iota(jnp.int32, (tokens, tokens), 0) == lax.broadcasted_iota(
        jnp.int32, (tokens, tokens), 1
    )
    lengths = jnp.sum(jnp.where(diagonal, visible_ref[...], 0), axis=-1, keepdims=True)
    out_ref[...] = jnp.broadcast_to(lengths, out_ref.shape)


def spread_lengths(visible):
    return pl.pallas_call(
        lengths_kernel,
        out_shape=jax.ShapeDtypeStruct((visible.shape[1], HEAD_WIDTH), jnp.int32),
        in_specs=[vmem()],
        out_specs=vmem(),
        compiler_params=params(),
        cost_estimate=cost(0, 2**15),
        name="spread_lengths",
    )(visible)


def half_of(rows, side):
    half = rows.shape[0] // 2
    return jnp.where(side == 0, rows[:half, :], rows[half:, :])


def tile_copies(masks, weight_ref, tile_refs, sems):
    depth = tile_refs[0].shape[0]
    rows = depth // FETCHES
    seq = lax.axis_index("seq")
    return [
        pltpu.make_async_copy(
            weight_ref.at[pl.ds(pl.multiple_of((seq ^ mask) * depth + n * rows, rows), rows), :],
            tile_ref.at[pl.ds(n * rows, rows), :],
            sems.at[i * FETCHES + n],
        )
        for i, (mask, tile_ref) in enumerate(zip(masks, tile_refs))
        for n in range(FETCHES)
    ]


def multiply(x_ref, w_ref, finish):
    columns = w_ref.shape[1]
    width = math.gcd(columns, 2048)
    for start in range(0, columns, width):
        at = slice(start, start + width)
        finish(at, jnp.dot(x_ref[...], w_ref[:, at], preferred_element_type=jnp.float32))


def attend_kernel(heads, far_masks, block_rows, rows_ref, lengths_ref, own_ref, *refs):
    pieces = 2 * len(far_masks) + 2
    piece_refs, weight_ref = refs[:pieces], refs[pieces]
    out_ref, theirs_ref, tile_ref, sems = refs[pieces + 1 :]
    seq, tp, rep = lax.axis_index("seq"), lax.axis_index("tp"), lax.axis_index("rep")
    copies = tile_copies([0], weight_ref, [tile_ref], sems)
    for copy in copies:
        copy.start()
    @pl.when(tp >= 0)
    def compute():
        tokens = out_ref.shape[0]
        half = block_rows // 2
        lane = lax.broadcasted_iota(jnp.int32, (1, half), 1)
        blocks = []

        def whole(ref, mask):
            for first in (0, half):
                rows, values = slice(first, first + half), slice(block_rows + first, block_rows + first + half)
                blocks.append((ref, rows, values, (seq ^ mask) * block_rows + first + lane))

        whole(own_ref, 0)
        for i, ref in enumerate(piece_refs[:-2]):
            core = rep if i % 2 == 0 else 1 - rep
            whole(ref, far_masks[i // 2] + core)
        for ref, core in zip(piece_refs[-2:], (rep, 1 - rep)):
            first = (seq ^ 1) * block_rows + core * half
            blocks.append((ref, slice(0, half), slice(half, 2 * half), first + lane))
        width = heads * HEAD_WIDTH
        fresh_key = rows_ref[:, width : width + HEAD_WIDTH].astype(jnp.float32)
        fresh_value = rows_ref[:, width + HEAD_WIDTH :].astype(jnp.float32)
        group = max(1, UNIT_ROWS // tokens)
        lengths = jnp.concatenate([lengths_ref[...]] * group, axis=0)
        fresh_key = jnp.concatenate([fresh_key] * group, axis=0)
        start = jnp.concatenate([fresh_value, jnp.ones_like(fresh_value)], axis=1)
        start = jnp.concatenate([start] * group, axis=0)
        for first in range(0, heads, group):
            query = jnp.concatenate(
                [
                    rows_ref[:, h * HEAD_WIDTH : (h + 1) * HEAD_WIDTH]
                    for h in range(first, first + group)
                ],
                axis=0,
            )
            own = jnp.sum(query.astype(jnp.float32) * fresh_key, axis=-1, keepdims=True)
            own = jnp.broadcast_to(own, (group * tokens, HEAD_WIDTH))
            top, scores = own, []
            for ref, rows, _, position in blocks:
                score = lax.dot_general(
                    query, ref[rows, :], (((1,), (1,)), ((), ())), preferred_element_type=jnp.float32
                )
                hidden = position >= side_by_side(lengths, half // HEAD_WIDTH)
                score = jnp.where(hidden, HIDDEN, score)
                for i in range(0, half, HEAD_WIDTH):
                    top = jnp.maximum(top, score[:, i : i + HEAD_WIDTH])
                scores.append(score)
            peak = jnp.broadcast_to(jnp.max(top, axis=-1, keepdims=True), own.shape)
            acc = start * side_by_side(jnp.exp2((own - peak) * EXPONENT), 2)
            for score, (ref, _, rows, _) in zip(scores, blocks):
                weights = jnp.exp2((score - side_by_side(peak, half // HEAD_WIDTH)) * EXPONENT)
                values = ref[rows, :]
                acc = acc + jnp.dot(
                    weights.astype(jnp.bfloat16),
                    jnp.concatenate([values, jnp.ones_like(values)], axis=1),
                    preferred_element_type=jnp.float32,
                )
            context = (acc[:, :HEAD_WIDTH] / acc[:, HEAD_WIDTH:]).astype(jnp.bfloat16)
            for i in range(group):
                column = (first + i) * HEAD_WIDTH
                head = context[i * tokens : (i + 1) * tokens, :]
                out_ref[:, column : column + HEAD_WIDTH] = head
                theirs_ref[:, column : column + HEAD_WIDTH] = half_of(head, 1 - tp)

    for copy in copies:
        copy.wait()


def attend(heads, far_masks, query_rows, lengths, own, pieces, weight):
    tokens = query_rows.shape[0]
    block_rows = own.shape[0] // 2
    work = tokens * heads * block_rows * 2 * (1 + len(far_masks))
    depth = heads * HEAD_WIDTH
    return pl.pallas_call(
        functools.partial(attend_kernel, heads, far_masks, block_rows),
        out_shape=[
            jax.ShapeDtypeStruct((tokens, depth), jnp.bfloat16),
            jax.ShapeDtypeStruct((tokens // 2, depth), jnp.bfloat16),
            jax.ShapeDtypeStruct((depth, weight.shape[1]), weight.dtype),
        ],
        in_specs=[vmem()] * (3 + len(pieces)) + [hbm()],
        out_specs=[vmem()] * 3,
        scratch_shapes=[pltpu.SemaphoreType.DMA((FETCHES,))],
        compiler_params=params(ATTEND_BYTES),
        cost_estimate=cost(6 * work * HEAD_WIDTH, 2**20, work),
        name="attend",
    )(query_rows, lengths, own, *pieces, weight)


def load_kernel(masks, weight_ref, x_ref, first_ref, acc_ref, *refs):
    tile_refs, sems = refs[:-1], refs[-1]
    tp = lax.axis_index("tp")
    copies = tile_copies(masks, weight_ref, tile_refs, sems)
    for copy in copies:
        copy.start()

    def finish(at, part):
        acc_ref[:, at] = part

    @pl.when(tp >= 0)
    def compute():
        multiply(x_ref, first_ref, finish)

    for copy in copies:
        copy.wait()


def load(weight, context, tile, masks):
    tokens, (depth, columns) = context.shape[0], tile.shape
    return pl.pallas_call(
        functools.partial(load_kernel, masks),
        out_shape=[
            jax.ShapeDtypeStruct((tokens, columns), jnp.float32),
        ]
        + [jax.ShapeDtypeStruct(tile.shape, tile.dtype)] * len(masks),
        in_specs=[hbm(), vmem(), vmem()],
        out_specs=[vmem()] * (1 + len(masks)),
        scratch_shapes=[pltpu.SemaphoreType.DMA((FETCHES * len(masks),))],
        compiler_params=params(LOAD_BYTES),
        cost_estimate=cost(2 * tokens * depth * columns, len(masks) * depth * columns * 2),
        name="load",
    )(weight, context, tile)


def project_kernel(side, pass_on, x_ref, w_ref, acc_ref, *refs):
    tp = lax.axis_index("tp")
    out_ref = refs[-1]
    if pass_on:
        out_ref = refs[1]
        refs[2][...] = half_of(refs[0][...], tp)

    def finish(at, part):
        acc = acc_ref[:, at]
        if side is not None:
            acc = half_of(acc, tp if side == 0 else 1 - tp)
        out_ref[:, at] = (part + acc).astype(out_ref.dtype)

    multiply(x_ref, w_ref, finish)


def project(context, tile, acc, side=None, dtype=jnp.float32, pass_on=None):
    tokens, columns = context.shape[0], tile.shape[1]
    shapes = [jax.ShapeDtypeStruct((tokens, columns), dtype)]
    operands = [context, tile, acc]
    if pass_on is not None:
        operands.append(pass_on)
        shapes.append(jax.ShapeDtypeStruct((tokens // 2, pass_on.shape[1]), pass_on.dtype))
    return pl.pallas_call(
        functools.partial(project_kernel, side, pass_on is not None),
        out_shape=shapes,
        in_specs=[vmem()] * len(operands),
        out_specs=[vmem()] * len(shapes),
        compiler_params=params(PROJECT_BYTES),
        cost_estimate=cost(2 * context.size * columns, 2 * tile.size),
        name="project",
    )(*operands)


def add_kernel(*refs):
    out_ref = refs[-1]
    count = (len(refs) - 1) // 2
    start = 0
    for keep_ref, got_ref in zip(refs[:count], refs[count:-1]):
        width = keep_ref.shape[1]
        total = keep_ref[...] + got_ref[...].astype(jnp.float32)
        out_ref[0, :, start : start + width] = total.astype(out_ref.dtype)
        start += width


def add(keeps, gots):
    shape = (1, keeps[0].shape[0], sum(a.shape[1] for a in keeps))
    return pl.pallas_call(
        add_kernel,
        out_shape=jax.ShapeDtypeStruct(shape, jnp.bfloat16),
        in_specs=[vmem()] * (2 * len(keeps)),
        out_specs=vmem(),
        compiler_params=params(PROJECT_BYTES),
        cost_estimate=cost(0, 2**19),
        name="add",
    )(*keeps, *gots)


def shards_by_head(
    queries, fresh_key_rows, fresh_value_rows, visible, prefix_keys, cached_value_rows, out_weight
):
    heads = queries.shape[2] // fresh_key_rows.shape[2]
    masks = list(range(1, lax.axis_size("seq")))
    rows = [queries[0], fresh_key_rows[0], fresh_value_rows[0]]
    seq, rep = lax.axis_index("seq"), lax.axis_index("rep")
    half_rows = prefix_keys.shape[0] // 2

    def cut(first, count, head):
        return jnp.concatenate(
            [
                lax.dynamic_slice(table, (first, head * HEAD_WIDTH), (count, HEAD_WIDTH))
                for table in (prefix_keys, cached_value_rows)
            ]
        )

    far_masks = masks[1::2]
    far = [swap_by_core(cut(0, 2 * half_rows, seq ^ (m + rep)), m) for m in far_masks]
    near = swap(cut(rep * half_rows, half_rows, seq ^ 1), "seq", 1)
    own = cut(0, 2 * half_rows, seq)
    query_rows = lax.all_to_all(
        pack_queries(rows, 1 + len(masks)), ("seq", "tp"), split_axis=0, concat_axis=0, tiled=True
    )
    lengths = spread_lengths(visible)
    far = settle(far, SETTLE_FIRST)
    pieces = [piece for mine in (*far, near) for piece in (mine, swap(mine, "rep", 1))]
    context, theirs, tile = attend(heads, far_masks, query_rows, lengths, own, pieces, out_weight)

    order = masks[-1:] + masks[:-1]
    chunks = [swap(context, "seq", mask) for mask in order[:-1]]
    first = swap(theirs, "seq", order[-1])
    acc, *tiles = load(out_weight, context, tile, order)
    for i, (chunk, tile) in enumerate(zip(chunks, tiles)):
        acc, *ours = project(chunk, tile, acc, pass_on=context if i == 0 else None)
        if i == 0:
            (second,) = settle([swap(ours[0], "seq", order[-1])], SETTLE_LAST)
    (sums,) = project(first, tiles[-1], acc, 1, jnp.bfloat16)
    got = swap(sums, "tp", 1)
    (kept,) = project(second, tiles[-1], acc, 0)
    return add([kept], [got])


def solution(mesh):
    in_specs = (
        P("rep", ("groups", "seq", "tp"), None),
        P("rep", ("groups", "seq", "tp"), None),
        P("rep", ("groups", "seq", "tp"), None),
        P("rep", "groups"),
        P(("groups", "seq"), "tp"),
        P(("groups", "seq"), "tp"),
        P("tp", "seq"),
    )
    out_specs = P("rep", ("groups", "tp"), "seq")
    sizes = mesh.shape
    seq_count = sizes["seq"]

    def shards(*args):
        local_heads = args[4].shape[1] // HEAD_WIDTH
        by_head = (
            local_heads == seq_count
            and seq_count in (4, 8)
            and sizes["tp"] == 2
            and sizes["rep"] == 2
            and args[0].shape[2] // args[1].shape[2] % 4 == 0
        )
        return (shards_by_head if by_head else shards_any)(*args)

    return jax.shard_map(shards, mesh=mesh, in_specs=in_specs, out_specs=out_specs, check_vma=False)
```

```python
import functools
import math

import jax
import jax.numpy as jnp
from jax import lax
from jax.experimental import pallas as pl
from jax.experimental.pallas import tpu as pltpu
from jax.sharding import PartitionSpec as P

HEAD_WIDTH = 128
HIDDEN = -1e30
SCALE = 1.0 / math.sqrt(HEAD_WIDTH)


def block_partial(query_heads, lengths, key_rows, value_rows, offset):
    kv_heads = query_heads.shape[1]
    row_count = key_rows.shape[0]
    step_rows = math.gcd(row_count, 512)
    stat_shape = query_heads.shape[:3]

    def masked_scores(turn_index):
        first_row = turn_index * step_rows
        key_block = lax.dynamic_slice_in_dim(key_rows, first_row, step_rows, 0)
        key_block = key_block.reshape(step_rows, kv_heads, HEAD_WIDTH)
        scores = (
            jnp.einsum("tkgd,pkd->tkgp", query_heads, key_block, preferred_element_type=jnp.float32)
            * SCALE
        )
        position = offset + first_row + jnp.arange(step_rows, dtype=jnp.int32)
        visible_mask = (position[None, :] < lengths[:, None])[:, None, None, :]
        return (scores, visible_mask, first_row)

    def peak_step(turn_index, peak_now):
        scores, visible_mask, _ = masked_scores(turn_index)
        return jnp.maximum(peak_now, jnp.max(jnp.where(visible_mask, scores, -jnp.inf), axis=-1))

    block_peak = lax.fori_loop(
        0, row_count // step_rows, peak_step, jnp.full(stat_shape, -jnp.inf, jnp.float32)
    )
    anchor = jnp.where(jnp.isinf(block_peak), 0.0, block_peak)

    def weight_step(turn_index, state_now):
        sum_now, acc_now = state_now
        scores, visible_mask, first_row = masked_scores(turn_index)
        value_block = lax.dynamic_slice_in_dim(value_rows, first_row, step_rows, 0)
        value_block = value_block.reshape(step_rows, kv_heads, HEAD_WIDTH)
        weights = jnp.where(visible_mask, jnp.exp(scores - anchor[..., None]), 0.0)
        sum_now = sum_now + jnp.sum(weights, axis=-1)
        acc_now = acc_now + jnp.einsum(
            "tkgp,pkd->tkgd",
            weights.astype(jnp.bfloat16),
            value_block,
            preferred_element_type=jnp.float32,
        )
        return (sum_now, acc_now)

    block_sum, block_acc = lax.fori_loop(
        0,
        row_count // step_rows,
        weight_step,
        (jnp.zeros(stat_shape, jnp.float32), jnp.zeros(query_heads.shape, jnp.float32)),
    )
    return (block_peak, block_sum, block_acc)


def shards_any(
    queries, fresh_key_rows, fresh_value_rows, visible, prefix_keys, cached_value_rows, out_weight
):
    query_rows, self_key_rows, own_values = (
        lax.all_to_all(queries[0], "tp", split_axis=1, concat_axis=0, tiled=True),
        lax.all_to_all(fresh_key_rows[0], "tp", split_axis=1, concat_axis=0, tiled=True),
        lax.all_to_all(fresh_value_rows[0], "tp", split_axis=1, concat_axis=0, tiled=True),
    )
    kv_heads = prefix_keys.shape[1] // HEAD_WIDTH
    tok_rows = query_rows.shape[0]
    block_rows = prefix_keys.shape[0]
    per_group = query_rows.shape[1] // (kv_heads * HEAD_WIDTH)
    seq_index = lax.axis_index("seq")
    query_heads = query_rows.reshape(tok_rows, kv_heads, per_group, HEAD_WIDTH)
    self_key_rows = self_key_rows.reshape(tok_rows, kv_heads, HEAD_WIDTH)
    own_vectors = own_values.reshape(tok_rows, kv_heads, 1, HEAD_WIDTH).astype(jnp.float32)
    self_score_row = (
        jnp.einsum(
            "tkgd,tkd->tkg", query_heads, self_key_rows, preferred_element_type=jnp.float32
        )
        * SCALE
    )
    seq_count = lax.axis_size("seq")
    everyone = lax.all_gather(query_rows, "seq", axis=0, tiled=True)
    blocks = everyone.reshape(seq_count, tok_rows, kv_heads, per_group, HEAD_WIDTH)
    all_lengths = visible[0].reshape(seq_count, tok_rows)
    prefix_start = seq_index * block_rows

    def partial_block(item_pair):
        return block_partial(
            item_pair[0], item_pair[1], prefix_keys, cached_value_rows, prefix_start
        )

    part_max, part_sum, part_acc = lax.map(partial_block, (blocks, all_lengths))
    part_max, part_sum, part_acc = (
        lax.all_to_all(part_max, "seq", split_axis=0, concat_axis=0, tiled=True),
        lax.all_to_all(part_sum, "seq", split_axis=0, concat_axis=0, tiled=True),
        lax.all_to_all(part_acc, "seq", split_axis=0, concat_axis=0, tiled=True),
    )
    run_max = jnp.max(part_max, axis=0)
    anchor = jnp.where(jnp.isinf(run_max), 0.0, run_max)
    part_factor = jnp.exp(part_max - anchor[None])
    run_sum = jnp.sum(part_sum * part_factor, axis=0)
    run_acc = jnp.sum(part_acc * part_factor[..., None], axis=0)
    row_peak = jnp.maximum(run_max, self_score_row)
    fade = jnp.exp(run_max - row_peak)
    own_weight = jnp.exp(self_score_row - row_peak)
    own_rounded = lax.optimization_barrier(own_weight.astype(jnp.bfloat16)).astype(jnp.float32)
    total_sum = run_sum * fade + own_weight
    total_acc = run_acc * fade[..., None] + own_rounded[..., None] * own_vectors
    context = (
        (total_acc / total_sum[..., None])
        .astype(jnp.bfloat16)
        .reshape(tok_rows, kv_heads * per_group * HEAD_WIDTH)
    )
    partial_out = jnp.dot(
        lax.all_gather(context, "seq", axis=0, tiled=True),
        out_weight,
        preferred_element_type=jnp.float32,
    )
    summed = lax.psum_scatter(partial_out, "tp", scatter_dimension=0, tiled=True)
    return summed.astype(jnp.bfloat16)[None]


EXPONENT = SCALE * math.log2(math.e)
VMEM_BYTES = 20 * 2**20
UNIT_ROWS = 256
FETCHES = 2
SETTLE_FIRST = 10**11
SETTLE_LAST = 10**10
PACK_BYTES = 56 * 2**20
ATTEND_BYTES = 40 * 2**20
LOAD_BYTES = 30 * 2**20
PROJECT_BYTES = 16 * 2**20


def swap(array, axis, mask):
    return lax.ppermute(array, axis, [(i, i ^ mask) for i in range(lax.axis_size(axis))])


def swap_by_core(array, mask):
    count = 2 * lax.axis_size("seq")
    pairs = [(i, i ^ (2 * (mask + i % 2))) for i in range(count)]
    return lax.ppermute(array, ("seq", "rep"), pairs)


def tile_at(index, width):
    return pl.ds(pl.multiple_of(index * width, width), width)


def side_by_side(array, times):
    return jnp.concatenate([array] * times, axis=1)


def vmem():
    return pl.BlockSpec(memory_space=pltpu.VMEM)


def hbm():
    return pl.BlockSpec(memory_space=pltpu.HBM)


def params(limit=VMEM_BYTES):
    return pltpu.CompilerParams(vmem_limit_bytes=limit)


def cost(flops, bytes_accessed, transcendentals=0):
    return pl.CostEstimate(
        flops=flops, bytes_accessed=bytes_accessed, transcendentals=transcendentals
    )


def pack_queries_kernel(seq_count, *refs):
    row_refs, out_ref, held_refs, sems = refs[:3], refs[3], refs[4:7], refs[7]
    copies = [
        pltpu.make_async_copy(ref, held, sems.at[i])
        for i, (ref, held) in enumerate(zip(row_refs, held_refs))
    ]
    for copy in copies:
        copy.start()
    for copy in copies:
        copy.wait()
    tokens = row_refs[0].shape[0]
    count = out_ref.shape[0] // tokens
    for owner in range(count):
        head = owner % 2 * seq_count + owner // 2
        to = 0
        for ref in held_refs:
            part = ref.shape[1] // count
            out_ref[owner * tokens : (owner + 1) * tokens, to : to + part] = ref[
                :, head * part : (head + 1) * part
            ]
            to += part


def pack_queries(rows, seq_count):
    count = 2 * seq_count
    shape = (rows[0].shape[0] * count, sum(a.shape[1] for a in rows) // count)
    return pl.pallas_call(
        functools.partial(pack_queries_kernel, seq_count),
        out_shape=jax.ShapeDtypeStruct(shape, jnp.bfloat16),
        in_specs=[hbm()] * 3,
        out_specs=vmem(),
        scratch_shapes=[pltpu.VMEM(a.shape, a.dtype) for a in rows]
        + [pltpu.SemaphoreType.DMA((3,))],
        compiler_params=params(PACK_BYTES),
        cost_estimate=cost(0, 2**19),
        name="pack_queries",
    )(*rows)


def settle_kernel(*refs):
    del refs


def settle(arrays, declared):
    count = len(arrays)
    return pl.pallas_call(
        settle_kernel,
        out_shape=[jax.ShapeDtypeStruct(a.shape, a.dtype) for a in arrays],
        in_specs=[vmem()] * count,
        out_specs=[vmem()] * count,
        input_output_aliases={i: i for i in range(count)},
        compiler_params=params(2**20),
        cost_estimate=cost(declared, 2**20),
        name="settle",
    )(*arrays)


def lengths_kernel(visible_ref, out_ref):
    tokens = out_ref.shape[0]
    diagonal = lax.broadcasted_iota(jnp.int32, (tokens, tokens), 0) == lax.broadcasted_iota(
        jnp.int32, (tokens, tokens), 1
    )
    lengths = jnp.sum(jnp.where(diagonal, visible_ref[...], 0), axis=-1, keepdims=True)
    out_ref[...] = jnp.broadcast_to(lengths, out_ref.shape)


def spread_lengths(visible):
    return pl.pallas_call(
        lengths_kernel,
        out_shape=jax.ShapeDtypeStruct((visible.shape[1], HEAD_WIDTH), jnp.int32),
        in_specs=[vmem()],
        out_specs=vmem(),
        compiler_params=params(),
        cost_estimate=cost(0, 2**15),
        name="spread_lengths",
    )(visible)


def half_of(rows, side):
    half = rows.shape[0] // 2
    return jnp.where(side == 0, rows[:half, :], rows[half:, :])


def tile_copies(masks, weight_ref, tile_refs, sems):
    depth = tile_refs[0].shape[0]
    rows = depth // FETCHES
    seq = lax.axis_index("seq")
    return [
        pltpu.make_async_copy(
            weight_ref.at[pl.ds(pl.multiple_of((seq ^ mask) * depth + n * rows, rows), rows), :],
            tile_ref.at[pl.ds(n * rows, rows), :],
            sems.at[i * FETCHES + n],
        )
        for i, (mask, tile_ref) in enumerate(zip(masks, tile_refs))
        for n in range(FETCHES)
    ]


def multiply(x_ref, w_ref, finish):
    columns = w_ref.shape[1]
    width = math.gcd(columns, 512)
    for start in range(0, columns, width):
        at = slice(start, start + width)
        finish(at, jnp.dot(x_ref[...], w_ref[:, at], preferred_element_type=jnp.float32))


def attend_kernel(heads, far_masks, block_rows, rows_ref, lengths_ref, own_ref, *refs):
    pieces = 2 * len(far_masks) + 2
    piece_refs, weight_ref = refs[:pieces], refs[pieces]
    out_ref, theirs_ref, tile_ref, sems = refs[pieces + 1 :]
    seq, tp, rep = lax.axis_index("seq"), lax.axis_index("tp"), lax.axis_index("rep")
    copies = tile_copies([0], weight_ref, [tile_ref], sems)
    for copy in copies:
        copy.start()
    @pl.when(tp >= 0)
    def compute():
        tokens = out_ref.shape[0]
        half = block_rows // 2
        lane = lax.broadcasted_iota(jnp.int32, (1, half), 1)
        blocks = []

        def whole(ref, mask):
            for first in (0, half):
                rows, values = slice(first, first + half), slice(block_rows + first, block_rows + first + half)
                blocks.append((ref, rows, values, (seq ^ mask) * block_rows + first + lane))

        whole(own_ref, 0)
        for i, ref in enumerate(piece_refs[:-2]):
            core = rep if i % 2 == 0 else 1 - rep
            whole(ref, far_masks[i // 2] + core)
        for ref, core in zip(piece_refs[-2:], (rep, 1 - rep)):
            first = (seq ^ 1) * block_rows + core * half
            blocks.append((ref, slice(0, half), slice(half, 2 * half), first + lane))
        width = heads * HEAD_WIDTH
        fresh_key = rows_ref[:, width : width + HEAD_WIDTH].astype(jnp.float32)
        fresh_value = rows_ref[:, width + HEAD_WIDTH :].astype(jnp.float32)
        group = max(1, UNIT_ROWS // tokens)
        lengths = jnp.concatenate([lengths_ref[...]] * group, axis=0)
        fresh_key = jnp.concatenate([fresh_key] * group, axis=0)
        start = jnp.concatenate([fresh_value, jnp.ones_like(fresh_value)], axis=1)
        start = jnp.concatenate([start] * group, axis=0)
        for first in range(0, heads, group):
            query = jnp.concatenate(
                [
                    rows_ref[:, h * HEAD_WIDTH : (h + 1) * HEAD_WIDTH]
                    for h in range(first, first + group)
                ],
                axis=0,
            )
            own = jnp.sum(query.astype(jnp.float32) * fresh_key, axis=-1, keepdims=True)
            own = jnp.broadcast_to(own, (group * tokens, HEAD_WIDTH))
            top, scores = own, []
            for ref, rows, _, position in blocks:
                score = lax.dot_general(
                    query, ref[rows, :], (((1,), (1,)), ((), ())), preferred_element_type=jnp.float32
                )
                hidden = position >= side_by_side(lengths, half // HEAD_WIDTH)
                score = jnp.where(hidden, HIDDEN, score)
                for i in range(0, half, HEAD_WIDTH):
                    top = jnp.maximum(top, score[:, i : i + HEAD_WIDTH])
                scores.append(score)
            peak = jnp.broadcast_to(jnp.max(top, axis=-1, keepdims=True), own.shape)
            acc = start * side_by_side(jnp.exp2((own - peak) * EXPONENT), 2)
            for score, (ref, _, rows, _) in zip(scores, blocks):
                weights = jnp.exp2((score - side_by_side(peak, half // HEAD_WIDTH)) * EXPONENT)
                values = ref[rows, :]
                acc = acc + jnp.dot(
                    weights.astype(jnp.bfloat16),
                    jnp.concatenate([values, jnp.ones_like(values)], axis=1),
                    preferred_element_type=jnp.float32,
                )
            context = (acc[:, :HEAD_WIDTH] / acc[:, HEAD_WIDTH:]).astype(jnp.bfloat16)
            for i in range(group):
                column = (first + i) * HEAD_WIDTH
                head = context[i * tokens : (i + 1) * tokens, :]
                out_ref[:, column : column + HEAD_WIDTH] = head
                theirs_ref[:, column : column + HEAD_WIDTH] = half_of(head, 1 - tp)

    for copy in copies:
        copy.wait()


def attend(heads, far_masks, query_rows, lengths, own, pieces, weight):
    tokens = query_rows.shape[0]
    block_rows = own.shape[0] // 2
    work = tokens * heads * block_rows * 2 * (1 + len(far_masks))
    depth = heads * HEAD_WIDTH
    return pl.pallas_call(
        functools.partial(attend_kernel, heads, far_masks, block_rows),
        out_shape=[
            jax.ShapeDtypeStruct((tokens, depth), jnp.bfloat16),
            jax.ShapeDtypeStruct((tokens // 2, depth), jnp.bfloat16),
            jax.ShapeDtypeStruct((depth, weight.shape[1]), weight.dtype),
        ],
        in_specs=[vmem()] * (3 + len(pieces)) + [hbm()],
        out_specs=[vmem()] * 3,
        scratch_shapes=[pltpu.SemaphoreType.DMA((FETCHES,))],
        compiler_params=params(ATTEND_BYTES),
        cost_estimate=cost(6 * work * HEAD_WIDTH, 2**20, work),
        name="attend",
    )(query_rows, lengths, own, *pieces, weight)


def load_kernel(masks, weight_ref, x_ref, first_ref, acc_ref, *refs):
    tile_refs, sems = refs[:-1], refs[-1]
    tp = lax.axis_index("tp")
    copies = tile_copies(masks, weight_ref, tile_refs, sems)
    for copy in copies:
        copy.start()

    def finish(at, part):
        acc_ref[:, at] = part

    @pl.when(tp >= 0)
    def compute():
        multiply(x_ref, first_ref, finish)

    for copy in copies:
        copy.wait()


def load(weight, context, tile, masks):
    tokens, (depth, columns) = context.shape[0], tile.shape
    return pl.pallas_call(
        functools.partial(load_kernel, masks),
        out_shape=[
            jax.ShapeDtypeStruct((tokens, columns), jnp.float32),
        ]
        + [jax.ShapeDtypeStruct(tile.shape, tile.dtype)] * len(masks),
        in_specs=[hbm(), vmem(), vmem()],
        out_specs=[vmem()] * (1 + len(masks)),
        scratch_shapes=[pltpu.SemaphoreType.DMA((FETCHES * len(masks),))],
        compiler_params=params(LOAD_BYTES),
        cost_estimate=cost(2 * tokens * depth * columns, len(masks) * depth * columns * 2),
        name="load",
    )(weight, context, tile)


def project_kernel(side, pass_on, x_ref, w_ref, acc_ref, *refs):
    tp = lax.axis_index("tp")
    out_ref = refs[-1]
    if pass_on:
        out_ref = refs[1]
        refs[2][...] = half_of(refs[0][...], tp)

    def finish(at, part):
        acc = acc_ref[:, at]
        if side is not None:
            acc = half_of(acc, tp if side == 0 else 1 - tp)
        out_ref[:, at] = (part + acc).astype(out_ref.dtype)

    multiply(x_ref, w_ref, finish)


def project(context, tile, acc, side=None, dtype=jnp.float32, pass_on=None):
    tokens, columns = context.shape[0], tile.shape[1]
    shapes = [jax.ShapeDtypeStruct((tokens, columns), dtype)]
    operands = [context, tile, acc]
    if pass_on is not None:
        operands.append(pass_on)
        shapes.append(jax.ShapeDtypeStruct((tokens // 2, pass_on.shape[1]), pass_on.dtype))
    return pl.pallas_call(
        functools.partial(project_kernel, side, pass_on is not None),
        out_shape=shapes,
        in_specs=[vmem()] * len(operands),
        out_specs=[vmem()] * len(shapes),
        compiler_params=params(PROJECT_BYTES),
        cost_estimate=cost(2 * context.size * columns, 2 * tile.size),
        name="project",
    )(*operands)


def add_kernel(*refs):
    out_ref = refs[-1]
    count = (len(refs) - 1) // 2
    start = 0
    for keep_ref, got_ref in zip(refs[:count], refs[count:-1]):
        width = keep_ref.shape[1]
        total = keep_ref[...] + got_ref[...].astype(jnp.float32)
        out_ref[0, :, start : start + width] = total.astype(out_ref.dtype)
        start += width


def add(keeps, gots):
    shape = (1, keeps[0].shape[0], sum(a.shape[1] for a in keeps))
    return pl.pallas_call(
        add_kernel,
        out_shape=jax.ShapeDtypeStruct(shape, jnp.bfloat16),
        in_specs=[vmem()] * (2 * len(keeps)),
        out_specs=vmem(),
        compiler_params=params(PROJECT_BYTES),
        cost_estimate=cost(0, 2**19),
        name="add",
    )(*keeps, *gots)


def shards_by_head(
    queries, fresh_key_rows, fresh_value_rows, visible, prefix_keys, cached_value_rows, out_weight
):
    heads = queries.shape[2] // fresh_key_rows.shape[2]
    masks = list(range(1, lax.axis_size("seq")))
    rows = [queries[0], fresh_key_rows[0], fresh_value_rows[0]]
    seq, rep = lax.axis_index("seq"), lax.axis_index("rep")
    half_rows = prefix_keys.shape[0] // 2

    def cut(first, count, head):
        return jnp.concatenate(
            [
                lax.dynamic_slice(table, (first, head * HEAD_WIDTH), (count, HEAD_WIDTH))
                for table in (prefix_keys, cached_value_rows)
            ]
        )

    far_masks = masks[1::2]
    far = [swap_by_core(cut(0, 2 * half_rows, seq ^ (m + rep)), m) for m in far_masks]
    near = swap(cut(rep * half_rows, half_rows, seq ^ 1), "seq", 1)
    own = cut(0, 2 * half_rows, seq)
    query_rows = lax.all_to_all(
        pack_queries(rows, 1 + len(masks)), ("seq", "tp"), split_axis=0, concat_axis=0, tiled=True
    )
    lengths = spread_lengths(visible)
    far = settle(far, SETTLE_FIRST)
    pieces = [piece for mine in (*far, near) for piece in (mine, swap(mine, "rep", 1))]
    context, theirs, tile = attend(heads, far_masks, query_rows, lengths, own, pieces, out_weight)

    order = masks[-1:] + masks[:-1]
    chunks = [swap(context, "seq", mask) for mask in order[:-1]]
    first = swap(theirs, "seq", order[-1])
    acc, *tiles = load(out_weight, context, tile, order)
    for i, (chunk, tile) in enumerate(zip(chunks, tiles)):
        acc, *ours = project(chunk, tile, acc, pass_on=context if i == 0 else None)
        if i == 0:
            (second,) = settle([swap(ours[0], "seq", order[-1])], SETTLE_LAST)
    (sums,) = project(first, tiles[-1], acc, 1, jnp.bfloat16)
    got = swap(sums, "tp", 1)
    (kept,) = project(second, tiles[-1], acc, 0)
    return add([kept], [got])


def solution(mesh):
    in_specs = (
        P("rep", ("groups", "seq", "tp"), None),
        P("rep", ("groups", "seq", "tp"), None),
        P("rep", ("groups", "seq", "tp"), None),
        P("rep", "groups"),
        P(("groups", "seq"), "tp"),
        P(("groups", "seq"), "tp"),
        P("tp", "seq"),
    )
    out_specs = P("rep", ("groups", "tp"), "seq")
    sizes = mesh.shape
    seq_count = sizes["seq"]

    def shards(*args):
        local_heads = args[4].shape[1] // HEAD_WIDTH
        by_head = (
            local_heads == seq_count
            and seq_count in (4, 8)
            and sizes["tp"] == 2
            and sizes["rep"] == 2
            and args[0].shape[2] // args[1].shape[2] % 4 == 0
        )
        return (shards_by_head if by_head else shards_any)(*args)

    return jax.shard_map(shards, mesh=mesh, in_specs=in_specs, out_specs=out_specs, check_vma=False)
```
